32 devices in a mesh: section: 2 (over x), dp: 4 (over z), tensor: 4 (over y, core).
Axes of the slice: x: 2, y: 2, z: 4, core: 2. Of those that a mesh axis runs over, the one named last changes fastest.
Arguments:
- block_input: float32 [2, 1024, 1536], P(None, ('dp', 'tensor')), may hold values from -6 to 6
- segments: int32 [2, 1024], P(None, 'dp'), may hold values from 0 to 4, as said below
- expert_ids: int32 [2, 2, 1024, 4], P('section', None, 'dp'), may hold values from 0 to 15, all different within a row; in each aligned block of 256 rows (0 to 255, 256 to 511, ..., all dimensions but the last counted through in order) at most 72 rows name the same one
- gate_values: float32 [2, 2, 1024, 4], P('section', None, 'dp'), may hold values from 0.15 to 0.45
- cotangent: float32 [2, 2, 1024, 1536], P('section', None, ('dp', 'tensor')), may hold values from -6 to 6
- attn_gain: bfloat16 [2, 1536], P('section', ('dp', 'tensor')), may hold values from 0.5 to 1.5
- query_weight: bfloat16 [2, 1536, 1536], P('section', 'dp', 'tensor'), may hold values from -0.21875 to 0.21875
- kv_weight: bfloat16 [2, 1536, 512], P('section', 'dp', 'tensor'), may hold values from -0.21875 to 0.21875
- out_weight: bfloat16 [2, 1536, 1536], P('section', 'tensor', 'dp'), may hold values from -1.25 to 1.25
- moe_gain: bfloat16 [2, 1536], P('section', ('dp', 'tensor')), may hold values from 0.5 to 1.5
- w_in: bfloat16 [2, 16, 1536, 1536], P('section', 'dp', None, 'tensor'), may hold values from -0.15625 to 0.15625
- w_out: bfloat16 [2, 16, 768, 1536], P('section', 'dp', 'tensor'), may hold values from -0.625 to 0.625
Outputs:
- block_out: float32 [2, 2, 1024, 1536], P('section', None, ('dp', 'tensor'))
- input_grad: float32 [2, 2, 1024, 1536], P('section', None, ('dp', 'tensor'))
- attn_gain_grad: float32 [2, 1536], P('section', ('dp', 'tensor'))
- query_grad: float32 [2, 1536, 1536], P('section', 'dp', 'tensor')
- kv_grad: float32 [2, 1536, 512], P('section', 'dp', 'tensor')
- out_grad: float32 [2, 1536, 1536], P('section', 'tensor', 'dp')
- moe_gain_grad: float32 [2, 1536], P('section', ('dp', 'tensor'))
- w_in_grad: float32 [2, 16, 1536, 1536], P('section', 'dp', None, 'tensor')
- w_out_grad: float32 [2, 16, 768, 1536], P('section', 'dp', 'tensor')
The draws below stay inside these ranges and needn't reach their ends.
Inputs may be any that keep to these rules, and one draw needn't show every extreme that they name: `segments`: within each sequence of 256 tokens segment numbers never fall from one token to the next and start at 0. `expert_ids`: each token names 4 different experts; within each sequence of 256 tokens of one layer and micro-batch no expert is named by more than 72 tokens.
All inputs are finite; a program needn't handle non-finite values.
Results may differ from the reference program's by a relative error of at most 0.04.
Values may be sent and summed in bfloat16 or wider, within the bound.
No kernel may reach another device: no remote copies, remote signals or barrier semaphores. Data moves between devices by JAX's collectives and lax.ppermute only.
A program may use at most 256 MiB of HBM per device.

```python
import math
import jax
import jax.numpy as jnp
import numpy as np
from jax import lax

D = 1536
H = 12
KVH = 2
HD = 128
FF = 768
E = 16
TOPK = 4
MB = 2
TOK_DEV = 64
SEQ = 256
TOKENS = 1024
CAP = 72
N_SECTION = 2
N_DP = 4
N_TENSOR = 4


def draw_segments(key, part):
    key = jax.random.fold_in(key, 7)
    keys_four = jax.random.split(key, 4)
    sequences = MB * N_DP
    first_cut = jax.random.randint(keys_four[0], (sequences, 1), 1, TOK_DEV)
    long_end = jax.random.randint(keys_four[1], (sequences, 1), SEQ - TOK_DEV + 1, SEQ)
    early_cut = jax.random.randint(keys_four[2], (sequences, 1), 1, first_cut + 1)
    late_cut = jax.random.randint(keys_four[3], (sequences, 1), long_end, SEQ)
    ordinal = jnp.arange(SEQ, dtype=jnp.int32)[None, :]
    segment_ids = (ordinal >= early_cut).astype(jnp.int32) + (ordinal >= first_cut).astype(jnp.int32)
    segment_ids = segment_ids + (ordinal >= long_end).astype(jnp.int32) + (ordinal >= late_cut).astype(jnp.int32)
    return segment_ids.reshape(MB, N_DP * SEQ)


def levels(rng, extent, shards, smallest, top_value):
    loudness = 1.0
    for position, shards_of in shards:
        heights = jax.random.uniform(jax.random.fold_in(jax.random.fold_in(rng, 6), position), (shards_of,), jnp.float32, smallest / len(shards), top_value / len(shards))
        loudness = loudness * jnp.repeat(jnp.exp(heights), extent[position] // shards_of).reshape((-1,) + (1,) * (len(extent) - 1 - position))
    return loudness


def assign_block(rng, own, number, rows, amount, top, reach, slope):
    sequence = jax.random.permutation(rng, amount)
    crowded, common = load_shares(amount, rows * top, reach, slope, True), load_shares(amount, rows * top, reach, slope, False)
    places = jnp.arange(amount)

    def named(sizes, offset_by):
        used = int((sizes > 0).sum())
        fixed = max(1, used // 4)
        passed = fixed + (places - fixed + offset_by * (used - fixed)) % max(1, amount - fixed)
        return jnp.zeros((amount,), jnp.int32).at[sequence[jnp.where(places < fixed, places, passed)]].set(jnp.asarray(sizes, jnp.int32))

    sizes = jnp.where(number % 4 == 0, named(crowded, number // 4), named(common, number - number // 4 - 1))
    mixed = jax.random.permutation(jax.random.fold_in(own, 3), amount)
    donor, taker = mixed[0:amount // 2 * 2:2], mixed[1:amount // 2 * 2:2]
    room = jnp.minimum(sizes[donor] - 1, reach - sizes[taker]) // 2
    room = jnp.where((donor == sequence[0]) | (taker == sequence[0]) | (sizes[taker] == 0), 0, jnp.maximum(room, 0))
    passed = jax.random.randint(jax.random.fold_in(own, 4), (amount // 2,), 0, 1 << 20) % (room + 1)
    sizes = sizes.at[donor].add(-passed).at[taker].add(passed)
    members = jnp.searchsorted(jnp.cumsum(sizes), jnp.arange(rows * top), side="right").astype(jnp.int32)
    grid = members.reshape(top, rows).T
    grid = grid[jax.random.permutation(jax.random.fold_in(own, 1), rows)]
    offset_by = jax.random.randint(jax.random.fold_in(own, 2), (rows, 1), 0, top)
    return jnp.take_along_axis(grid, (jnp.arange(top)[None, :] + offset_by) % top, axis=1)


def load_shares(count, total, bound, lean, full):
    loads = [(1 << 20) // math.isqrt(grade ** lean) + 1 for grade in range(1, count + 1)]
    largest = bound if full else min(bound, max(-(-total // count), total * loads[0] // sum(loads)))
    least = 1 if total - largest >= count - 1 else 0
    counts, rest = [largest] + [least] * (count - 1), total - largest - least * (count - 1)
    while rest > 0:
        candidates = [i for i in range(1, count) if counts[i] < largest] or [i for i in range(1, count) if counts[i] < bound]
        mass, budget = sum([loads[i] for i in candidates]), rest
        for i in candidates:
            addition = min(bound - counts[i], max(1, budget * loads[i] // mass), rest)
            counts[i] = counts[i] + addition
            rest = rest - addition
    return np.array(counts)


def noise(stream_key, extent, deviation, most, cuts=(), held_as=jnp.bfloat16):
    level = levels(stream_key, extent, cuts, -0.22, 0.18) if cuts else 1.0
    values = jax.random.normal(stream_key, extent, jnp.float32) * deviation * level
    return jnp.minimum(jnp.maximum(values, -most), most).astype(held_as)


def setup_inputs(seed: int = 0) -> dict:
    splits = jax.random.split(jax.random.key(seed), 13)
    block_input = noise(splits[0], (MB, TOKENS, D), 1.0, 6.0, ((1, 16),), jnp.float32)
    segments = draw_segments(jax.random.fold_in(splits[12], 71), 0)
    expert_ids_keys = jax.random.split(jax.random.fold_in(splits[2], 1), N_SECTION * MB * TOKENS // SEQ)
    expert_ids_turns = jax.random.permutation(jax.random.fold_in(splits[2], 3), N_SECTION * MB * TOKENS // SEQ)
    expert_ids = jax.vmap(lambda own, number: assign_block(jax.random.fold_in(splits[2], 2), own, number, SEQ, E, TOPK, CAP, 1))(expert_ids_keys, expert_ids_turns).reshape((N_SECTION, MB, TOKENS, TOPK))
    gate_values = jnp.clip(jnp.exp(math.log(0.45) - 1.0986122 * jax.random.uniform(splits[3], (N_SECTION, MB, TOKENS, TOPK), jnp.float32) ** levels(splits[3], (N_SECTION, MB, TOKENS, TOPK), ((0, 2), (2, 4)), -0.2, 0.2)), 0.15, 0.45)
    cotangent = noise(splits[4], (N_SECTION, MB, TOKENS, D), 1.0, 6.0, ((0, 2), (2, 16)), jnp.float32)
    attn_gain = jnp.clip(1.0 + 0.1 * jax.random.normal(splits[5], (N_SECTION, D), jnp.float32), 0.5, 1.5).astype(jnp.bfloat16)
    query_weight = noise(splits[6], (N_SECTION, D, H * HD), (D // 2) ** -0.5, 0.21875, ((0, 2), (1, 4), (2, 4)))
    kv_weight = noise(splits[7], (N_SECTION, D, 2 * KVH * HD), (D // 2) ** -0.5, 0.21875, ((0, 2), (1, 4), (2, 4)))
    out_weight = noise(splits[8], (N_SECTION, H * HD, D), (H * HD // 64) ** -0.5, 1.25, ((0, 2), (1, 4), (2, 4)))
    moe_gain = jnp.clip(1.0 + 0.1 * jax.random.normal(splits[9], (N_SECTION, D), jnp.float32), 0.5, 1.5).astype(jnp.bfloat16)
    w_in = noise(splits[10], (N_SECTION, E, D, 2 * FF), D ** -0.5, 0.15625, ((0, 2), (1, 4), (3, 4)))
    w_out = noise(splits[11], (N_SECTION, E, FF, D), (FF // 8) ** -0.5, 0.625, ((0, 2), (1, 4), (2, 4)))
    return {"block_input": block_input, "segments": segments, "expert_ids": expert_ids, "gate_values": gate_values, "cotangent": cotangent, "attn_gain": attn_gain, "query_weight": query_weight, "kv_weight": kv_weight, "out_weight": out_weight, "moe_gain": moe_gain, "w_in": w_in, "w_out": w_out}


EPS = 1e-06
THETA = 10000.0
HIGHEST = lax.Precision.HIGHEST

@jax.custom_vjp
def low(v):
    return lax.optimization_barrier(v.astype(jnp.bfloat16)).astype(jnp.float32)

@jax.custom_vjp
def low_back(v):
    return v

def low_keep(v):
    return (low(v), None)

def low_pass(kept, grad):
    return (grad,)

def back_keep(v):
    return (v, None)

def back_low(kept, grad):
    return (low(grad),)
low.defvjp(low_keep, low_pass)
low_back.defvjp(back_keep, back_low)

def positions(segment):
    length = segment.shape[0]
    ordinal = jnp.arange(length, dtype=jnp.int32)
    change = jnp.concatenate([jnp.ones((1,), dtype=jnp.bool_), segment[1:] != segment[:-1]])
    starts = lax.cummax(jnp.where(change, ordinal, 0).astype(jnp.int32), axis=0)
    return ordinal - starts

def rotate(values, places, sign):
    half_dim = values.shape[-1] // 2
    frequency = THETA ** (-2.0 * jnp.arange(half_dim, dtype=jnp.float32) / values.shape[-1])
    angles = places.astype(jnp.float32)[:, None] * frequency[None, :]
    cosine = jnp.cos(angles)[:, None, :]
    sine_part = sign * jnp.sin(angles)[:, None, :]
    first_half = values[..., :half_dim]
    second_half = values[..., half_dim:]
    return jnp.concatenate([first_half * cosine - second_half * sine_part, second_half * cosine + first_half * sine_part], axis=-1)

def inverse_rms(layer_rows):
    return lax.rsqrt(lax.optimization_barrier(jnp.mean(layer_rows * layer_rows, axis=-1, keepdims=True)) + EPS)

def destinations(chosen, experts, capacity):
    flat_ids = chosen.reshape(-1).astype(jnp.int32)
    one_hot = (flat_ids[:, None] == jnp.arange(experts, dtype=jnp.int32)[None, :]).astype(jnp.int32)
    earlier = jnp.cumsum(one_hot, axis=0) - one_hot
    return (flat_ids * capacity + lax.optimization_barrier(jnp.sum(earlier * one_hot, axis=1))).astype(jnp.int32)

def matmul(left, right):
    return jnp.dot(left, right, precision=HIGHEST)

def layer(layer_rows, segment, expert_picks, shares, gain_attn, query_w, kv_w, out_w, gain_moe, expert_in, expert_out):
    row_count = layer_rows.shape[0]
    places = positions(segment)
    normed = low(layer_rows * inverse_rms(layer_rows) * gain_attn)
    query_lin = low_back(matmul(normed, query_w)).reshape(row_count, H, HD)
    queries = low(rotate(query_lin, places, 1.0))
    kv_lin = low_back(matmul(normed, kv_w))
    key_rows = low(rotate(kv_lin[:, :KVH * HD].reshape(row_count, KVH, HD), places, 1.0))
    values = low(kv_lin[:, KVH * HD:].reshape(row_count, KVH, HD))
    keys_all = jnp.repeat(key_rows, H // KVH, axis=1)
    values_all = jnp.repeat(values, H // KVH, axis=1)
    scores = low_back(HD ** (-0.5) * jnp.einsum('qhd,khd->hqk', queries, keys_all, precision=HIGHEST))
    ordinal = jnp.arange(row_count, dtype=jnp.int32)
    allowed = (ordinal[None, :] <= ordinal[:, None]) & (segment[None, :] == segment[:, None])
    scores = jnp.where(allowed[None], scores, -1e+30)
    attention_probs = low(jax.nn.softmax(scores, axis=-1))
    attended = low(low_back(jnp.einsum('hqk,khd->qhd', attention_probs, values_all, precision=HIGHEST))).reshape(row_count, H * HD)
    middle = layer_rows + low_back(matmul(attended, out_w))
    mixed_in = low(middle * inverse_rms(middle) * gain_moe)
    slot_ids = destinations(expert_picks, E, CAP)
    buffer = jnp.zeros((E * CAP, D), jnp.float32).at[slot_ids].set(jnp.repeat(mixed_in, TOPK, axis=0)).reshape(E, CAP, D)
    gate_up = low_back(jnp.einsum('ecd,edf->ecf', buffer, expert_in, precision=HIGHEST))
    gate_up = gate_up.reshape(E, CAP, N_TENSOR, 2, FF // N_TENSOR)
    gate_part = gate_up[:, :, :, 0, :].reshape(E, CAP, FF)
    up_part = gate_up[:, :, :, 1, :].reshape(E, CAP, FF)
    hidden = low(jax.nn.silu(gate_part) * up_part)
    result = low_back(jnp.einsum('ecf,efd->ecd', hidden, expert_out, precision=HIGHEST)).reshape(E * CAP, D)
    mixed_out = lax.optimization_barrier(jnp.sum(shares[:, :, None] * result[slot_ids].reshape(row_count, TOPK, D), axis=1))
    return middle + mixed_out

def reference(block_input, segments, expert_ids, gate_values, cotangent, attn_gain, query_weight, kv_weight, out_weight, moe_gain, w_in, w_out):
    params = tuple((weight_arr.astype(jnp.float32) for weight_arr in (attn_gain, query_weight, kv_weight, out_weight, moe_gain, w_in, w_out)))
    sequences = MB * N_DP
    inputs = block_input.astype(jnp.float32).reshape(sequences, SEQ, D)
    segment_rows = segments.reshape(sequences, SEQ)
    chosen = expert_ids.reshape(N_SECTION, sequences, SEQ, TOPK).transpose(1, 0, 2, 3)
    gates = gate_values.astype(jnp.float32).reshape(N_SECTION, sequences, SEQ, TOPK).transpose(1, 0, 2, 3)
    upstream = cotangent.astype(jnp.float32).reshape(N_SECTION, sequences, SEQ, D).transpose(1, 0, 2, 3)

    def forward(weights, offsets):

        def one_sequence(bundle):
            seq_rows, segment, expert_picks, shares, shifts = bundle
            results = []
            hidden_rows = seq_rows
            for section_num in range(N_SECTION):
                layer_weights = [weight_set[section_num] for weight_set in weights]
                hidden_rows = layer(hidden_rows + shifts[section_num], segment, expert_picks[section_num], shares[section_num], *layer_weights)
                results.append(hidden_rows)
            return jnp.stack(results)
        return lax.map(jax.checkpoint(one_sequence), (inputs, segment_rows, chosen, gates, offsets))
    offsets = jnp.zeros((sequences, N_SECTION, SEQ, D), jnp.float32)
    outputs, pullback = jax.vjp(forward, params, offsets)
    grad_params, grad_offsets = pullback(upstream)
    block_out = outputs.transpose(1, 0, 2, 3).reshape(N_SECTION, MB, N_DP * SEQ, D)
    input_grad = grad_offsets.transpose(1, 0, 2, 3).reshape(N_SECTION, MB, N_DP * SEQ, D)
    return (block_out, input_grad, grad_params[0], grad_params[1], grad_params[2], grad_params[3], grad_params[4], grad_params[5], grad_params[6])
```

```python
import functools

import jax
import jax.numpy as jnp
from jax import lax
from jax.experimental import pallas as pl
from jax.experimental.pallas import tpu as pltpu
from jax.sharding import PartitionSpec as P

H = 12
KVH = 2
HD = 128
E = 16

EPS = 1e-06
THETA = 10000.0
BF = jnp.bfloat16
F32 = jnp.float32
MIB = 1024 * 1024


def dot(a, b, ca, cb):
    return lax.dot_general(a, b, (((ca,), (cb,)), ((), ())), preferred_element_type=F32)


def by_tensor(value, flip):
    size = lax.axis_size("tensor")
    return lax.ppermute(value, "tensor", [(i, i ^ flip) for i in range(size)])


def by_dp(value, flip):
    size = lax.axis_size("dp")
    return lax.ppermute(value, "dp", [(i, i ^ flip) for i in range(size)])


def by_section(value):
    return lax.ppermute(value, "section", [(0, 1), (1, 0)])


def to_section(value, host):
    return lax.ppermute(value, "section", [(1 - host, host)])


def kv_turn(value):
    return lax.ppermute(value, "tensor", [(0, 0), (1, 2), (2, 1), (3, 3)])


def over_tensor(value):
    across = by_tensor(value, 2)
    core = by_tensor(value, 1)
    return [value, core, across, by_tensor(across, 1)]


def sum_over_tensor(keep, send):
    total = keep + by_tensor(send, 1)
    return total[0], by_tensor(total[1], 2)


def rope(value, cosine, sine):
    return value * cosine + pltpu.roll(value, HD // 2, 1) * sine


def allowed_pairs(idx_row, idx_col, start_col):
    keys = idx_row[...]
    return (keys <= idx_col[...]) & (keys >= start_col[...])


def attn_fwd_kernel(
    heads, rows,
    a0, a1, a2, a3, wq, wkv, wo, cosine, sine, idx_row, idx_col, start_col,
    keep, send, q_out, k_out, v_out, lse_out, o_out, a_all,
):
    for r, ref in enumerate((a0, a1, a2, a3)):
        a_all[r * rows : (r + 1) * rows, :] = ref[...]
    a = a_all[...]
    q = dot(a, wq[...], 1, 0)
    kv = dot(a, wkv[...], 1, 0)
    co, si = cosine[...], sine[...]
    k = rope(kv[:, :HD], co, si).astype(BF)
    v = kv[:, HD:].astype(BF)
    k_out[...] = k
    v_out[...] = v
    allowed = allowed_pairs(idx_row, idx_col, start_col)
    lane = lax.broadcasted_iota(jnp.int32, (q.shape[0], HD), 1)
    lse_all = jnp.zeros((q.shape[0], HD), F32)
    for h in range(heads):
        qh = rope(q[:, h * HD : (h + 1) * HD], co, si).astype(BF)
        q_out[:, h * HD : (h + 1) * HD] = qh
        s = jnp.where(allowed, HD ** (-0.5) * dot(qh, k, 1, 1), -1e30)
        top = jnp.max(s, axis=1, keepdims=True)
        lse = top + jnp.log(jnp.sum(jnp.exp(s - top), axis=1, keepdims=True))
        p = jnp.exp(s - lse).astype(BF)
        o_out[:, h * HD : (h + 1) * HD] = dot(p, v, 1, 0).astype(BF)
        lse_all = jnp.where(lane == h, lse, lse_all)
    lse_out[...] = lse_all
    part = dot(o_out[...], wo[...], 1, 0).astype(BF)
    for r in range(4):
        (send if r % 2 else keep)[r // 2] = part[r * rows : (r + 1) * rows, :]


def attn_bwd_kernel(
    heads, rows,
    d0, d1, d2, d3, q_in, k_in, v_in, lse_in, wq, wkv, wo, cosine, sine, idx_row, idx_col, start_col,
    keep, send, dq_out, dkv_out, d_all,
):
    for r, ref in enumerate((d0, d1, d2, d3)):
        d_all[r * rows : (r + 1) * rows, :] = ref[...]
    do = dot(d_all[...], wo[...], 1, 1).astype(BF)
    co, si = cosine[...], -sine[...]
    k, v = k_in[...], v_in[...]
    allowed = allowed_pairs(idx_row, idx_col, start_col)
    dk = jnp.zeros((do.shape[0], HD), F32)
    dv = jnp.zeros((do.shape[0], HD), F32)
    for h in range(heads):
        qh = q_in[:, h * HD : (h + 1) * HD]
        doh = do[:, h * HD : (h + 1) * HD]
        s = jnp.where(allowed, HD ** (-0.5) * dot(qh, k, 1, 1), -1e30)
        p = jnp.exp(s - lse_in[:, h : h + 1])
        dv = dv + dot(p.astype(BF), doh, 0, 0)
        dp = dot(doh, v, 1, 1)
        ds = (p * (dp - jnp.sum(p * dp, axis=1, keepdims=True))).astype(BF)
        dq = HD ** (-0.5) * dot(ds, k, 1, 0)
        dk = dk + dot(ds, qh, 0, 0)
        dq_out[:, h * HD : (h + 1) * HD] = rope(dq, co, si).astype(BF)
    dkv_out[:, :HD] = rope(HD ** (-0.5) * dk, co, si).astype(BF)
    dkv_out[:, HD:] = dv.astype(BF)
    part = (dot(dq_out[...], wq[...], 1, 1) + dot(dkv_out[...], wkv[...], 1, 1)).astype(BF)
    for r in range(4):
        (send if r % 2 else keep)[r // 2] = part[r * rows : (r + 1) * rows, :]


def attn_wgrad_kernel(
    rows,
    a0, a1, a2, a3, d0, d1, d2, d3, o_in, dq, dkv,
    dwq, dwk, dwv, dwo, a_all, d_all,
):
    for r, ref in enumerate((a0, a1, a2, a3)):
        a_all[r * rows : (r + 1) * rows, :] = ref[...]
    for r, ref in enumerate((d0, d1, d2, d3)):
        d_all[r * rows : (r + 1) * rows, :] = ref[...]
    dwo[...] = dot(o_in[...], d_all[...], 0, 0).astype(BF)
    a = a_all[...]
    dwq[...] = dot(a, dq[...], 0, 0).astype(BF)
    dwk[...] = dot(a, dkv[:, :HD], 0, 0).astype(BF)
    dwv[...] = dot(a, dkv[:, HD:], 0, 0).astype(BF)


def slot_rows(pos_row, s, experts, cap):
    tokens = pos_row.shape[2]
    slot = lax.broadcasted_iota(jnp.int32, (experts * cap, tokens), 0)
    hit = slot == pos_row[s, 0:1, :]
    for e in range(1, experts):
        hit = hit | (slot == pos_row[s, e : e + 1, :])
    return hit


def slot_cols(pos_col, s, experts, cap):
    tokens = pos_col.shape[1]
    slot = lax.broadcasted_iota(jnp.int32, (tokens, experts * cap), 1)
    hit = slot == pos_col[s, :, 0:1]
    for e in range(1, experts):
        hit = hit | (slot == pos_col[s, :, e : e + 1])
    return hit.astype(F32).astype(BF)


def fetch_sequence(blocks, s, into, rows):
    for r in range(4):
        into[r * rows : (r + 1) * rows, :] = blocks[s // 2 * 4 + r][s % 2]


def dispatch(blocks, pos_row, gate_row, into, gates, seq, experts, cap, rows, count, scaled):
    for s in range(count):
        fetch_sequence(blocks, s, seq, rows)
        hit = slot_rows(pos_row, s, experts, cap)
        picked = dot(hit.astype(F32).astype(BF), seq[...], 1, 0)
        own = lax.broadcasted_iota(jnp.int32, hit.shape, 0) // cap
        gate = jnp.zeros(hit.shape, F32)
        for e in range(experts):
            gate = jnp.where(hit & (own == e), gate_row[s, e : e + 1, :], gate)
        gate = jnp.sum(gate, axis=1, keepdims=True)
        if scaled:
            picked = picked * gate
        else:
            gates[s] = gate
        picked = picked.astype(BF)
        for e in range(experts):
            into[e, s * cap : (s + 1) * cap, :] = picked[e * cap : (e + 1) * cap, :]


def combine(values, pos_col, keeps, sends, experts, cap, rows, count):
    for s in range(count):
        total = dot(slot_cols(pos_col, s, experts, cap), values[s], 1, 0).astype(BF)
        for r in range(4):
            (sends if r % 2 else keeps)[s // 2][r // 2, s % 2] = total[r * rows : (r + 1) * rows, :]


def moe_fwd_kernel(experts, cap, rows, count, *refs):
    blocks, refs = refs[: count * 2], refs[count * 2 :]
    pos_row, pos_col, gate_row, w_in, w_out, x_out, gu_out = refs[:7]
    keeps, sends = refs[7 : 7 + count // 2], refs[7 + count // 2 : 7 + count]
    x_all, result, gates, seq = refs[7 + count :]
    step = pl.program_id(0)

    @pl.when(step == 0)
    def _():
        dispatch(blocks, pos_row, gate_row, x_all, gates, seq, experts, cap, rows, count, False)

    x = x_all[step]
    x_out[0] = x
    gu = dot(x, w_in[0], 1, 0)
    gu_out[0] = gu
    half = gu.shape[1] // 2
    gate, up = gu[:, :half], gu[:, half:]
    z = (gate / (1.0 + jnp.exp(-gate)) * up).astype(BF)
    out = dot(z, w_out[0], 1, 0)
    for s in range(count):
        at = pl.ds(pl.multiple_of(step * cap, 16), cap)
        result[s, at, :] = (out[s * cap : (s + 1) * cap, :] * gates[s, at, :]).astype(BF)

    @pl.when(step == experts - 1)
    def _():
        combine(result, pos_col, keeps, sends, experts, cap, rows, count)


def moe_bwd_kernel(experts, cap, rows, count, *refs):
    blocks, refs = refs[: count * 2], refs[count * 2 :]
    pos_row, pos_col, gate_row, gu_in, w_in, w_out, dr_out, z_out, dgu_out = refs[:9]
    keeps, sends = refs[9 : 9 + count // 2], refs[9 + count // 2 : 9 + count]
    dr_all, result, seq = refs[9 + count :]
    step = pl.program_id(0)

    @pl.when(step == 0)
    def _():
        dispatch(blocks, pos_row, gate_row, dr_all, None, seq, experts, cap, rows, count, True)

    dr = dr_all[step]
    dr_out[0] = dr
    gu = gu_in[0]
    half = gu.shape[1] // 2
    gate, up = gu[:, :half], gu[:, half:]
    sg = 1.0 / (1.0 + jnp.exp(-gate))
    act = gate * sg
    z_out[0] = (act * up).astype(BF)
    dz = dot(dr, w_out[0], 1, 1)
    dgu_out[0, :, :half] = (dz * up * sg * (1.0 + gate * (1.0 - sg))).astype(BF)
    dgu_out[0, :, half:] = (dz * act).astype(BF)
    out = dot(dgu_out[0], w_in[0], 1, 1).astype(BF)
    for s in range(count):
        result[s, pl.ds(pl.multiple_of(step * cap, 16), cap), :] = out[s * cap : (s + 1) * cap, :]

    @pl.when(step == experts - 1)
    def _():
        combine(result, pos_col, keeps, sends, experts, cap, rows, count)


def moe_wgrad_kernel(sel, *refs):
    first, second, (dwin, dwout) = refs[:8], refs[8:16], refs[16:]

    def run(x0, x1, dg0, dg1, z0, z1, dr0, dr1):
        dwin[0] = dot(x0[0], dg0[0], 0, 0) + dot(x1[0], dg1[0], 0, 0)
        dwout[0] = dot(z0[0], dr0[0], 0, 0) + dot(z1[0], dr1[0], 0, 0)

    @pl.when(sel[0] == 0)
    def _():
        run(*first)

    @pl.when(sel[0] == 1)
    def _():
        run(*second)


def inverse_rms(rows):
    return lax.rsqrt(jnp.mean(rows * rows, axis=-1, keepdims=True) + EPS)


def norm_backward(rows, factor, gain, upstream):
    weighted = upstream * gain
    projected = jnp.mean(weighted * rows, axis=-1, keepdims=True)
    grad_rows = factor * weighted - rows * (factor * factor * factor) * projected
    return grad_rows, jnp.sum(upstream * rows * factor, axis=0)


def whole(shape):
    return pl.BlockSpec(shape, lambda *_: (0,) * len(shape))


def per_device(
    block_input, segments, expert_ids, gate_values, cotangent, attn_gain,
    query_weight, kv_weight, out_weight, moe_gain, w_in, w_out,
):
    sec = lax.axis_index("section")
    dp = lax.axis_index("dp")
    t = lax.axis_index("tensor")
    n_dp = lax.axis_size("dp")
    n_t = lax.axis_size("tensor")
    first = sec == 0
    core0 = t % 2 == 0
    rows, width = block_input.shape[1], block_input.shape[2]
    seq = segments.shape[1]
    top = expert_ids.shape[3]
    heads = query_weight.shape[2] // HD
    qcols = heads * HD
    experts, ffn = w_in.shape[1], w_out.shape[2]
    cap = -(-(seq * top * 9 // (8 * E)) // 16) * 16
    slots = n_dp * cap
    flips = jnp.arange(n_t, dtype=jnp.int32) ^ t
    groups = n_dp // 2

    gain_all = lax.all_gather(
        jnp.stack([attn_gain[0], moe_gain[0]])[None], ("section", "dp", "tensor"), axis=0, tiled=True
    )
    gain_all = gain_all.reshape(2, n_dp * n_t, 2, -1).transpose(0, 2, 1, 3).reshape(2, 2, 1, width)
    gain_all = gain_all.astype(F32)

    shard = jnp.concatenate([query_weight[0], kv_turn(kv_weight[0])], axis=1)
    shard_far = by_section(shard)
    out_far = by_section(out_weight[0])
    layer_weights = []
    for l in range(2):
        here = sec == l
        qkv = lax.all_gather(jnp.where(here, shard, shard_far), "dp", axis=0, tiled=True)
        wo = lax.all_gather(jnp.where(here, out_weight[0], out_far), "dp", axis=1, tiled=True)
        kv_own = qkv[:, qcols:]
        kv_core = by_tensor(kv_own, 1)
        wkv = jnp.where(
            core0,
            jnp.concatenate([kv_own, kv_core], axis=1),
            jnp.concatenate([kv_core, kv_own], axis=1),
        )
        layer_weights.append((qkv[:, :qcols], wkv, wo))

    segment = jnp.where(first, segments[0], segments[1])
    ordinal = jnp.arange(seq, dtype=jnp.int32)
    start = jnp.sum((segment[None, :] < segment[:, None]).astype(jnp.int32), axis=1)
    places = (ordinal - start).astype(F32)

    def turned(vector):
        return vector.reshape(n_t, rows)[flips].reshape(seq)

    idx = turned(ordinal)
    start_col = turned(start)[:, None]
    frequency = THETA ** (-2.0 * jnp.arange(HD // 2, dtype=F32) / HD)
    angles = turned(places)[:, None] * frequency[None, :]
    cosine = jnp.cos(angles)
    cosine = jnp.concatenate([cosine, cosine], axis=1)
    sine = jnp.sin(angles)
    sine = jnp.concatenate([-sine, sine], axis=1)
    place_args = (cosine, sine, idx[None, :], idx[:, None], start_col)

    routing = jnp.concatenate([expert_ids[0].astype(F32), gate_values[0]], axis=2)
    routing = lax.all_gather(routing[None], "dp", axis=0, tiled=True)
    routing = routing[jnp.arange(n_dp, dtype=jnp.int32) ^ dp]
    routing = routing.reshape(n_dp, 2, n_t, rows, 2 * top)[:, :, flips].reshape(n_dp, 2, seq, 2 * top)
    names = (dp * experts + jnp.arange(experts, dtype=jnp.int32)).astype(F32)
    chosen = routing[:, :, :, :top, None] == names
    member = jnp.sum(chosen.astype(F32), axis=3)
    gates = jnp.sum(jnp.where(chosen, routing[:, :, :, top:, None], 0.0), axis=3)
    lower = (ordinal[:, None] > ordinal[None, :]).astype(BF)
    rank = jnp.einsum("ij,smje->smie", lower, member.astype(BF), preferred_element_type=F32)
    slot = rank + (jnp.arange(experts, dtype=jnp.int32) * cap).astype(F32)
    slot = jnp.where(member > 0.5, slot, -1.0).astype(jnp.int32)
    pos_col = slot.transpose(1, 0, 2, 3)
    pos_row = slot.transpose(1, 0, 3, 2)
    gate_row = gates.transpose(1, 0, 3, 2)

    block = jax.ShapeDtypeStruct((rows, width), BF)
    pair = jax.ShapeDtypeStruct((2, rows, width), BF)
    quad = jax.ShapeDtypeStruct((2, 2, rows, width), BF)

    def shape(*dims, dtype=BF):
        return jax.ShapeDtypeStruct(dims, dtype)

    def params(limit):
        return pltpu.CompilerParams(vmem_limit_bytes=limit * MIB)

    def attn_fwd(a_blocks, weights):
        return pl.pallas_call(
            functools.partial(attn_fwd_kernel, heads, rows),
            out_shape=(
                pair, pair, shape(seq, qcols), shape(seq, HD), shape(seq, HD),
                shape(seq, HD, dtype=F32), shape(seq, qcols),
            ),
            scratch_shapes=[pltpu.VMEM((seq, width), BF)],
            compiler_params=params(40),
            cost_estimate=pl.CostEstimate(
                flops=2 * seq * width * (2 * qcols + 2 * HD), bytes_accessed=6 * MIB, transcendentals=0
            ),
            name="attn_fwd",
        )(*a_blocks, *weights, *place_args)

    def attn_bwd(d_blocks, saved, weights):
        return pl.pallas_call(
            functools.partial(attn_bwd_kernel, heads, rows),
            out_shape=(pair, pair, shape(seq, qcols), shape(seq, 2 * HD)),
            scratch_shapes=[pltpu.VMEM((seq, width), BF)],
            compiler_params=params(40),
            cost_estimate=pl.CostEstimate(
                flops=2 * seq * width * (2 * qcols + 2 * HD), bytes_accessed=6 * MIB, transcendentals=0
            ),
            name="attn_bwd",
        )(*d_blocks, *saved, *weights, *place_args)

    def attn_wgrad(a_blocks, d_blocks, attended, dq, dkv):
        return pl.pallas_call(
            functools.partial(attn_wgrad_kernel, rows),
            out_shape=(shape(width, qcols), shape(width, HD), shape(width, HD), shape(qcols, width)),
            scratch_shapes=[pltpu.VMEM((seq, width), BF), pltpu.VMEM((seq, width), BF)],
            compiler_params=params(40),
            cost_estimate=pl.CostEstimate(
                flops=2 * seq * width * (2 * qcols + 2 * HD), bytes_accessed=6 * MIB, transcendentals=0
            ),
            name="attn_wgrad",
        )(*a_blocks, *d_blocks, attended, dq, dkv)

    def per_expert(*dims):
        return pl.BlockSpec((1,) + dims, lambda e: (e, 0, 0))

    route_specs = [
        whole((n_dp, experts, seq)), whole((n_dp, seq, experts)), whole((n_dp, experts, seq)),
    ]
    block_specs = [whole((2, rows, width))] * (2 * n_dp)
    sum_specs = [whole((2, 2, rows, width))] * n_dp
    seq_scratch = pltpu.VMEM((seq, width), BF)
    moe_flops = 2 * experts * slots * width * 3 * ffn + 4 * n_dp * experts * cap * seq * width

    def moe_fwd(blocks, b):
        out = pl.pallas_call(
            functools.partial(moe_fwd_kernel, experts, cap, rows, n_dp),
            grid=(experts,),
            in_specs=block_specs + route_specs + [per_expert(width, 2 * ffn), per_expert(ffn, width)],
            out_specs=[per_expert(slots, width), per_expert(slots, 2 * ffn)] + sum_specs,
            out_shape=[shape(experts, slots, width), shape(experts, slots, 2 * ffn, dtype=F32)]
            + [quad] * n_dp,
            scratch_shapes=[
                pltpu.VMEM((experts, slots, width), BF),
                pltpu.VMEM((n_dp, experts * cap, width), BF),
                pltpu.VMEM((n_dp, experts * cap, 1), F32),
                seq_scratch,
            ],
            compiler_params=params(56),
            cost_estimate=pl.CostEstimate(flops=moe_flops, bytes_accessed=20 * MIB, transcendentals=0),
            name="moe_fwd",
        )(*blocks, pos_row[b], pos_col[b], gate_row[b], w_in[0], w_out[0])
        return out[0], out[1], out[2 : 2 + groups], out[2 + groups :]

    def moe_bwd(blocks, gu, b):
        out = pl.pallas_call(
            functools.partial(moe_bwd_kernel, experts, cap, rows, n_dp),
            grid=(experts,),
            in_specs=block_specs
            + route_specs
            + [per_expert(slots, 2 * ffn), per_expert(width, 2 * ffn), per_expert(ffn, width)],
            out_specs=[per_expert(slots, width), per_expert(slots, ffn), per_expert(slots, 2 * ffn)]
            + sum_specs,
            out_shape=[
                shape(experts, slots, width), shape(experts, slots, ffn), shape(experts, slots, 2 * ffn),
            ]
            + [quad] * n_dp,
            scratch_shapes=[
                pltpu.VMEM((experts, slots, width), BF),
                pltpu.VMEM((n_dp, experts * cap, width), BF),
                seq_scratch,
            ],
            compiler_params=params(56),
            cost_estimate=pl.CostEstimate(flops=moe_flops, bytes_accessed=20 * MIB, transcendentals=0),
            name="moe_bwd",
        )(*blocks, pos_row[b], pos_col[b], gate_row[b], gu, w_in[0], w_out[0])
        return out[0], out[1], out[2], out[3 : 3 + groups], out[3 + groups :]

    def moe_wgrad(sets):
        def spec(which, *dims):
            return pl.BlockSpec((1,) + dims, lambda e, sel: (jnp.where(sel[0] == which, e, 0), 0, 0))

        in_specs = []
        for which in range(2):
            for dims in ((slots, width), (slots, 2 * ffn), (slots, ffn), (slots, width)):
                in_specs += [spec(which, *dims)] * 2
        return pl.pallas_call(
            moe_wgrad_kernel,
            grid_spec=pltpu.PrefetchScalarGridSpec(
                num_scalar_prefetch=1,
                grid=(experts,),
                in_specs=in_specs,
                out_specs=[
                    pl.BlockSpec((1, width, 2 * ffn), lambda e, sel: (e, 0, 0)),
                    pl.BlockSpec((1, ffn, width), lambda e, sel: (e, 0, 0)),
                ],
            ),
            out_shape=[
                shape(experts, width, 2 * ffn, dtype=F32), shape(experts, ffn, width, dtype=F32),
            ],
            compiler_params=params(56),
            cost_estimate=pl.CostEstimate(flops=2 * moe_flops, bytes_accessed=40 * MIB, transcendentals=0),
            name="moe_wgrad",
        )(sec.astype(jnp.int32)[None], *sets[0], *sets[1])

    def spread_pairs(own):
        parts = [own] + [by_dp(own, k) for k in range(1, n_dp)]
        return [jnp.stack(parts[2 * j : 2 * j + 2]) for j in range(groups)]

    def fill(pairs):
        return [value for pair_rows in pairs for value in over_tensor(pair_rows)]

    def to_host(own, host):
        near = spread_pairs(own)
        far = [to_section(pair_rows, host) for pair_rows in near]
        return fill(near), fill(far)

    def tensor_sums(keeps, sends):
        sums = []
        for keep, send in zip(keeps, sends):
            total = keep + by_tensor(send, 1)
            sums.append(total[0] + by_tensor(total[1], 2))
        return sums

    def from_host(near, far, host):
        here = sec == host
        near, far = tensor_sums(*near), tensor_sums(*far)
        total = None
        for j in reversed(range(groups)):
            back = lax.ppermute(far[j], "section", [(host, 1 - host)])
            mine = jnp.where(here, near[j], back)
            for i in reversed(range(2)):
                k = 2 * j + i
                term = (mine[i] if k == 0 else by_dp(mine[i], k)).astype(F32)
                total = term if total is None else total + term
        return total

    x = jnp.where(first, block_input[0], block_input[1])
    cot_far = by_section(jnp.where(first, cotangent[0, 1], cotangent[0, 0]))
    cot_near = jnp.where(first, cotangent[0, 0], cotangent[0, 1])
    cots = (jnp.where(first, cot_near, cot_far), jnp.where(first, cot_far, cot_near))

    kept = []
    outs = []
    experts_kept = []
    for l in range(2):
        r1 = inverse_rms(x)
        a_blocks = over_tensor((x * r1 * gain_all[l, 0]).astype(BF))
        keep, send, q, k, v, lse, attended = attn_fwd(a_blocks, layer_weights[l])
        part0, part1 = sum_over_tensor(keep, send)
        mid = x + (part0.astype(F32) + part1.astype(F32))
        r2 = inverse_rms(mid)
        m = (mid * r2 * gain_all[l, 1]).astype(BF)
        near, far = to_host(m, l)
        x_near, gu_near, *near_sums = moe_fwd(near, l)
        x_far, gu_far, *far_sums = moe_fwd(far, 1 - l)
        out = mid + from_host(near_sums, far_sums, l)
        kept.append((x, r1, a_blocks, (q, k, v, lse), attended, mid, r2))
        experts_kept.append((x_near, x_far, gu_near, gu_far))
        outs.append(out)
        x = out

    grads = [None, None]
    gain_sums = [None, None]
    in_grads = [None, None]
    sets = [None, None]
    g = cots[1]
    for l in (1, 0):
        x, r1, a_blocks, saved, attended, mid, r2 = kept[l]
        x_near, x_far, gu_near, gu_far = experts_kept[l]
        if l == 1:
            both = cotangent[0].astype(BF)
            parts = [both] + [by_dp(both, k) for k in range(1, n_dp)]
            near, far = (
                fill([jnp.stack([parts[2 * j][b], parts[2 * j + 1][b]]) for j in range(groups)])
                for b in (1, 0)
            )
        else:
            near, far = to_host(g.astype(BF), l)
        dr_near, z_near, dgu_near, *near_sums = moe_bwd(near, gu_near, l)
        dr_far, z_far, dgu_far, *far_sums = moe_bwd(far, gu_far, 1 - l)
        sets[l] = (x_near, x_far, dgu_near, dgu_far, z_near, z_far, dr_near, dr_far)
        dm = from_host(near_sums, far_sums, l)
        back, gain_moe_sum = norm_backward(mid, r2, gain_all[l, 1], dm)
        dmid = g + back
        d_blocks = over_tensor(dmid.astype(BF))
        keep, send, dq, dkv = attn_bwd(d_blocks, saved, layer_weights[l])
        part0, part1 = sum_over_tensor(keep, send)
        da = part0.astype(F32) + part1.astype(F32)
        back, gain_attn_sum = norm_backward(x, r1, gain_all[l, 0], da)
        in_grads[l] = dmid + back
        gain_sums[l] = jnp.stack([gain_attn_sum, gain_moe_sum])
        dwq, dwk, dwv, dwo = attn_wgrad(a_blocks, d_blocks, attended, dq, dkv)
        dwkv = jnp.where(core0, dwk, dwv) + by_tensor(jnp.where(core0, dwv, dwk), 1)
        grads[l] = (jnp.concatenate([dwq, dwkv], axis=1), dwo)
        if l == 1:
            g = cots[0] + in_grads[1]

    dw_in, dw_out = moe_wgrad(sets)

    qrows = query_weight.shape[1]
    ocols = out_weight.shape[2]

    def dp_sum(value, size, axis):
        total = None
        for k in reversed(range(n_dp)):
            piece = lax.dynamic_slice_in_dim(value, (dp ^ k) * size, size, axis)
            term = (piece if k == 0 else by_dp(piece, k)).astype(F32)
            total = term if total is None else total + term
        return total

    reduced = [(dp_sum(grads[l][0], qrows, 0), dp_sum(grads[l][1], ocols, 1)) for l in range(2)]

    def at_home(value0, value1):
        far = by_section(jnp.where(first, value1, value0).astype(BF)).astype(F32)
        return jnp.where(first, value0, value1) + far

    grad_qkv = at_home(reduced[0][0], reduced[1][0])
    grad_out = at_home(reduced[0][1], reduced[1][1])
    grad_kv = kv_turn(grad_qkv[:, qcols:])

    gains = jnp.stack(gain_sums)
    gains = gains + by_tensor(gains, 1)
    gains = gains + by_tensor(gains, 2)
    flip = 1
    while flip < n_dp:
        gains = gains + by_dp(gains, flip)
        flip *= 2
    gains = jnp.where(first, gains[0], gains[1]) + by_section(jnp.where(first, gains[1], gains[0]))
    cols = attn_gain.shape[1]
    gains = lax.dynamic_slice_in_dim(gains, (dp * n_t + t) * cols, cols, 1)

    def both_batches(value0, value1):
        far = by_section(jnp.where(first, value1, value0).astype(BF)).astype(F32)
        near = jnp.where(first, value0, value1)
        return jnp.stack([jnp.where(first, near, far), jnp.where(first, far, near)])[None]

    return (
        both_batches(*outs),
        both_batches(*in_grads),
        gains[0:1],
        grad_qkv[None, :, :qcols],
        grad_kv[None],
        grad_out[None],
        gains[1:2],
        dw_in[None],
        dw_out[None],
    )


def solution(mesh):
    return jax.shard_map(
        per_device,
        mesh=mesh,
        in_specs=(
            P(None, ("dp", "tensor"), None),
            P(None, "dp"),
            P("section", None, "dp", None),
            P("section", None, "dp", None),
            P("section", None, ("dp", "tensor"), None),
            P("section", ("dp", "tensor")),
            P("section", "dp", "tensor"),
            P("section", "dp", "tensor"),
            P("section", "tensor", "dp"),
            P("section", ("dp", "tensor")),
            P("section", "dp", None, "tensor"),
            P("section", "dp", "tensor", None),
        ),
        out_specs=(
            P("section", None, ("dp", "tensor"), None),
            P("section", None, ("dp", "tensor"), None),
            P("section", ("dp", "tensor")),
            P("section", "dp", "tensor"),
            P("section", "dp", "tensor"),
            P("section", "tensor", "dp"),
            P("section", ("dp", "tensor")),
            P("section", "dp", None, "tensor"),
            P("section", "dp", "tensor", None),
        ),
        check_vma=False,
    )
```

```python
import functools

import jax
import jax.numpy as jnp
from jax import lax
from jax.experimental import pallas as pl
from jax.experimental.pallas import tpu as pltpu
from jax.sharding import PartitionSpec as P

H = 12
KVH = 2
HD = 128
E = 16

EPS = 1e-06
THETA = 10000.0
BF = jnp.bfloat16
F32 = jnp.float32
MIB = 1024 * 1024
COST = 4
IN_VMEM = 4


def dot(a, b, ca, cb):
    return lax.dot_general(a, b, (((ca,), (cb,)), ((), ())), preferred_element_type=F32)


def move(value, section=0, dp=0, tensor=0):
    n_dp, n_t = lax.axis_size("dp"), lax.axis_size("tensor")
    pairs = []
    for s in range(2):
        for d in range(n_dp):
            for t in range(n_t):
                here = (s * n_dp + d) * n_t + t
                pairs.append((here, ((s ^ section) * n_dp + (d ^ dp)) * n_t + (t ^ tensor)))
    return lax.ppermute(value, ("section", "dp", "tensor"), pairs)


def kv_turn(value):
    return lax.ppermute(value, "tensor", [(0, 0), (1, 2), (2, 1), (3, 3)])


def over_tensor(value):
    across = move(value, tensor=2)
    return [value, move(value, tensor=1), across, move(across, tensor=1)]


def after(value, *tokens):
    return jnp.where(there(*tokens), value, jnp.zeros_like(value))


def there(*tokens):
    marks = [token[(0,) * token.ndim].astype(F32) for token in tokens]
    total = functools.reduce(jnp.add, marks)
    return total == total


def sum_over_tensor(keep, send):
    total = keep + move(send, tensor=1)
    return total[0], move(total[1], tensor=2)


def rope(value, cosine, sine):
    return value * cosine + pltpu.roll(value, HD // 2, 1) * sine


def allowed_pairs(idx_row, idx_col, start_col):
    keys = idx_row[...]
    return (keys <= idx_col[...]) & (keys >= start_col[...])


def assemble(refs, weights):
    (blocks,) = refs
    n_dp, half = blocks.shape[1:3]
    for k in range(n_dp):
        for part in range(2):
            at = (2 * k + part) * half
            weights[at : at + half, :] = blocks[part, k]


def whole_sequence(blocks, into):
    rows = blocks[0].shape[0]
    for r, ref in enumerate(blocks):
        into[r * rows : (r + 1) * rows, :] = ref[...]


def attn_fwd_kernel(heads, n_w, me, *refs):
    w_refs, ins, outs, (a_all, weights) = take(refs, n_w, 9, 7, 2)
    a0, a1, a2, a3, cosine, sine, idx_row, idx_col, start_col = ins
    keep, send, q_out, k_out, v_out, lse_out, o_out = outs
    rows, qcols = a0.shape[0], heads * HD
    assemble(w_refs, weights)
    whole_sequence((a0, a1, a2, a3), a_all)
    qkv = dot(a_all[...], weights[:, : qcols + 2 * HD], 1, 0)
    co, si = cosine[...], sine[...]
    k = rope(qkv[:, qcols : qcols + HD], co, si).astype(BF)
    v = qkv[:, qcols + HD :].astype(BF)
    k_out[...] = k
    v_out[...] = v
    allowed = allowed_pairs(idx_row, idx_col, start_col)
    lane = lax.broadcasted_iota(jnp.int32, (k.shape[0], HD), 1)
    lse_all = jnp.zeros((k.shape[0], HD), F32)
    for h in range(heads):
        qh = rope(qkv[:, h * HD : (h + 1) * HD], co, si).astype(BF)
        q_out[:, h * HD : (h + 1) * HD] = qh
        s = jnp.where(allowed, HD ** (-0.5) * dot(qh, k, 1, 1), -1e30)
        top = jnp.max(s, axis=1, keepdims=True)
        lse = top + jnp.log(jnp.sum(jnp.exp(s - top), axis=1, keepdims=True))
        p = jnp.exp(s - lse).astype(BF)
        o_out[:, h * HD : (h + 1) * HD] = dot(p, v, 1, 0).astype(BF)
        lse_all = jnp.where(lane == h, lse, lse_all)
    lse_out[...] = lse_all
    part = dot(o_out[...], weights[:, qcols + 2 * HD :], 1, 1).astype(BF)
    for r in range(4):
        (send if r % 2 else keep)[r // 2] = part[r * rows : (r + 1) * rows, :]


def attn_bwd_kernel(heads, n_w, me, *refs):
    w_refs, ins, outs, (d_all, weights, dqkv) = take(refs, n_w, 13, 5, 3)
    d0, d1, d2, d3, q_in, k_in, v_in, lse_in, cosine, sine, idx_row, idx_col, start_col = ins
    keep, send, dq_out, kv_keep, kv_send = outs
    rows, qcols = d0.shape[0], heads * HD
    assemble(w_refs, weights)
    whole_sequence((d0, d1, d2, d3), d_all)
    do = dot(d_all[...], weights[:, qcols + 2 * HD :], 1, 0).astype(BF)
    co, si = cosine[...], -sine[...]
    k, v = k_in[...], v_in[...]
    allowed = allowed_pairs(idx_row, idx_col, start_col)
    dk = jnp.zeros((do.shape[0], HD), F32)
    dv = jnp.zeros((do.shape[0], HD), F32)
    for h in range(heads):
        qh = q_in[:, h * HD : (h + 1) * HD]
        doh = do[:, h * HD : (h + 1) * HD]
        s = jnp.where(allowed, HD ** (-0.5) * dot(qh, k, 1, 1), -1e30)
        p = jnp.exp(s - lse_in[:, h : h + 1])
        dv = dv + dot(p.astype(BF), doh, 0, 0)
        dp = dot(doh, v, 1, 1)
        ds = (p * (dp - jnp.sum(p * dp, axis=1, keepdims=True))).astype(BF)
        dq = HD ** (-0.5) * dot(ds, k, 1, 0)
        dk = dk + dot(ds, qh, 0, 0)
        dqkv[:, h * HD : (h + 1) * HD] = rope(dq, co, si).astype(BF)
    dk = rope(HD ** (-0.5) * dk, co, si).astype(BF)
    dv = dv.astype(BF)
    dqkv[:, qcols : qcols + HD] = dk
    dqkv[:, qcols + HD :] = dv
    dq_out[...] = dqkv[:, :qcols]
    core0 = me[2] == 0
    kv_keep[...] = jnp.where(core0, dk, dv)
    kv_send[...] = jnp.where(core0, dv, dk)
    part = dot(dqkv[...], weights[:, : qcols + 2 * HD], 1, 1).astype(BF)
    for r in range(4):
        (send if r % 2 else keep)[r // 2] = part[r * rows : (r + 1) * rows, :]


def total_of(terms, places):
    total = None
    for ref, place in zip(terms, places):
        term = (ref[...] if place is None else ref[place]).astype(F32)
        total = term if total is None else total + term
    return total


def finish_kernel(places, base, gain, *refs):
    terms, (out, normed) = refs[: len(places)], refs[len(places) :]
    total = base[...]
    if places:
        total = total + total_of(terms, places)
    out[...] = total
    r = lax.rsqrt(jnp.mean(total * total, axis=1, keepdims=True) + EPS)
    normed[...] = (total * r * gain[...]).astype(BF)


def norm_back_kernel(places, rows_in, gain, upper, *refs):
    terms, rest = refs[: len(places)], refs[len(places) :]
    grad = total_of(terms, places)
    x = rows_in[...]
    r = lax.rsqrt(jnp.mean(x * x, axis=1, keepdims=True) + EPS)
    weighted = grad * gain[...]
    projected = jnp.mean(weighted * x, axis=1, keepdims=True)
    total = upper[...] + (r * weighted - x * (r * r * r) * projected)
    if len(rest) == 3:
        out, low, gain_sum = rest
        low[...] = total.astype(BF)
    else:
        more, out, following, low, gain_sum = rest
        after = more[...] + total
        following[...] = after
        low[...] = after.astype(BF)
    out[...] = total
    gain_sum[...] = jnp.sum(grad * x * r, axis=0, keepdims=True)


def split_rows(me, n_dp, grad, mine, theirs, flipped):
    half = grad.shape[0] // (2 * n_dp)
    for k in range(n_dp):
        start = (me[0] ^ k if flipped else k) * (2 * half)
        near = pl.multiple_of(start + me[1] * half, 16)
        far = pl.multiple_of(start + (1 - me[1]) * half, 16)
        mine[k] = grad[pl.ds(near, half), :]
        theirs[k] = grad[pl.ds(far, half), :]


def out_grad(blocks, attended, d_all, into):
    whole_sequence(blocks, d_all)
    into[...] = dot(d_all[...], attended[...], 0, 0).astype(BF)


def qkv_grad(blocks, dq, kv_keep, kv_got, a_all, into):
    whole_sequence(blocks, a_all)
    a = a_all[...]
    qcols = dq.shape[1]
    into[:, :qcols] = dot(a, dq[...], 0, 0).astype(BF)
    rows = blocks[0].shape[0]
    got = [kv_got[r * rows : (r + 1) * rows, :] for r in (1, 0, 3, 2)]
    kv = (kv_keep[...].astype(F32) + jnp.concatenate(got, axis=0).astype(F32)).astype(BF)
    into[:, qcols : qcols + HD] = dot(a, kv, 0, 0).astype(BF)


def attn_wgrad_kernel(
    flipped, n_dp, me, a0, a1, a2, a3, dq, kv_keep, kv_got, d0, d1, d2, d3, attended, mine, theirs, tokens, grad
):
    cols = dq.shape[1] + HD
    qkv_grad((a0, a1, a2, a3), dq, kv_keep, kv_got, tokens, grad.at[:, :cols])
    out_grad((d0, d1, d2, d3), attended, tokens, grad.at[:, cols:])
    split_rows(me, n_dp, grad, mine, theirs, flipped)


def slot_rows(pos_row, s, experts, cap):
    slot = lax.broadcasted_iota(jnp.int32, (cap, pos_row.shape[2]), 0)
    hits = [(slot == pos_row[s, e : e + 1, :]).astype(F32) for e in range(experts)]
    return jnp.concatenate(hits, axis=0).astype(BF)


def start_all(*copies):
    for copy in copies:
        copy.start()
    return list(copies)


def wait_all(copies):
    for copy in copies:
        copy.wait()


def slot_gates(hit, gate_cols, s, experts, cap):
    both = dot(hit, gate_cols[s], 1, 0)
    lane = lax.broadcasted_iota(jnp.int32, both.shape, 1)
    own = lax.broadcasted_iota(jnp.int32, both.shape, 0) // cap
    return jnp.sum(jnp.where((lane == own) | (lane == own + experts), both, 0.0), axis=1, keepdims=True)


def gathered(me, ref, batch, count):
    return [[(ref, ((me[0] ^ s) * 4 + (me[3] ^ r), batch)) for r in range(4)] for s in range(count)]


def dispatch(blocks, tokens, pos_row, gate_cols, into, gates, experts, cap, scaled, fetched=None):
    for s, places in enumerate(blocks):
        for r, (ref, at) in enumerate(places):
            rows = ref.shape[-2]
            if fetched is not None:
                fetched[s][r].wait()
            elif len(blocks) > IN_VMEM:
                pltpu.sync_copy(ref.at[at], tokens.at[pl.ds(r * rows, rows)])
            else:
                tokens[s, r * rows : (r + 1) * rows, :] = ref[at]
        sequence = tokens if len(blocks) > IN_VMEM else tokens.at[s]
        hit = slot_rows(pos_row, s, experts, cap)
        picked = dot(hit, sequence[...], 1, 0)
        if scaled:
            picked = picked * slot_gates(hit, gate_cols, s, experts, cap)
        elif gates is not None:
            gates[s] = slot_gates(hit, gate_cols, s, experts, cap)
        picked = picked.astype(BF)
        for e in range(experts):
            into[e, s * cap : (s + 1) * cap, :] = picked[e * cap : (e + 1) * cap, :]


def place(out, result, e, cap, gates):
    for s in range(result.shape[0]):
        value = out[s * cap : (s + 1) * cap, :]
        if gates is not None:
            value = value * gates[s, e * cap : (e + 1) * cap, :]
        result[s, e * cap : (e + 1) * cap, :] = value.astype(BF)


def combine(values, pos_row, keep, send, experts, cap, rows):
    for s in range(values.shape[0]):
        total = dot(slot_rows(pos_row, s, experts, cap), values[s], 0, 0).astype(BF)
        for r in range(4):
            (send if r % 2 else keep)[r // 2, s] = total[r * rows : (r + 1) * rows, :]


def silu_parts(gu):
    half = gu.shape[1] // 2
    gate, up = gu[:, :half], gu[:, half:]
    sg = 1.0 / (1.0 + jnp.exp(-gate))
    return gate, up, sg


def gate_up_grad(dz, gu, out):
    half = gu.shape[1] // 2
    gate, up, sg = silu_parts(gu)
    out[:, :half] = (dz * up * sg * (1.0 + gate * (1.0 - sg))).astype(BF)
    out[:, half:] = (dz * gate * sg).astype(BF)


def take(refs, *counts):
    parts, at = [], 0
    for count in counts:
        parts.append(refs[at : at + count])
        at += count
    return parts


def sequences(refs, count):
    return [[(refs[r], s) for r in range(4)] for s in range(count)]


def expert_weights(w_in, w_out, wi, wo, sems):
    return [
        start_all(
            pltpu.make_async_copy(w_in.at[e], wi.at[e], sems.at[2 * e]),
            pltpu.make_async_copy(w_out.at[e], wo.at[e], sems.at[2 * e + 1]),
        )
        for e in range(w_in.shape[0])
    ]


def moe_fwd_kernel(experts, cap, rows, count, *refs):
    blocks, ins, outs, scratch = take(refs, 4, 4, 4, 8)
    pos_row, gate_cols, w_in, w_out = ins
    x_out, gu_out, keep, send = outs
    tokens, x_all, result, gates, gu_all, wi, wo, sems = scratch
    weights = expert_weights(w_in, w_out, wi, wo, sems)
    dispatch(sequences(blocks, count), tokens, pos_row, gate_cols, x_all, gates, experts, cap, False)
    done = start_all(pltpu.make_async_copy(x_all, x_out, sems.at[2 * experts]))
    for e in range(experts):
        wait_all(weights[e])
        gu = dot(x_all[e], wi[e], 1, 0)
        gu_all[e] = gu
        gate, up, sg = silu_parts(gu)
        z = (gate * sg * up).astype(BF)
        place(dot(z, wo[e], 1, 0), result, e, cap, gates)
    done += start_all(pltpu.make_async_copy(gu_all, gu_out, sems.at[2 * experts + 1]))
    combine(result, pos_row, keep, send, experts, cap, rows)
    wait_all(done)


def moe_bwd_kernel(experts, cap, rows, count, *refs):
    blocks, ins, outs, scratch = take(refs, 4, 5, 5, 9)
    pos_row, gate_cols, gu_in, w_in, w_out = ins
    dr_out, z_out, dgu_out, keep, send = outs
    tokens, dr_all, result, gu_all, z_all, dgu_all, wi, wo, sems = scratch
    fetched = start_all(pltpu.make_async_copy(gu_in, gu_all, sems.at[2 * experts + 3]))
    weights = expert_weights(w_in, w_out, wi, wo, sems)
    dispatch(sequences(blocks, count), tokens, pos_row, gate_cols, dr_all, None, experts, cap, True)
    done = start_all(pltpu.make_async_copy(dr_all, dr_out, sems.at[2 * experts]))
    wait_all(fetched)
    for e in range(experts):
        wait_all(weights[e])
        gu = gu_all[e]
        gate, up, sg = silu_parts(gu)
        z_all[e] = (gate * sg * up).astype(BF)
        gate_up_grad(dot(dr_all[e], wo[e], 1, 1), gu, dgu_all.at[e])
        place(dot(dgu_all[e], wi[e], 1, 1), result, e, cap, None)
    done += start_all(
        pltpu.make_async_copy(z_all, z_out, sems.at[2 * experts + 1]),
        pltpu.make_async_copy(dgu_all, dgu_out, sems.at[2 * experts + 2]),
    )
    combine(result, pos_row, keep, send, experts, cap, rows)
    wait_all(done)


def moe_turn_kernel(experts, cap, rows, count, batch, me, *refs):
    blocks, (grads,), ins, outs, scratch = take(refs, 4, 1, 4, 6, 11)
    pos_row, gate_cols, w_in, w_out = ins
    x_out, z_out, dr_out, dgu_out, keep, send = outs
    tokens, x_all, dr_all, result, z_all, dgu_all, wi, wo, sems, grad_tokens, block_sems = scratch
    weights = expert_weights(w_in, w_out, wi, wo, sems)
    places = gathered(me, grads, batch, count)
    if count <= IN_VMEM:
        copies = [
            start_all(*[
                pltpu.make_async_copy(
                    ref.at[at], grad_tokens.at[s, pl.ds(r * rows, rows)], block_sems.at[s, r]
                )
                for r, (ref, at) in enumerate(places[s])
            ])
            for s in range(count)
        ]
        routed = pos_row, gate_cols
        dispatch(sequences(blocks, count), tokens, *routed, x_all, None, experts, cap, False)
        done = start_all(pltpu.make_async_copy(x_all, x_out, sems.at[2 * experts + 1]))
        dispatch(places, grad_tokens, *routed, dr_all, None, experts, cap, True, copies)
    else:
        dispatch(sequences(blocks, count), tokens, pos_row, gate_cols, x_all, None, experts, cap, False)
        done = start_all(pltpu.make_async_copy(x_all, x_out, sems.at[2 * experts + 1]))
        dispatch(places, tokens, pos_row, gate_cols, dr_all, None, experts, cap, True)
    done += start_all(pltpu.make_async_copy(dr_all, dr_out, sems.at[2 * experts]))
    for e in range(experts):
        wait_all(weights[e])
        gu = dot(x_all[e], wi[e], 1, 0)
        gate, up, sg = silu_parts(gu)
        z_all[e] = (gate * sg * up).astype(BF)
        gate_up_grad(dot(dr_all[e], wo[e], 1, 1), gu, dgu_all.at[e])
        place(dot(dgu_all[e], wi[e], 1, 1), result, e, cap, None)
    done += start_all(
        pltpu.make_async_copy(z_all, z_out, sems.at[2 * experts + 2]),
        pltpu.make_async_copy(dgu_all, dgu_out, sems.at[2 * experts + 3]),
    )
    combine(result, pos_row, keep, send, experts, cap, rows)
    wait_all(done)


def moe_out_kernel(experts, cap, rows, count, me, z, pos_row, gate_cols, w_out, keep, send, result):
    gates = []
    for s in range(count):
        gates.append(slot_gates(slot_rows(pos_row, s, experts, cap), gate_cols, s, experts, cap))
    for e in range(experts):
        out = dot(z[e], w_out[e], 1, 0)
        for s in range(count):
            value = out[s * cap : (s + 1) * cap, :] * gates[s][e * cap : (e + 1) * cap, :]
            result[s, e * cap : (e + 1) * cap, :] = value.astype(BF)
    for s in range(count):
        total = dot(slot_rows(pos_row, s, experts, cap), result[s], 0, 0).astype(BF)
        for r in range(4):
            (send if r % 2 else keep)[r // 2, me[0] ^ s] = total[r * rows : (r + 1) * rows, :]


def moe_wgrad_kernel(sel, *refs):
    first, second, (_, dwin, dwout) = refs[:8], refs[8:16], refs[16:]

    def run(x0, x1, dg0, dg1, z0, z1, dr0, dr1):
        dwin[0] = dot(x0[0], dg0[0], 0, 0) + dot(x1[0], dg1[0], 0, 0)
        dwout[0] = dot(z0[0], dr0[0], 0, 0) + dot(z1[0], dr1[0], 0, 0)

    @pl.when(sel[0] == 0)
    def _():
        run(*first)

    @pl.when(sel[0] == 1)
    def _():
        run(*second)


def per_device(
    block_input, segments, expert_ids, gate_values, cotangent, attn_gain,
    query_weight, kv_weight, out_weight, moe_gain, w_in, w_out,
):
    sec = lax.axis_index("section")
    dp = lax.axis_index("dp")
    t = lax.axis_index("tensor")
    n_dp = lax.axis_size("dp")
    n_t = lax.axis_size("tensor")
    first = sec == 0
    core0 = t % 2 == 0
    me = jnp.stack([dp, sec, t % 2, t]).astype(jnp.int32)
    rows, width = block_input.shape[1], block_input.shape[2]
    seq = segments.shape[1]
    top = expert_ids.shape[3]
    heads = query_weight.shape[2] // HD
    qcols = heads * HD
    experts, ffn = w_in.shape[1], w_out.shape[2]
    cap = -(-(seq * top * 9 // (8 * E)) // 16) * 16
    slots = n_dp * cap
    dp_order = jnp.arange(n_dp, dtype=jnp.int32) ^ dp
    t_order = jnp.arange(n_t, dtype=jnp.int32) ^ t
    drows = width // n_dp
    half = drows // 2

    pair = jax.ShapeDtypeStruct((2, rows, width), BF)
    smem = pl.BlockSpec(memory_space=pltpu.SMEM)
    vmem = pl.BlockSpec(memory_space=pltpu.VMEM)
    any_space = pl.BlockSpec(memory_space=pl.ANY)
    hbm = pl.BlockSpec(memory_space=pltpu.HBM)
    seq_scratch = pltpu.VMEM((seq, width), BF)

    def shape(*dims, dtype=BF):
        return jax.ShapeDtypeStruct(dims, dtype)

    def call(
        kernel, name, ins, outs, scratch, limit, cost, in_specs=None, out_specs=None, hold=(), tokens=()
    ):
        n_ins, n_outs, n_hold, n_tok = len(ins), len(outs), len(hold), len(tokens)

        def body(*refs):
            given, results, rest = take(refs, n_ins + n_tok + n_hold, n_outs + n_hold, len(scratch))
            kernel(*given[:n_ins], *results[:n_outs], *rest)

        out = pl.pallas_call(
            body,
            out_shape=list(outs) + [jax.ShapeDtypeStruct(h.shape, h.dtype) for h in hold],
            in_specs=(in_specs or [smem] + [vmem] * (n_ins - 1)) + [any_space] * (n_tok + n_hold),
            out_specs=(out_specs or [vmem] * n_outs) + [any_space] * n_hold,
            scratch_shapes=scratch,
            input_output_aliases={n_ins + n_tok + i: n_outs + i for i in range(n_hold)},
            compiler_params=pltpu.CompilerParams(vmem_limit_bytes=limit * MIB),
            cost_estimate=pl.CostEstimate(flops=cost * 10**9, bytes_accessed=cost * 3 * MIB, transcendentals=0),
            name=name,
        )(*ins, *tokens, *hold)
        return out[:n_outs], out[n_outs:]

    acols = 2 * qcols + 2 * HD
    weights_scratch = pltpu.VMEM((width, acols), BF)

    def attn_fwd(a_blocks, weights, token=()):
        ins = (me, *weights, *a_blocks, *place_args)
        outs = [
            pair, pair, shape(seq, qcols), shape(seq, HD), shape(seq, HD),
            shape(seq, HD, dtype=F32), shape(seq, qcols),
        ]
        return call(
            functools.partial(attn_fwd_kernel, heads, len(weights)), "attn_fwd",
            ins, outs, [seq_scratch, weights_scratch], 20, 0, tokens=token,
        )

    def attn_bwd(d_blocks, saved, weights, tokens=()):
        ins = (me, *weights, *d_blocks, *saved, *place_args)
        return call(
            functools.partial(attn_bwd_kernel, heads, len(weights)), "attn_bwd",
            ins, [pair, pair, shape(seq, qcols), shape(seq, HD), shape(seq, HD)],
            [seq_scratch, weights_scratch, pltpu.VMEM((seq, qcols + 2 * HD), BF)], 20, 0, tokens=tokens,
        )

    tok_f32, tok_bf = shape(rows, width, dtype=F32), shape(rows, width)

    def finish(base, gain, terms, hold=()):
        (out, normed), held = call(
            functools.partial(finish_kernel, [at for _, at in terms]), "finish",
            (base, gain, *[value for value, _ in terms]), [tok_f32, tok_bf], [], 8, 0,
            [vmem] * (2 + len(terms)), hold=hold,
        )
        return out, normed, held

    def norm_back(x, gain, upper, terms, more=(), tokens=()):
        return call(
            functools.partial(norm_back_kernel, [at for _, at in terms]), "norm_back",
            (x, gain, upper, *[value for value, _ in terms], *more),
            [tok_f32] * (1 + len(more)) + [tok_bf, shape(1, width, dtype=F32)], [], 8, 0,
            [vmem] * (3 + len(terms) + len(more)), tokens=tokens,
        )

    def halves_grad(kernel, name, ins, cols):
        return call(
            functools.partial(kernel, n_dp), name, (me, *ins), [shape(n_dp, half, cols)] * 2,
            [seq_scratch, pltpu.VMEM((width, cols), BF)], 20, 1,
        )[0]

    slot_scratch = pltpu.VMEM((experts, slots, width), BF)
    token_scratch = pltpu.VMEM((n_dp, seq, width), BF) if n_dp <= IN_VMEM else seq_scratch
    result_scratch = pltpu.VMEM((n_dp, experts * cap, width), BF)
    weight_scratch = [pltpu.VMEM((experts, width, 2 * ffn), BF), pltpu.VMEM((experts, ffn, width), BF)]
    z_scratch = pltpu.VMEM((experts, slots, ffn), BF)
    dgu_scratch = pltpu.VMEM((experts, slots, 2 * ffn), BF)
    gu_scratch = pltpu.VMEM((experts, slots, 2 * ffn), F32)
    copy_sems = pltpu.SemaphoreType.DMA((2 * experts + 4,))
    row_shape = shape(experts, slots, width)
    gu_shape = shape(experts, slots, 2 * ffn, dtype=F32)
    z_shape = shape(experts, slots, ffn)
    dgu_shape = shape(experts, slots, 2 * ffn)
    sum_shapes = [shape(2, n_dp, rows, width)] * 2
    limit = 48
    block_space = vmem if n_dp <= IN_VMEM else hbm
    expert_args = (w_in[0], w_out[0])

    def moe_fwd(blocks, b, tokens=(), hold=()):
        (x, gu, keep, send), held = call(
            functools.partial(moe_fwd_kernel, experts, cap, rows, n_dp), "moe_fwd",
            (*blocks, *routes[b], *expert_args), [row_shape, gu_shape] + sum_shapes,
            [
                token_scratch, slot_scratch, result_scratch, pltpu.VMEM((n_dp, experts * cap, 1), F32),
                gu_scratch, *weight_scratch, copy_sems,
            ],
            limit, COST, [block_space] * 4 + [vmem] * 2 + [hbm] * 2, [hbm] * 2 + [vmem] * 2,
            hold, tokens,
        )
        return (x, gu), (keep, send), held

    def moe_bwd(blocks, gu, b, tokens=(), hold=()):
        (dr, z, dgu, keep, send), held = call(
            functools.partial(moe_bwd_kernel, experts, cap, rows, n_dp), "moe_bwd",
            (*blocks, *routes[b], gu, *expert_args), [row_shape, z_shape, dgu_shape] + sum_shapes,
            [
                token_scratch, slot_scratch, result_scratch, gu_scratch, z_scratch, dgu_scratch,
                *weight_scratch, copy_sems,
            ],
            limit, COST, [block_space] * 4 + [vmem] * 2 + [hbm] * 3, [hbm] * 3 + [vmem] * 2,
            hold, tokens,
        )
        return (dgu, z, dr), (keep, send), held

    def moe_turn(blocks, grads, b, tokens=()):
        (x, z, dr, dgu, keep, send), _ = call(
            functools.partial(moe_turn_kernel, experts, cap, rows, n_dp, b), "moe_turn",
            (me, *blocks, grads, *routes[b], *expert_args),
            [row_shape, z_shape, row_shape, dgu_shape] + sum_shapes,
            [
                token_scratch, slot_scratch, slot_scratch, result_scratch, z_scratch, dgu_scratch,
                *weight_scratch, copy_sems,
                token_scratch,
                pltpu.SemaphoreType.DMA((n_dp, 4)),
            ],
            limit + 4, COST * 2,
            [smem] + [block_space] * 4 + [hbm] + [vmem] * 2 + [hbm] * 2,
            [hbm] * 4 + [vmem] * 2, tokens=tokens,
        )
        return (x, dgu, z, dr), (keep, send)

    def moe_out(z, b, *tokens):
        return call(
            functools.partial(moe_out_kernel, experts, cap, rows, n_dp), "moe_out",
            (me, z, *routes[b], w_out[0]), sum_shapes, [result_scratch], 20, COST, tokens=tokens,
        )[0]

    def moe_wgrad(sets, token):
        def spec(which, *dims):
            return pl.BlockSpec((1,) + dims, lambda e, sel: (jnp.where(sel[0] == which, e, 0), 0, 0))

        in_specs = []
        for which in range(2):
            for dims in ((slots, width), (slots, 2 * ffn), (slots, ffn), (slots, width)):
                in_specs += [spec(which, *dims)] * 2
        flat = [value for which in range(2) for parts in zip(*sets[which]) for value in parts]
        return pl.pallas_call(
            moe_wgrad_kernel,
            grid_spec=pltpu.PrefetchScalarGridSpec(
                num_scalar_prefetch=1,
                grid=(experts,),
                in_specs=in_specs + [any_space],
                out_specs=[
                    pl.BlockSpec((1, width, 2 * ffn), lambda e, sel: (e, 0, 0)),
                    pl.BlockSpec((1, ffn, width), lambda e, sel: (e, 0, 0)),
                ],
            ),
            out_shape=[
                shape(experts, width, 2 * ffn, dtype=F32), shape(experts, ffn, width, dtype=F32),
            ],
            compiler_params=pltpu.CompilerParams(vmem_limit_bytes=48 * MIB),
            cost_estimate=pl.CostEstimate(flops=10**10, bytes_accessed=40 * MIB, transcendentals=0),
            name="moe_wgrad",
        )(sec.astype(jnp.int32)[None], *flat, token)

    gains = jnp.concatenate([attn_gain, moe_gain], axis=0)
    gains = jnp.stack(over_tensor(gains))[t_order].transpose(1, 0, 2).reshape(2, drows)
    gains = jnp.stack([gains] + [move(gains, dp=k) for k in range(1, n_dp)])[dp_order]
    gains = gains.transpose(1, 0, 2).reshape(2, 1, width)
    gains_far = move(gains, section=1)
    layer_gain = [jnp.where(sec == l, gains, gains_far).astype(F32) for l in range(2)]
    (gains0, gains1) = layer_gain

    def seeds_of(matrix):
        low, high = matrix[:half], matrix[half:]
        return jnp.where(first, low, high), move(jnp.where(first, high, low), section=1)

    def gather_weights(seed):
        return lax.all_gather(seed[None, None], ("section", "dp"), axis=0, tiled=True).reshape(
            2, n_dp, half, acols
        )

    kv_own = kv_turn(kv_weight[0])
    kv_core = move(kv_own, tensor=1)
    key_value = jnp.where(
        core0, jnp.concatenate([kv_own, kv_core], axis=1), jnp.concatenate([kv_core, kv_own], axis=1)
    )
    routing = jnp.concatenate([expert_ids[0].astype(F32), gate_values[0]], axis=2)
    routing = [routing] + [move(routing, dp=k) for k in range(1, n_dp)]
    seed_near, seed_far = seeds_of(
        jnp.concatenate([query_weight[0], key_value, out_weight[0].T], axis=1)
    )

    segment = jnp.where(first, segments[0], segments[1])
    ordinal = jnp.arange(seq, dtype=jnp.int32)
    start = jnp.sum((segment[None, :] < segment[:, None]).astype(jnp.int32), axis=1)
    places = (ordinal - start).astype(F32)

    def turned(vector):
        return vector.reshape(n_t, rows)[t_order].reshape(seq)

    idx = turned(ordinal)
    start_col = turned(start)[:, None]
    frequency = THETA ** (-2.0 * jnp.arange(HD // 2, dtype=F32) / HD)
    angles = turned(places)[:, None] * frequency[None, :]
    cosine = jnp.cos(angles)
    cosine = jnp.concatenate([cosine, cosine], axis=1)
    sine = jnp.sin(angles)
    sine = jnp.concatenate([-sine, sine], axis=1)
    place_args = (cosine, sine, idx[None, :], idx[:, None], start_col)

    def routes_of(routing):
        routing = jnp.stack(routing)
        routing = routing.reshape(n_dp, 2, n_t, rows, 2 * top)[:, :, t_order]
        routing = routing.reshape(n_dp, 2, seq, 2 * top)
        names = (dp * experts + jnp.arange(experts, dtype=jnp.int32)).astype(F32)
        chosen = routing[:, :, :, :top, None] == names
        member = jnp.sum(chosen.astype(F32), axis=3)
        gates = jnp.sum(jnp.where(chosen, routing[:, :, :, top:, None], 0.0), axis=3)
        lower = (ordinal[:, None] > ordinal[None, :]).astype(BF)
        rank = jnp.einsum("ij,smje->smei", lower, member.astype(BF), preferred_element_type=F32)
        slot = jnp.where(member.transpose(0, 1, 3, 2) > 0.5, rank, -1.0).astype(jnp.int32)
        gate_high = gates.astype(BF)
        gate_low = (gates - gate_high.astype(F32)).astype(BF)
        gate_cols = jnp.concatenate([gate_high, gate_low], axis=3)
        gate_cols = jnp.pad(gate_cols, ((0, 0), (0, 0), (0, 0), (0, HD - 2 * experts)))
        return [(slot[:, b], gate_cols[:, b]) for b in range(2)]

    def to_host(own, *tokens):
        parts = jnp.stack([own] + [move(own, dp=k) for k in range(1, n_dp)])
        if tokens:
            parts = after(parts, *tokens)
        across = move(parts, tensor=2)
        near = [parts, move(parts, tensor=1), across, move(across, tensor=1)]
        parts, across = move(parts, section=1), move(across, section=1)
        return near, [parts, move(parts, tensor=1), across, move(across, tensor=1)]

    def core_sum(sums):
        return sums[0] + move(sums[1], tensor=1)

    def dp_terms(parts):
        return [(parts, 0)] + [(move(parts[k], dp=k), None) for k in range(1, n_dp)]

    def from_host(near, far, host, *tokens):
        here = sec == host
        across = move(jnp.where(here, near[1], move(far[1], section=1)), tensor=2)
        if tokens:
            here = here & there(*tokens)
        total = jnp.where(here, near[0], move(far[0], section=1)) + across
        return dp_terms(total), total

    x0 = jnp.where(first, block_input[0], block_input[1])
    seed = jnp.where(first & there(*routing[1:]), seed_near, seed_far)
    weights0 = (gather_weights(seed),)
    _, a, _ = finish(x0, gains0[0], [])

    routes = routes_of(routing)
    a_blocks = over_tensor(a)
    (keep, send, *saved, attended), _ = attn_fwd(
        a_blocks, weights0, [part for route in routes for part in route]
    )
    part0, part1 = sum_over_tensor(keep, send)
    mid, m, _ = finish(x0, gains0[1], [(part0, None), (part1, None)])
    kept0 = (x0, a_blocks, saved, attended, mid, weights0)
    cot_far = move(jnp.where(first, cotangent[0, 1], cotangent[0, 0]), section=1)
    cot_near = jnp.where(first, cotangent[0, 0], cotangent[0, 1])
    cots = jnp.stack([jnp.where(first, cot_near, cot_far), jnp.where(first, cot_far, cot_near)])
    near, far = to_host(m, cots)
    seed = jnp.where(first & there(near[0]), seed_far, seed_near)
    weights1 = (gather_weights(seed),)
    cot_all = after(cotangent[0].astype(BF), near[2])
    cot_all = lax.all_gather(cot_all[None], ("dp", "tensor"), axis=0, tiled=True)
    kept_near, sums_near, _ = moe_fwd(near, 0)
    kept_far, sums_far, _ = moe_fwd(far, 1, (sums_near[1],))
    terms, total = from_host(core_sum(sums_near), core_sum(sums_far), 0)
    out0, a, _ = finish(mid, gains1[0], terms)

    a_blocks = over_tensor(a)
    (keep, send, *saved, attended), _ = attn_fwd(a_blocks, weights1)
    part0, part1 = sum_over_tensor(keep, send)
    mid, m, _ = finish(out0, gains1[1], [(part0, None), (part1, None)])
    kept1 = (out0, a_blocks, saved, attended, mid, weights1)
    near, far = to_host(m)
    set_near, sums_near = moe_turn(near, cot_all, 1)
    set_far, sums_far = moe_turn(far, cot_all, 0, (sums_near[1],))
    sets = [None, (set_near, set_far)]
    terms, total = from_host(core_sum(sums_near), core_sum(sums_far), 1)
    out_near, out_far = (
        core_sum(moe_out(part[2], b, sums_far[0])) for b, part in ((1, set_near), (0, set_far))
    )
    out_far = move(after(out_far, total), section=1)

    cot_far = move(jnp.where(first, cotangent[0, 1], cotangent[0, 0]), section=1)
    cot_near = jnp.where(first, cotangent[0, 0], cotangent[0, 1])
    cots = (jnp.where(first, cot_near, cot_far), jnp.where(first, cot_far, cot_near))

    def attention_back(kept, l, g, terms, more, *tokens):
        x, a_blocks, saved, attended, mid, weights = kept
        (dmid, d, moe_gain_sum), _ = norm_back(mid, layer_gain[l][1], g, terms, tokens=tokens)
        d_blocks = over_tensor(d)
        (keep, send, dq, kv_keep, kv_send), _ = attn_bwd(d_blocks, saved, weights)
        args = (*a_blocks, dq, kv_keep, move(kv_send, tensor=1), *d_blocks, attended)
        mine, theirs = halves_grad(
            functools.partial(attn_wgrad_kernel, l == 0), "attn_wgrad", args, 2 * qcols + HD
        )
        part0, part1 = sum_over_tensor(keep, send)
        (*outs, attn_gain_sum), _ = norm_back(
            x, layer_gain[l][0], dmid, [(part0, None), (part1, None)], more
        )
        return outs, jnp.concatenate([attn_gain_sum, moe_gain_sum]), mine, theirs

    (in_grad1, g, g_low), gain_sums1, mine, theirs = attention_back(
        kept1, 1, cots[1], terms, (cots[0],), out_far
    )
    out1 = jnp.where(first, out_far, out_near)
    out_across = move(out1[1], tensor=2)
    theirs = move(theirs, section=1)
    near, far = to_host(g_low, out_across, theirs)
    out1 = lax.psum_scatter(out1[0] + out_across, "dp", scatter_dimension=0, tiled=True)
    out1 = mid + out1[0].astype(F32)
    shard1 = lax.psum_scatter(mine + theirs, "dp", scatter_dimension=0, tiled=True)
    shard1 = shard1[0].astype(F32)
    grads_near, sums_near, _ = moe_bwd(near, kept_near[1], 0)
    grads_far, sums_far, _ = moe_bwd(far, kept_far[1], 1, (sums_near[1],))
    sets[0] = ((kept_near[0], *grads_near), (kept_far[0], *grads_far))
    terms, _ = from_host(core_sum(sums_near), core_sum(sums_far), 0)
    (in_grad0, _), gain_sums0, mine, theirs = attention_back(kept0, 0, g, terms, ())

    gain_sums = jnp.concatenate([gain_sums0, gain_sums1])
    gain_sums = gain_sums + move(gain_sums, tensor=1)
    gain_sums = gain_sums + move(gain_sums, tensor=2)
    gain_sums = gain_sums.astype(BF).reshape(4, n_dp, drows).transpose(1, 0, 2)[dp_order]
    gain_sums = jnp.pad(gain_sums, ((0, 0), (0, 12), (0, 2 * qcols + HD - drows)))
    parts = jnp.concatenate([mine + move(theirs, section=1), gain_sums], axis=1)
    parts = [parts[0]] + [move(parts[k], dp=k) for k in range(1, n_dp)]
    dw_in, dw_out = moe_wgrad(sets, parts[1])
    shard0 = sum(part.astype(F32) for part in parts)
    shard0 = jnp.where(there(dw_in), shard0, 0.0)

    gain0, gain1 = shard0[half : half + 2], shard0[half + 2 : half + 4]
    own = jnp.where(first, shard0[:half], shard1)
    own_gain = jnp.where(first, gain0, gain1)[:, :drows]
    far = jnp.concatenate([
        jnp.where(first, shard1, shard0[:half]),
        jnp.pad(jnp.where(first, gain1, gain0), ((0, 14), (0, 0))),
    ])
    far = move(far.astype(BF), section=1).astype(F32)
    grad_shard = jnp.where(
        first, jnp.concatenate([own, far[:half]]), jnp.concatenate([far[:half], own])
    )
    gains = own_gain + far[half : half + 2, :drows]
    gains = lax.dynamic_slice_in_dim(gains, t * attn_gain.shape[1], attn_gain.shape[1], 1)
    cols = qcols + HD
    grad_out = grad_shard[:, cols:].T
    grad_kv = kv_turn(grad_shard[:, qcols:cols])
    def both_batches(value0, value1):
        far = move(jnp.where(first, value1, value0).astype(BF), section=1).astype(F32)
        near = jnp.where(first, value0, value1)
        return jnp.stack([jnp.where(first, near, far), jnp.where(first, far, near)])[None]

    return (
        both_batches(out0, out1),
        both_batches(in_grad0, in_grad1),
        gains[0:1],
        grad_shard[None, :, :qcols],
        grad_kv[None],
        grad_out[None],
        gains[1:2],
        dw_in[None],
        dw_out[None],
    )


def solution(mesh):
    return jax.shard_map(
        per_device,
        mesh=mesh,
        in_specs=(
            P(None, ("dp", "tensor"), None),
            P(None, "dp"),
            P("section", None, "dp", None),
            P("section", None, "dp", None),
            P("section", None, ("dp", "tensor"), None),
            P("section", ("dp", "tensor")),
            P("section", "dp", "tensor"),
            P("section", "dp", "tensor"),
            P("section", "tensor", "dp"),
            P("section", ("dp", "tensor")),
            P("section", "dp", None, "tensor"),
            P("section", "dp", "tensor", None),
        ),
        out_specs=(
            P("section", None, ("dp", "tensor"), None),
            P("section", None, ("dp", "tensor"), None),
            P("section", ("dp", "tensor")),
            P("section", "dp", "tensor"),
            P("section", "dp", "tensor"),
            P("section", "tensor", "dp"),
            P("section", ("dp", "tensor")),
            P("section", "dp", None, "tensor"),
            P("section", "dp", "tensor", None),
        ),
        check_vma=False,
    )
```

```python
import functools

import jax
import jax.numpy as jnp
from jax import lax
from jax.experimental import pallas as pl
from jax.experimental.pallas import tpu as pltpu
from jax.sharding import PartitionSpec as P

H = 12
KVH = 2
HD = 128
E = 16

EPS = 1e-06
THETA = 10000.0
BF = jnp.bfloat16
F32 = jnp.float32
MIB = 1024 * 1024
COST = 4
TOGETHER = 4
DEPTH = 4


def dot(a, b, ca, cb):
    return lax.dot_general(a, b, (((ca,), (cb,)), ((), ())), preferred_element_type=F32)


def move(value, section=0, dp=0, tensor=0):
    n_dp, n_t = lax.axis_size("dp"), lax.axis_size("tensor")
    pairs = []
    for s in range(2):
        for d in range(n_dp):
            for t in range(n_t):
                here = (s * n_dp + d) * n_t + t
                pairs.append((here, ((s ^ section) * n_dp + (d ^ dp)) * n_t + (t ^ tensor)))
    return lax.ppermute(value, ("section", "dp", "tensor"), pairs)


def kv_turn(value):
    return lax.ppermute(value, "tensor", [(0, 0), (1, 2), (2, 1), (3, 3)])


def over_tensor(value):
    across = move(value, tensor=2)
    return [value, move(value, tensor=1), across, move(across, tensor=1)]


def after(value, *tokens):
    ready = functools.reduce(jnp.logical_and, [token == token for token in tokens])
    return jnp.where(ready, value, jnp.zeros_like(value))


def there(*tokens):
    marks = [token[(0,) * token.ndim].astype(F32) for token in tokens]
    total = functools.reduce(jnp.add, marks)
    return total == total


def sum_over_tensor(keep, send):
    total = keep + move(send, tensor=1)
    return total[0], move(total[1], tensor=2)


def rope(value, cosine, sine):
    return value * cosine + pltpu.roll(value, HD // 2, 1) * sine


def allowed_pairs(me, rows, start):
    def places(axis):
        at = lax.broadcasted_iota(jnp.int32, (4 * rows, 4 * rows), axis)
        return (me[3] ^ (at // rows)) * rows + at % rows

    keys = places(1)
    return (keys <= places(0)) & (keys >= start.astype(jnp.int32))


def assemble(blocks, weights, sems):
    halves, n_dp, half = blocks.shape[:3]
    return start_all(*[
        pltpu.make_async_copy(
            blocks.at[part, k], weights.at[pl.ds((2 * k + part) * half, half)], sems.at[part, k]
        )
        for part in range(halves)
        for k in range(n_dp)
    ])


def whole_sequence(blocks, into):
    rows = blocks[0].shape[0]
    for r, ref in enumerate(blocks):
        into[r * rows : (r + 1) * rows, :] = ref[...]


def attn_fwd_kernel(heads, me, blocks, a0, a1, a2, a3, table, keep, send, saved, a_all, weights, sems):
    rows, qcols = a0.shape[0], heads * HD
    copies = assemble(blocks, weights, sems)
    whole_sequence((a0, a1, a2, a3), a_all)
    wait_all(copies)
    qkv = dot(a_all[...], weights[:, : qcols + 2 * HD], 1, 0)
    co, si = table[:, :HD], table[:, HD : 2 * HD]
    k = rope(qkv[:, qcols : qcols + HD], co, si).astype(BF)
    v = qkv[:, qcols + HD :].astype(BF)
    saved[:, qcols : qcols + HD] = k
    saved[:, qcols + HD : qcols + 2 * HD] = v
    allowed = allowed_pairs(me, rows, table[:, 2 * HD : 2 * HD + 1])
    for h in range(heads):
        qh = rope(qkv[:, h * HD : (h + 1) * HD], co, si).astype(BF)
        saved[:, h * HD : (h + 1) * HD] = qh
        p = softmax(qh, k, allowed).astype(BF)
        at = qcols + 2 * HD + h * HD
        saved[:, at : at + HD] = dot(p, v, 1, 0).astype(BF)
    part = dot(saved[:, qcols + 2 * HD :], weights[:, qcols + 2 * HD :], 1, 1).astype(BF)
    for r in range(4):
        (send if r % 2 else keep)[r // 2] = part[r * rows : (r + 1) * rows, :]


def softmax(qh, k, allowed):
    s = jnp.where(allowed, HD ** (-0.5) * dot(qh, k, 1, 1), -1e30)
    e = jnp.exp(s - jnp.max(s, axis=1, keepdims=True))
    return e * (1.0 / jnp.sum(e, axis=1, keepdims=True))


def attn_bwd_kernel(
    heads, me, blocks, d0, d1, d2, d3, saved, table,
    keep, send, dq_out, kv_send, d_all, weights, sems, dqkv,
):
    rows, qcols = d0.shape[0], heads * HD
    copies = assemble(blocks, weights, sems)
    whole_sequence((d0, d1, d2, d3), d_all)
    wait_all(copies)
    do = dot(d_all[...], weights[:, qcols + 2 * HD :], 1, 0).astype(BF)
    co, si = table[:, :HD], -table[:, HD : 2 * HD]
    k, v = saved[:, qcols : qcols + HD], saved[:, qcols + HD : qcols + 2 * HD]
    allowed = allowed_pairs(me, rows, table[:, 2 * HD : 2 * HD + 1])
    dk = jnp.zeros((do.shape[0], HD), F32)
    dv = jnp.zeros((do.shape[0], HD), F32)
    for h in range(heads):
        qh = saved[:, h * HD : (h + 1) * HD]
        doh = do[:, h * HD : (h + 1) * HD]
        p = softmax(qh, k, allowed)
        dv = dv + dot(p.astype(BF), doh, 0, 0)
        dp = dot(doh, v, 1, 1)
        ds = (p * (dp - jnp.sum(p * dp, axis=1, keepdims=True))).astype(BF)
        dq = HD ** (-0.5) * dot(ds, k, 1, 0)
        dk = dk + dot(ds, qh, 0, 0)
        dqkv[:, h * HD : (h + 1) * HD] = rope(dq, co, si).astype(BF)
    dk = rope(HD ** (-0.5) * dk, co, si).astype(BF)
    dv = dv.astype(BF)
    dqkv[:, qcols : qcols + HD] = dk
    dqkv[:, qcols + HD :] = dv
    core0 = me[2] == 0
    dq_out[:, :qcols] = dqkv[:, :qcols]
    dq_out[:, qcols:] = jnp.where(core0, dk, dv)
    kv_send[...] = jnp.where(core0, dv, dk)
    part = dot(dqkv[...], weights[:, : qcols + 2 * HD], 1, 1).astype(BF)
    for r in range(4):
        (send if r % 2 else keep)[r // 2] = part[r * rows : (r + 1) * rows, :]


def total_of(terms, places):
    total = None
    for ref, place in zip(terms, places):
        term = (ref[...] if place is None else ref[place]).astype(F32)
        total = term if total is None else total + term
    return total


def finish_kernel(places, base, gain, *refs):
    terms, (out, normed) = refs[: len(places)], refs[len(places) :]
    total = base[...]
    if places:
        total = total + total_of(terms, places)
    out[...] = total
    r = lax.rsqrt(jnp.mean(total * total, axis=1, keepdims=True) + EPS)
    normed[...] = (total * r * gain[...]).astype(BF)


def norm_back_kernel(places, rows_in, gain, upper, *refs):
    terms, rest = refs[: len(places)], refs[len(places) :]
    grad = total_of(terms, places)
    x = rows_in[...]
    r = lax.rsqrt(jnp.mean(x * x, axis=1, keepdims=True) + EPS)
    weighted = grad * gain[...]
    projected = jnp.mean(weighted * x, axis=1, keepdims=True)
    total = upper[...] + (r * weighted - x * (r * r * r) * projected)
    if len(rest) == 3:
        out, low, gain_sum = rest
        low[...] = total.astype(BF)
    else:
        more, out, following, low, gain_sum = rest
        after = more[...] + total
        following[...] = after
        low[...] = after.astype(BF)
    out[...] = total
    gain_sum[...] = jnp.sum(grad * x * r, axis=0, keepdims=True)


def split_rows(me, n_dp, grad, mine, theirs, flipped):
    half = grad.shape[0] // (2 * n_dp)
    for k in range(n_dp):
        start = (me[0] ^ k if flipped else k) * (2 * half)
        near = pl.multiple_of(start + me[1] * half, 16)
        far = pl.multiple_of(start + (1 - me[1]) * half, 16)
        mine[k] = grad[pl.ds(near, half), :]
        theirs[k] = grad[pl.ds(far, half), :]


def attn_wgrad_kernel(flipped, n_dp, me, a_all, d_all, saved, dq, kv_got, mine, theirs, grad):
    cols = dq.shape[1]
    qcols = cols - HD
    rows = a_all.shape[0] // 4
    got = [kv_got[r * rows : (r + 1) * rows, :] for r in (1, 0, 3, 2)]
    kv = (dq[:, qcols:].astype(F32) + jnp.concatenate(got, axis=0).astype(F32)).astype(BF)
    a = a_all[...]
    grad[:, :qcols] = dot(a, dq[:, :qcols], 0, 0).astype(BF)
    grad[:, qcols:cols] = dot(a, kv, 0, 0).astype(BF)
    grad[:, cols:] = dot(d_all[...], saved[:, qcols + 2 * HD :], 0, 0).astype(BF)
    split_rows(me, n_dp, grad, mine, theirs, flipped)


def slot_rows(pos_row, s, experts, cap):
    slot = lax.broadcasted_iota(jnp.int32, (cap, pos_row.shape[2]), 0)
    hits = [(slot == pos_row[s, e : e + 1, :]).astype(F32) for e in range(experts)]
    return jnp.concatenate(hits, axis=0).astype(BF)


def start_all(*copies):
    for copy in copies:
        copy.start()
    return list(copies)


def wait_all(copies):
    for copy in copies:
        copy.wait()


def slot_gates(hit, gate_cols, s, experts, cap):
    both = dot(hit, gate_cols[s], 1, 0)
    lane = lax.broadcasted_iota(jnp.int32, both.shape, 1)
    own = lax.broadcasted_iota(jnp.int32, both.shape, 0) // cap
    return jnp.sum(jnp.where((lane == own) | (lane == own + experts), both, 0.0), axis=1, keepdims=True)


def gathered(me, ref, batch, count):
    return [[(ref, ((me[0] ^ s) * 4 + (me[3] ^ r), batch)) for r in range(4)] for s in range(count)]


def sequences(refs, count):
    out = []
    for at in range(0, len(refs), 8):
        out.append([(refs[at + r], None) for r in range(4)])
        out += [[(refs[at + 4 + r], s) for r in range(4)] for s in range(count - 1)]
    return out


def dispatch(tasks, ring, sems, pos_row, gate_cols, gates, experts, cap, following=()):
    def fetch(i):
        copies = []
        for r, (ref, at) in enumerate(tasks[i][0]):
            rows = ref.shape[-2]
            target = ring.at[i % DEPTH, pl.ds(r * rows, rows)]
            source = ref if at is None else ref.at[at]
            copies.append(pltpu.make_async_copy(source, target, sems.at[i % DEPTH, r]))
        return start_all(*copies)

    coming = [fetch(i) for i in range(min(DEPTH, len(tasks)))]
    following = list(following)
    for i, (_, s, into) in enumerate(tasks):
        wait_all(coming[i])
        hit = slot_rows(pos_row, s, experts, cap)
        picked = dot(hit, ring[i % DEPTH], 1, 0).astype(BF)
        for e in range(experts):
            into[e, s * cap : (s + 1) * cap, :] = picked[e * cap : (e + 1) * cap, :]
        if gates is not None and i < pos_row.shape[0]:
            gate = slot_gates(hit, gate_cols, s, experts, cap)
            for e in range(experts):
                gates[e, s * cap : (s + 1) * cap, :] = gate[e * cap : (e + 1) * cap, :]
        if i + DEPTH < len(tasks):
            coming.append(fetch(i + DEPTH))
        for copy in following[:2]:
            copy.start()
        following = following[2:]
    start_all(*following)


def place(out, result, e, cap):
    out = out.astype(BF)
    for s in range(result.shape[0]):
        result[s, e * cap : (e + 1) * cap, :] = out[s * cap : (s + 1) * cap, :]


def combine(values, pos_row, keep, send, experts, cap, rows, order=None):
    for s in range(values.shape[0]):
        total = dot(slot_rows(pos_row, s, experts, cap), values[s], 0, 0).astype(BF)
        at = s if order is None else order[s]
        for r in range(4):
            (send if r % 2 else keep)[r // 2, at] = total[r * rows : (r + 1) * rows, :]


def silu_parts(gu):
    half = gu.shape[1] // 2
    gate, up = gu[:, :half], gu[:, half:]
    sg = 1.0 / (1.0 + jnp.exp(-gate))
    return gate, up, sg


def gate_up_grad(dz, gate, up, sg, out):
    half = gate.shape[1]
    out[:, :half] = (dz * up * sg * (1.0 + gate * (1.0 - sg))).astype(BF)
    out[:, half:] = (dz * gate * sg).astype(BF)


def take(refs, *counts):
    parts, at = [], 0
    for count in counts:
        parts.append(refs[at : at + count])
        at += count
    return parts


def expert_weights(w_in, w_out, wi, wo, sems):
    copies = [
        [
            pltpu.make_async_copy(w_in.at[e], wi.at[e], sems.at[2 * e]),
            pltpu.make_async_copy(w_out.at[e], wo.at[e], sems.at[2 * e + 1]),
        ]
        for e in range(w_in.shape[0])
    ]
    return copies, [copy for pair in copies for copy in pair]


def moe_fwd_kernel(experts, cap, rows, count, n_blocks, *refs):
    blocks, ins, outs, scratch = take(refs, n_blocks, 4, 3, 9)
    pos_row, gate_cols, w_in, w_out = ins
    gu_out, keep, send = outs
    ring, x_all, result, gates, gu_all, wi, wo, sems, ring_sems = scratch
    weights, coming = expert_weights(w_in, w_out, wi, wo, sems)
    tasks = [(places, s, x_all) for s, places in enumerate(sequences(blocks, count))]
    dispatch(tasks, ring, ring_sems, pos_row, gate_cols, gates, experts, cap, coming)
    for e in range(experts):
        wait_all(weights[e])
        gu = dot(x_all[e], wi[e], 1, 0)
        gu_all[e] = gu
        gate, up, sg = silu_parts(gu)
        z = (gate * sg * up * gates[e]).astype(BF)
        place(dot(z, wo[e], 1, 0), result, e, cap)
    done = start_all(pltpu.make_async_copy(gu_all, gu_out, sems.at[2 * experts]))
    combine(result, pos_row, keep, send, experts, cap, rows)
    wait_all(done)


def moe_bwd_kernel(experts, cap, rows, count, n_blocks, *refs):
    blocks, ins, outs, scratch = take(refs, n_blocks, 5, 4, 11)
    pos_row, gate_cols, gu_in, w_in, w_out = ins
    z_out, dgu_out, keep, send = outs
    ring, dr_all, result, gates, gu_all, z_all, dgu_all, wi, wo, sems, ring_sems = scratch
    weights, coming = expert_weights(w_in, w_out, wi, wo, sems)
    fetched = pltpu.make_async_copy(gu_in, gu_all, sems.at[2 * experts])
    tasks = [(places, s, dr_all) for s, places in enumerate(sequences(blocks, count))]
    dispatch(tasks, ring, ring_sems, pos_row, gate_cols, gates, experts, cap, [fetched] + coming)
    fetched.wait()
    for e in range(experts):
        wait_all(weights[e])
        gate, up, sg = silu_parts(gu_all[e])
        z_all[e] = (gate * sg * up * gates[e]).astype(BF)
        gate_up_grad(dot(dr_all[e], wo[e], 1, 1) * gates[e], gate, up, sg, dgu_all.at[e])
        place(dot(dgu_all[e], wi[e], 1, 1), result, e, cap)
    done = start_all(
        pltpu.make_async_copy(z_all, z_out, sems.at[2 * experts + 1]),
        pltpu.make_async_copy(dgu_all, dgu_out, sems.at[2 * experts + 2]),
    )
    combine(result, pos_row, keep, send, experts, cap, rows)
    wait_all(done)


def moe_turn_kernel(experts, cap, rows, count, n_blocks, batches, me, *refs):
    blocks, ins, outs, scratch = take(refs, n_blocks, 5, 4, 11)
    grads, pos_row, gate_cols, w_in, w_out = ins
    z_out, dgu_out, keep, send = outs
    ring, x_all, dr_all, result, gates, z_all, dgu_all, wi, wo, sems, ring_sems = scratch
    weights, coming = expert_weights(w_in, w_out, wi, wo, sems)
    grad_places = [places for batch in batches for places in gathered(me, grads, batch, count)]
    tasks = [(places, s, x_all) for s, places in enumerate(sequences(blocks, count))]
    tasks += [(places, s, dr_all) for s, places in enumerate(grad_places)]
    dispatch(tasks, ring, ring_sems, pos_row, gate_cols, gates, experts, cap, coming)
    for e in range(experts):
        wait_all(weights[e])
        gu = dot(x_all[e], wi[e], 1, 0)
        gate, up, sg = silu_parts(gu)
        z_all[e] = (gate * sg * up * gates[e]).astype(BF)
        gate_up_grad(dot(dr_all[e], wo[e], 1, 1) * gates[e], gate, up, sg, dgu_all.at[e])
        place(dot(dgu_all[e], wi[e], 1, 1), result, e, cap)
    done = start_all(
        pltpu.make_async_copy(z_all, z_out, sems.at[2 * experts]),
        pltpu.make_async_copy(dgu_all, dgu_out, sems.at[2 * experts + 1]),
    )
    combine(result, pos_row, keep, send, experts, cap, rows)
    wait_all(done)


def moe_out_kernel(experts, cap, rows, count, me, z, pos_row, w_out, keep, send, result):
    for e in range(experts):
        place(dot(z[e], w_out[e], 1, 0), result, e, cap)
    order = [s // count * count + (me[0] ^ (s % count)) for s in range(pos_row.shape[0])]
    combine(result, pos_row, keep, send, experts, cap, rows, order)


def moe_wgrad_kernel(experts, cap, count, n_blocks, *refs):
    me, refs = refs[0], refs[1:]
    x0, g0, x1, ins, hidden, outs, scratch = take(refs, n_blocks, n_blocks, n_blocks, 2, 4, 2, 9)
    cots, pos_row = ins
    dwin, dwout = outs
    ring, x_all, dr_all, dgu, z, din, dout, sems, ring_sems = scratch

    def tokens(x_places, g_places, dgu_in, z_in):
        fetched = start_all(
            pltpu.make_async_copy(dgu_in, dgu, sems.at[4]), pltpu.make_async_copy(z_in, z, sems.at[5])
        )
        tasks = [(places, s, x_all) for s, places in enumerate(x_places)]
        tasks += [(places, s, dr_all) for s, places in enumerate(g_places)]
        dispatch(tasks, ring, ring_sems, pos_row, None, None, experts, cap)
        wait_all(fetched)

    @pl.when(me[1] == 0)
    def _():
        tokens(sequences(x0, count), sequences(g0, count), hidden[0], hidden[1])

    @pl.when(me[1] == 1)
    def _():
        places = [part for batch in (1, 0) for part in gathered(me, cots, batch, count)]
        tokens(sequences(x1, count), places, hidden[2], hidden[3])

    leaving = [[], []]
    for e in range(experts):
        slot = e % 2
        wait_all(leaving[slot])
        din[slot] = dot(x_all[e], dgu[e], 0, 0)
        dout[slot] = dot(z[e], dr_all[e], 0, 0)
        leaving[slot] = start_all(
            pltpu.make_async_copy(din.at[slot], dwin.at[e], sems.at[slot]),
            pltpu.make_async_copy(dout.at[slot], dwout.at[e], sems.at[2 + slot]),
        )
    wait_all(leaving[0] + leaving[1])


def per_device(
    block_input, segments, expert_ids, gate_values, cotangent, attn_gain,
    query_weight, kv_weight, out_weight, moe_gain, w_in, w_out,
):
    sec = lax.axis_index("section")
    dp = lax.axis_index("dp")
    t = lax.axis_index("tensor")
    n_dp = lax.axis_size("dp")
    n_t = lax.axis_size("tensor")
    first = sec == 0
    core0 = t % 2 == 0
    me = jnp.stack([dp, sec, t % 2, t]).astype(jnp.int32)
    rows, width = block_input.shape[1], block_input.shape[2]
    seq = segments.shape[1]
    top = expert_ids.shape[3]
    heads = query_weight.shape[2] // HD
    qcols = heads * HD
    experts, ffn = w_in.shape[1], w_out.shape[2]
    cap = -(-(seq * top * 9 // (8 * E)) // 16) * 16
    sides = 2 if n_dp <= TOGETHER else 1
    total = 2 * n_dp
    slots = total * cap
    dp_order = jnp.arange(n_dp, dtype=jnp.int32) ^ dp
    t_order = jnp.arange(n_t, dtype=jnp.int32) ^ t
    drows = width // n_dp
    half = drows // 2

    pair = jax.ShapeDtypeStruct((2, rows, width), BF)
    smem = pl.BlockSpec(memory_space=pltpu.SMEM)
    vmem = pl.BlockSpec(memory_space=pltpu.VMEM)
    any_space = pl.BlockSpec(memory_space=pl.ANY)
    hbm = pl.BlockSpec(memory_space=pltpu.HBM)
    seq_scratch = pltpu.VMEM((seq, width), BF)

    def me_after(*tokens):
        return jnp.where(there(*tokens), me, 0) if tokens else me

    def shape(*dims, dtype=BF):
        return jax.ShapeDtypeStruct(dims, dtype)

    def call(
        kernel, name, ins, outs, scratch, limit, cost, in_specs=None, out_specs=None, hold=(), tokens=()
    ):
        n_ins, n_outs, n_hold, n_tok = len(ins), len(outs), len(hold), len(tokens)

        def body(*refs):
            given, results, rest = take(refs, n_ins + n_tok + n_hold, n_outs + n_hold, len(scratch))
            kernel(*given[:n_ins], *results[:n_outs], *rest)

        out = pl.pallas_call(
            body,
            out_shape=list(outs) + [jax.ShapeDtypeStruct(h.shape, h.dtype) for h in hold],
            in_specs=(in_specs or [smem] + [vmem] * (n_ins - 1)) + [any_space] * (n_tok + n_hold),
            out_specs=(out_specs or [vmem] * n_outs) + [any_space] * n_hold,
            scratch_shapes=scratch,
            input_output_aliases={n_ins + n_tok + i: n_outs + i for i in range(n_hold)},
            compiler_params=pltpu.CompilerParams(vmem_limit_bytes=limit * MIB),
            cost_estimate=pl.CostEstimate(flops=cost * 10**9, bytes_accessed=cost * 3 * MIB, transcendentals=0),
            name=name,
        )(*ins, *tokens, *hold)
        return out[:n_outs], out[n_outs:]

    acols = 2 * qcols + 2 * HD
    weights_scratch = pltpu.VMEM((width, acols), BF)
    weights_sems = pltpu.SemaphoreType.DMA((2, n_dp))

    def attn_fwd(a_blocks, weights, tokens=()):
        return call(
            functools.partial(attn_fwd_kernel, heads), "attn_fwd",
            (me, weights, *a_blocks, table),
            [pair, pair, shape(seq, acols), shape(seq, width)],
            [weights_scratch, weights_sems], 20, 0, [smem, hbm] + [vmem] * 5, tokens=tokens,
        )[0]

    def attn_bwd(d_blocks, saved, weights):
        return call(
            functools.partial(attn_bwd_kernel, heads), "attn_bwd",
            (me, weights, *d_blocks, saved, table),
            [pair, pair, shape(seq, qcols + HD), shape(seq, HD), shape(seq, width)],
            [weights_scratch, weights_sems, pltpu.VMEM((seq, qcols + 2 * HD), BF)], 20, 0,
            [smem, hbm] + [vmem] * 6,
        )[0]

    tok_f32, tok_bf = shape(rows, width, dtype=F32), shape(rows, width)

    def finish(base, gain, terms, hold=()):
        (out, normed), held = call(
            functools.partial(finish_kernel, [at for _, at in terms]), "finish",
            (base, gain, *[value for value, _ in terms]), [tok_f32, tok_bf], [], 8, 0,
            [vmem] * (2 + len(terms)), hold=hold,
        )
        return out, normed, held

    def norm_back(x, gain, upper, terms, more=(), tokens=()):
        return call(
            functools.partial(norm_back_kernel, [at for _, at in terms]), "norm_back",
            (x, gain, upper, *[value for value, _ in terms], *more),
            [tok_f32] * (1 + len(more)) + [tok_bf, shape(1, width, dtype=F32)], [], 8, 0,
            [vmem] * (3 + len(terms) + len(more)), tokens=tokens,
        )

    def halves_grad(kernel, name, ins, cols):
        return call(
            functools.partial(kernel, n_dp), name, (me, *ins), [shape(n_dp, half, cols)] * 2,
            [pltpu.VMEM((width, cols), BF)], 20, 1,
        )[0]

    count = sides * n_dp
    part_slots = count * cap
    weight_scratch = [pltpu.VMEM((experts, width, 2 * ffn), BF), pltpu.VMEM((experts, ffn, width), BF)]
    ring_scratch = pltpu.VMEM((DEPTH, seq, width), BF)
    slot_scratch = pltpu.VMEM((experts, part_slots, width), BF)
    result_scratch = pltpu.VMEM((count, experts * cap, width), BF)
    z_scratch = pltpu.VMEM((experts, part_slots, ffn), BF)
    dgu_scratch = pltpu.VMEM((experts, part_slots, 2 * ffn), BF)
    gu_scratch = pltpu.VMEM((experts, part_slots, 2 * ffn), F32)
    gate_scratch = pltpu.VMEM((experts, part_slots, 1), F32)
    copy_sems = pltpu.SemaphoreType.DMA((2 * experts + 3,))
    ring_sems = pltpu.SemaphoreType.DMA((DEPTH, 4))
    gu_shape = shape(experts, part_slots, 2 * ffn, dtype=F32)
    z_shape = shape(experts, part_slots, ffn)
    dgu_shape = shape(experts, part_slots, 2 * ffn)
    sum_shapes = [shape(2, count, rows, width)] * 2
    expert_args = (w_in[0], w_out[0])

    def by_sides(run, arrays, axes):
        if sides == 2:
            return run(arrays, (0, 1))
        size = [value.shape[axis] // 2 for value, axis in zip(arrays, axes)]
        outs = []
        for side in range(2):
            parts = [
                lax.slice_in_dim(value, side * n, (side + 1) * n, axis=axis)
                for value, n, axis in zip(arrays, size, axes)
            ]
            outs.append(run(parts, (side,)))
        return [jnp.concatenate(both, axis=1) for both in zip(*outs)]

    def of_sides(blocks, which):
        return [part for side in which for part in blocks[side]]

    def moe_fwd(blocks, route):
        def run(arrays, which):
            parts = of_sides(blocks, which)
            return call(
                functools.partial(moe_fwd_kernel, experts, cap, rows, n_dp, len(parts)), "moe_fwd",
                (*parts, *arrays, *expert_args), [gu_shape] + sum_shapes,
                [
                    ring_scratch, slot_scratch, result_scratch, gate_scratch, gu_scratch, *weight_scratch, copy_sems, ring_sems,
                ],
                48, COST, [any_space] * len(parts) + [vmem] * 2 + [hbm] * 2, [hbm] + [vmem] * 2,
            )[0]

        gu, keep, send = by_sides(run, route, (0, 0))
        return gu, (keep, send)

    def moe_bwd(blocks, gu, route):
        def run(arrays, which):
            parts = of_sides(blocks, which)
            return call(
                functools.partial(moe_bwd_kernel, experts, cap, rows, n_dp, len(parts)), "moe_bwd",
                (*parts, *arrays, *expert_args), [z_shape, dgu_shape] + sum_shapes,
                [
                    ring_scratch, slot_scratch, result_scratch, gate_scratch, gu_scratch, z_scratch,
                    dgu_scratch,
                    *weight_scratch, copy_sems, ring_sems,
                ],
                50, COST, [any_space] * len(parts) + [vmem] * 2 + [hbm] * 3, [hbm] * 2 + [vmem] * 2,
            )[0]

        z, dgu, keep, send = by_sides(run, (*route, gu), (0, 0, 1))
        return (dgu, z), (keep, send)

    def moe_turn(blocks, grads, route):
        def run(arrays, which):
            parts = of_sides(blocks, which)
            batches = [1 - side for side in which]
            return call(
                functools.partial(
                    moe_turn_kernel, experts, cap, rows, n_dp, len(parts), batches
                ),
                "moe_turn", (me, *parts, grads, *arrays, *expert_args),
                [z_shape, dgu_shape] + sum_shapes,
                [
                    ring_scratch, slot_scratch, slot_scratch, result_scratch, gate_scratch, z_scratch,
                    dgu_scratch,
                    *weight_scratch, copy_sems, ring_sems,
                ],
                57, COST * 2, [smem] + [any_space] * (len(parts) + 1) + [vmem] * 2 + [hbm] * 2,
                [hbm] * 2 + [vmem] * 2,
            )[0]

        z, dgu, keep, send = by_sides(run, route, (0, 0))
        return (dgu, z), (keep, send)

    def moe_out(z, route, *tokens):
        def run(arrays, which):
            return call(
                functools.partial(moe_out_kernel, experts, cap, rows, n_dp), "moe_out",
                (me_after(*tokens), *arrays, w_out[0]), sum_shapes, [result_scratch], 32, COST,
            )[0]

        return by_sides(run, (z, route[0]), (1, 0))

    def moe_wgrad(blocks0, grads0, blocks1, hidden, route, *tokens):
        arrays = [of_sides(blocks, (0, 1)) for blocks in (blocks0, grads0, blocks1)]
        return call(
            functools.partial(moe_wgrad_kernel, experts, cap, n_dp, len(arrays[0])), "moe_wgrad",
            (me_after(*tokens), *arrays[0], *arrays[1], *arrays[2], cot_all, route, *hidden),
            [shape(experts, width, 2 * ffn, dtype=F32), shape(experts, ffn, width, dtype=F32)],
            [
                ring_scratch, pltpu.VMEM((experts, slots, width), BF), pltpu.VMEM((experts, slots, width), BF),
                pltpu.VMEM((experts, slots, 2 * ffn), BF), pltpu.VMEM((experts, slots, ffn), BF),
                pltpu.VMEM((2, width, 2 * ffn), F32), pltpu.VMEM((2, ffn, width), F32),
                pltpu.SemaphoreType.DMA((6,)), ring_sems,
            ],
            48, 10, [smem] + [hbm] * (3 * len(arrays[0]) + 1) + [vmem] + [hbm] * 4, [hbm] * 2,
        )[0]

    gains = jnp.concatenate([attn_gain, moe_gain], axis=0)
    gains = jnp.stack(over_tensor(gains))[t_order].transpose(1, 0, 2).reshape(2, drows)
    gains = jnp.stack([gains] + [move(gains, dp=k) for k in range(1, n_dp)])[dp_order]
    gains = gains.transpose(1, 0, 2).reshape(2, 1, width)
    gains_far = move(gains, section=1)
    layer_gain = [jnp.where(sec == l, gains, gains_far).astype(F32) for l in range(2)]
    (gains0, gains1) = layer_gain

    def seeds_of(matrix):
        low, high = matrix[:half], matrix[half:]
        return jnp.where(first, low, high), move(jnp.where(first, high, low), section=1)

    def gather_weights(seed):
        return lax.all_gather(seed[None, None], ("section", "dp"), axis=0, tiled=True).reshape(
            2, n_dp, half, acols
        )

    kv_own = kv_turn(kv_weight[0])
    kv_core = move(kv_own, tensor=1)
    key_value = jnp.where(
        core0, jnp.concatenate([kv_own, kv_core], axis=1), jnp.concatenate([kv_core, kv_own], axis=1)
    )
    routing = jnp.concatenate([expert_ids[0].astype(F32), gate_values[0]], axis=2)
    routing = [routing] + [move(routing, dp=k) for k in range(1, n_dp)]
    seed_near, seed_far = seeds_of(
        jnp.concatenate([query_weight[0], key_value, out_weight[0].T], axis=1)
    )

    segment = jnp.where(first, segments[0], segments[1])
    ordinal = jnp.arange(seq, dtype=jnp.int32)
    start = jnp.sum((segment[None, :] < segment[:, None]).astype(jnp.int32), axis=1)
    places = (ordinal - start).astype(F32)

    def turned(vector):
        return vector.reshape(n_t, rows)[t_order].reshape(seq)

    start_col = turned(start)[:, None]
    frequency = THETA ** (-2.0 * jnp.arange(HD // 2, dtype=F32) / HD)
    angles = turned(places)[:, None] * frequency[None, :]
    cosine = jnp.cos(angles)
    cosine = jnp.concatenate([cosine, cosine], axis=1)
    sine = jnp.sin(angles)
    sine = jnp.concatenate([-sine, sine], axis=1)
    table = jnp.concatenate([cosine, sine, jnp.pad(start_col.astype(F32), ((0, 0), (0, HD - 1)))], axis=1)

    def routes_of(routing):
        routing = jnp.stack(routing)
        routing = routing.reshape(n_dp, 2, n_t, rows, 2 * top)[:, :, t_order]
        routing = routing.reshape(n_dp, 2, seq, 2 * top)
        names = (dp * experts + jnp.arange(experts, dtype=jnp.int32)).astype(F32)
        chosen = routing[:, :, :, :top, None] == names
        member = jnp.sum(chosen.astype(F32), axis=3)
        gates = jnp.sum(jnp.where(chosen, routing[:, :, :, top:, None], 0.0), axis=3)
        lower = (ordinal[:, None] > ordinal[None, :]).astype(BF)
        rank = jnp.einsum("ij,smje->smei", lower, member.astype(BF), preferred_element_type=F32)
        slot = jnp.where(member.transpose(0, 1, 3, 2) > 0.5, rank, -1.0).astype(jnp.int32)
        gate_high = gates.astype(BF)
        gate_low = (gates - gate_high.astype(F32)).astype(BF)
        gate_cols = jnp.concatenate([gate_high, gate_low], axis=3)
        gate_cols = jnp.pad(gate_cols, ((0, 0), (0, 0), (0, 0), (0, HD - 2 * experts)))
        return [
            tuple(jnp.concatenate([part[:, b], part[:, 1 - b]]) for part in (slot, gate_cols))
            for b in range(2)
        ]

    def spread(value):
        near, far = [value, move(value, tensor=2)], [move(value, section=1), move(value, section=1, tensor=2)]
        return [[part[0], move(part[0], tensor=1), part[1], move(part[1], tensor=1)] for part in (near, far)]

    def to_host(own, *tokens):
        near_own, far_own = spread(own)
        others = jnp.stack([move(own, dp=k) for k in range(1, n_dp)])
        near, far = spread(after(others, near_own[2], far_own[0], far_own[2], *tokens))
        return near_own + near, far_own + far

    def core_sums(keep, send, *tokens):
        got = move(send, tensor=1)
        sums = [
            [keep[y, at : at + n_dp] + got[y, at : at + n_dp] for y in range(2)] for at in (0, n_dp)
        ]
        if tokens:
            sums[1][1] = after(sums[1][1], *tokens)
        return sums

    def gather_sums(near, far, host, *tokens):
        near = near[0] + move(near[1], tensor=2)
        far = move(far[0], section=1) + move(far[1], section=1, tensor=2)
        total = jnp.where(sec == host, near, far)
        return after(total, *tokens) if tokens else total

    def parts_of(near, far, which):
        return [[part[which] for part in side] for side in (near, far)]

    def others_sums(near, far, host, *tokens):
        return gather_sums(*parts_of(near, far, slice(1, None)), host, *tokens)

    def all_sums(near, far, others, host, *tokens):
        total = gather_sums(*parts_of(near, far, 0), host).astype(F32)
        for k in range(1, n_dp):
            total = total + move(others[k - 1], dp=k).astype(F32)
        return [(after(total, *tokens) if tokens else total, None)]

    def from_host(near, far, host):
        return all_sums(near, far, others_sums(near, far, host), host)

    x0 = jnp.where(first, block_input[0], block_input[1])
    seed = jnp.where(first & there(*routing[1:]), seed_near, seed_far)
    weights0 = gather_weights(seed)
    _, a, _ = finish(x0, gains0[0], [])

    routes = routes_of(routing)
    a_blocks = over_tensor(a)
    keep, send, saved, a_all = attn_fwd(
        a_blocks, weights0, routes[0]
    )
    part0, part1 = sum_over_tensor(keep, send)
    mid, m, _ = finish(x0, gains0[1], [(part0, None), (part1, None)])
    kept0 = (x0, a_all, saved, mid, weights0)
    cot_far = move(jnp.where(first, cotangent[0, 1], cotangent[0, 0]), section=1)
    cot_near = jnp.where(first, cotangent[0, 0], cotangent[0, 1])
    cots = jnp.stack([jnp.where(first, cot_near, cot_far), jnp.where(first, cot_far, cot_near)])
    near, far = to_host(m, cots[0])
    there_now = [part.reshape(-1, width)[:half, :acols] for part in (near[6], far[4], far[6])]
    weights1 = gather_weights(after(jnp.where(first, seed_far, seed_near), *there_now))
    cot_all = after(cotangent[0].astype(BF), *[part[:1] for part in (near[6], far[4], far[6])])
    cot_all = lax.all_gather(cot_all[None], ("dp", "tensor"), axis=0, tiled=True)
    blocks0 = (near, far)
    gu0, sums = moe_fwd(blocks0, routes[0])
    terms = from_host(*core_sums(*sums), 0)
    out0, a, _ = finish(mid, gains1[0], terms)

    a_blocks = over_tensor(a)
    keep, send, saved, a_all = attn_fwd(a_blocks, weights1)
    part0, part1 = sum_over_tensor(keep, send)
    mid, m, _ = finish(out0, gains1[1], [(part0, None), (part1, None)])
    kept1 = (out0, a_all, saved, mid, weights1)
    near, far = to_host(m)
    blocks1 = (near, far)
    hidden1, sums = moe_turn(blocks1, cot_all, routes[1])
    terms = from_host(*core_sums(*sums), 1)

    cot_far = move(jnp.where(first, cotangent[0, 1], cotangent[0, 0]), section=1)
    cot_near = jnp.where(first, cotangent[0, 0], cotangent[0, 1])
    cots = (jnp.where(first, cot_near, cot_far), jnp.where(first, cot_far, cot_near))

    def attention_back(kept, l, g, terms, more, beside=None):
        x, a_all, saved, mid, weights = kept
        (dmid, d, moe_gain_sum), _ = norm_back(mid, layer_gain[l][1], g, terms)
        d_blocks = over_tensor(d)
        extra = core_sums(*beside(d)) if beside is not None else None
        if extra is not None:
            d_blocks[3] = after(d_blocks[3], extra[1][0][0])
        keep, send, dq, kv_send, d_all = attn_bwd(d_blocks, saved, weights)
        args = (a_all, d_all, saved, dq, move(kv_send, tensor=1))
        mine, theirs = halves_grad(
            functools.partial(attn_wgrad_kernel, l == 0), "attn_wgrad", args, 2 * qcols + HD
        )
        part0, part1 = sum_over_tensor(keep, send)
        (*outs, attn_gain_sum), _ = norm_back(
            x, layer_gain[l][0], dmid, [(part0, None), (part1, None)], more
        )
        return outs, jnp.concatenate([attn_gain_sum, moe_gain_sum]), mine, theirs, extra

    (in_grad1, g, g_low), gain_sums1, mine, theirs, outs = attention_back(
        kept1, 1, cots[1], terms, (cots[0],), lambda d: moe_out(hidden1[1], routes[1], d)
    )
    out_near, out_far = (jnp.stack(side) for side in outs)
    out_far = move(out_far, section=1)
    grad1 = jnp.where(first, jnp.stack([mine, theirs]), jnp.stack([theirs, mine]))
    near, far = to_host(g_low, grad1[0, 0, :1, :1], out_far[0, :1])
    shard1_sum = lax.psum_scatter(
        grad1.reshape(2 * n_dp, half, acols - HD), ("section", "dp"), scatter_dimension=0, tiled=True
    )
    grads0 = (near, far)
    hidden0, sums = moe_bwd(grads0, gu0, routes[0])
    near_far = core_sums(*sums, shard1_sum[0, :1, :1])
    route = jnp.where(first, routes[0][0], routes[1][0])
    dw_in, dw_out = moe_wgrad(
        blocks0, grads0, blocks1, (*hidden0, *hidden1), route, near_far[1][1]
    )
    others = others_sums(*near_far, 0, dw_out[0, :rows])
    out1 = after(jnp.where(first, out_far, out_near), others[:1])
    out_across = move(out1[1], tensor=2)
    terms = all_sums(*near_far, others, 0, out_across[0])
    out1_sum = lax.psum_scatter(out1[0] + out_across, "dp", scatter_dimension=0, tiled=True)
    (in_grad0, _), gain_sums0, mine, theirs, _ = attention_back(kept0, 0, g, terms, ())

    gain_sums = jnp.concatenate([gain_sums0, gain_sums1])
    gain_sums = gain_sums + move(gain_sums, tensor=1)
    gain_sums = gain_sums + move(gain_sums, tensor=2)
    gain_sums = gain_sums.astype(BF).reshape(4, n_dp, drows).transpose(1, 0, 2)[dp_order]
    gain_sums = jnp.pad(gain_sums, ((0, 0), (0, 12), (0, 2 * qcols + HD - drows)))
    parts = jnp.concatenate([mine + move(theirs, section=1), gain_sums], axis=1)
    parts = [parts[0]] + [move(parts[k], dp=k) for k in range(1, n_dp)]
    out1 = mid + out1_sum[0].astype(F32)
    shard1 = shard1_sum[0].astype(F32)
    shard0 = sum(part.astype(F32) for part in parts)

    gain0, gain1 = shard0[half : half + 2], shard0[half + 2 : half + 4]
    own = jnp.where(first, shard0[:half], shard1)
    own_gain = jnp.where(first, gain0, gain1)[:, :drows]
    far = jnp.concatenate([
        jnp.where(first, shard1, shard0[:half]),
        jnp.pad(jnp.where(first, gain1, gain0), ((0, 14), (0, 0))),
    ])
    far = move(far.astype(BF), section=1).astype(F32)
    grad_shard = jnp.where(
        first, jnp.concatenate([own, far[:half]]), jnp.concatenate([far[:half], own])
    )
    gains = own_gain + far[half : half + 2, :drows]
    gains = lax.dynamic_slice_in_dim(gains, t * attn_gain.shape[1], attn_gain.shape[1], 1)
    cols = qcols + HD
    grad_out = grad_shard[:, cols:].T
    grad_kv = kv_turn(grad_shard[:, qcols:cols])
    def mine_and_theirs(value0, value1):
        return jnp.where(first, value0, value1), jnp.where(first, value1, value0)

    out_near, out_far = mine_and_theirs(out0, out1)
    grad_near, grad_far = mine_and_theirs(in_grad0, in_grad1)
    theirs = move(jnp.stack([out_far, grad_far]).astype(BF), section=1).astype(F32)

    def both_batches(near, far):
        return jnp.where(first, jnp.stack([near, far]), jnp.stack([far, near]))[None]

    return (
        both_batches(out_near, theirs[0]),
        both_batches(grad_near, theirs[1]),
        gains[0:1],
        grad_shard[None, :, :qcols],
        grad_kv[None],
        grad_out[None],
        gains[1:2],
        dw_in[None],
        dw_out[None],
    )


def solution(mesh):
    return jax.shard_map(
        per_device,
        mesh=mesh,
        in_specs=(
            P(None, ("dp", "tensor"), None),
            P(None, "dp"),
            P("section", None, "dp", None),
            P("section", None, "dp", None),
            P("section", None, ("dp", "tensor"), None),
            P("section", ("dp", "tensor")),
            P("section", "dp", "tensor"),
            P("section", "dp", "tensor"),
            P("section", "tensor", "dp"),
            P("section", ("dp", "tensor")),
            P("section", "dp", None, "tensor"),
            P("section", "dp", "tensor", None),
        ),
        out_specs=(
            P("section", None, ("dp", "tensor"), None),
            P("section", None, ("dp", "tensor"), None),
            P("section", ("dp", "tensor")),
            P("section", "dp", "tensor"),
            P("section", "dp", "tensor"),
            P("section", "tensor", "dp"),
            P("section", ("dp", "tensor")),
            P("section", "dp", None, "tensor"),
            P("section", "dp", "tensor", None),
        ),
        check_vma=False,
    )
```

```python
import functools

import jax
import jax.numpy as jnp
from jax import lax
from jax.experimental import pallas as pl
from jax.experimental.pallas import tpu as pltpu
from jax.sharding import PartitionSpec as P

H = 12
KVH = 2
HD = 128
E = 16

EPS = 1e-06
THETA = 10000.0
BF = jnp.bfloat16
F32 = jnp.float32
MIB = 1024 * 1024
COST = 4
TOGETHER = 4
DEPTH = 4


def dot(a, b, ca, cb):
    return lax.dot_general(a, b, (((ca,), (cb,)), ((), ())), preferred_element_type=F32)


def move(value, section=0, dp=0, tensor=0):
    n_dp, n_t = lax.axis_size("dp"), lax.axis_size("tensor")
    pairs = []
    for s in range(2):
        for d in range(n_dp):
            for t in range(n_t):
                here = (s * n_dp + d) * n_t + t
                pairs.append((here, ((s ^ section) * n_dp + (d ^ dp)) * n_t + (t ^ tensor)))
    return lax.ppermute(value, ("section", "dp", "tensor"), pairs)


def kv_turn(value):
    return lax.ppermute(value, "tensor", [(0, 0), (1, 2), (2, 1), (3, 3)])


def over_tensor(value):
    across = move(value, tensor=2)
    return [value, move(value, tensor=1), across, move(across, tensor=1)]


def after(value, *tokens):
    ready = functools.reduce(jnp.logical_and, [token == token for token in tokens])
    return jnp.where(ready, value, jnp.zeros_like(value))


def there(*tokens):
    marks = [token[(0,) * token.ndim].astype(F32) for token in tokens]
    total = functools.reduce(jnp.add, marks)
    return total == total


def sum_over_tensor(keep, send):
    total = keep + move(send, tensor=1)
    return total[0], move(total[1], tensor=2)


def rope(value, cosine, sine):
    return value * cosine + pltpu.roll(value, HD // 2, 1) * sine


def allowed_pairs(me, rows, start):
    def places(axis):
        at = lax.broadcasted_iota(jnp.int32, (4 * rows, 4 * rows), axis)
        return (me[3] ^ (at // rows)) * rows + at % rows

    keys = places(1)
    return (keys <= places(0)) & (keys >= start.astype(jnp.int32))


def assemble(blocks, weights, sems):
    halves, n_dp, half = blocks.shape[:3]
    return start_all(*[
        pltpu.make_async_copy(
            blocks.at[part, k], weights.at[pl.ds((2 * k + part) * half, half)], sems.at[part, k]
        )
        for part in range(halves)
        for k in range(n_dp)
    ])


def whole_sequence(blocks, into):
    rows = blocks[0].shape[0]
    for r, ref in enumerate(blocks):
        into[r * rows : (r + 1) * rows, :] = ref[...]


def attn_fwd_kernel(heads, me, blocks, a0, a1, a2, a3, table, keep, send, saved, a_all, weights, sems):
    rows, qcols = a0.shape[0], heads * HD
    copies = assemble(blocks, weights, sems)
    whole_sequence((a0, a1, a2, a3), a_all)
    wait_all(copies)
    qkv = dot(a_all[...], weights[:, : qcols + 2 * HD], 1, 0)
    co, si = table[:, :HD], table[:, HD : 2 * HD]
    k = rope(qkv[:, qcols : qcols + HD], co, si).astype(BF)
    v = qkv[:, qcols + HD :].astype(BF)
    saved[:, qcols : qcols + HD] = k
    saved[:, qcols + HD : qcols + 2 * HD] = v
    allowed = allowed_pairs(me, rows, table[:, 2 * HD : 2 * HD + 1])
    for h in range(heads):
        qh = rope(qkv[:, h * HD : (h + 1) * HD], co, si).astype(BF)
        saved[:, h * HD : (h + 1) * HD] = qh
        p = softmax(qh, k, allowed).astype(BF)
        at = qcols + 2 * HD + h * HD
        saved[:, at : at + HD] = dot(p, v, 1, 0).astype(BF)
    part = dot(saved[:, qcols + 2 * HD :], weights[:, qcols + 2 * HD :], 1, 1).astype(BF)
    for r in range(4):
        (send if r % 2 else keep)[r // 2] = part[r * rows : (r + 1) * rows, :]


def softmax(qh, k, allowed):
    s = jnp.where(allowed, HD ** (-0.5) * dot(qh, k, 1, 1), -1e30)
    e = jnp.exp(s - jnp.max(s, axis=1, keepdims=True))
    return e * (1.0 / jnp.sum(e, axis=1, keepdims=True))


def attn_bwd_kernel(
    heads, me, blocks, d0, d1, d2, d3, saved, table,
    keep, send, dq_out, kv_send, d_all, weights, sems, dqkv,
):
    rows, qcols = d0.shape[0], heads * HD
    copies = assemble(blocks, weights, sems)
    whole_sequence((d0, d1, d2, d3), d_all)
    wait_all(copies)
    do = dot(d_all[...], weights[:, qcols + 2 * HD :], 1, 0).astype(BF)
    co, si = table[:, :HD], -table[:, HD : 2 * HD]
    k, v = saved[:, qcols : qcols + HD], saved[:, qcols + HD : qcols + 2 * HD]
    allowed = allowed_pairs(me, rows, table[:, 2 * HD : 2 * HD + 1])
    dk = jnp.zeros((do.shape[0], HD), F32)
    dv = jnp.zeros((do.shape[0], HD), F32)
    for h in range(heads):
        qh = saved[:, h * HD : (h + 1) * HD]
        doh = do[:, h * HD : (h + 1) * HD]
        p = softmax(qh, k, allowed)
        dv = dv + dot(p.astype(BF), doh, 0, 0)
        dp = dot(doh, v, 1, 1)
        ds = (p * (dp - jnp.sum(p * dp, axis=1, keepdims=True))).astype(BF)
        dq = HD ** (-0.5) * dot(ds, k, 1, 0)
        dk = dk + dot(ds, qh, 0, 0)
        dqkv[:, h * HD : (h + 1) * HD] = rope(dq, co, si).astype(BF)
    dk = rope(HD ** (-0.5) * dk, co, si).astype(BF)
    dv = dv.astype(BF)
    dqkv[:, qcols : qcols + HD] = dk
    dqkv[:, qcols + HD :] = dv
    core0 = me[2] == 0
    dq_out[:, :qcols] = dqkv[:, :qcols]
    dq_out[:, qcols:] = jnp.where(core0, dk, dv)
    kv_send[...] = jnp.where(core0, dv, dk)
    part = dot(dqkv[...], weights[:, : qcols + 2 * HD], 1, 1).astype(BF)
    for r in range(4):
        (send if r % 2 else keep)[r // 2] = part[r * rows : (r + 1) * rows, :]


def total_of(terms, places):
    total = None
    for ref, place in zip(terms, places):
        term = (ref[...] if place is None else ref[place]).astype(F32)
        total = term if total is None else total + term
    return total


def finish_kernel(places, base, gain, *refs):
    terms, (out, normed) = refs[: len(places)], refs[len(places) :]
    total = base[...]
    if places:
        total = total + total_of(terms, places)
    out[...] = total
    r = lax.rsqrt(jnp.mean(total * total, axis=1, keepdims=True) + EPS)
    normed[...] = (total * r * gain[...]).astype(BF)


def norm_back_kernel(places, rows_in, gain, upper, *refs):
    terms, rest = refs[: len(places)], refs[len(places) :]
    grad = total_of(terms, places)
    x = rows_in[...]
    r = lax.rsqrt(jnp.mean(x * x, axis=1, keepdims=True) + EPS)
    weighted = grad * gain[...]
    projected = jnp.mean(weighted * x, axis=1, keepdims=True)
    total = upper[...] + (r * weighted - x * (r * r * r) * projected)
    if len(rest) == 3:
        out, low, gain_sum = rest
        low[...] = total.astype(BF)
    else:
        more, out, following, low, gain_sum = rest
        after = more[...] + total
        following[...] = after
        low[...] = after.astype(BF)
    out[...] = total
    gain_sum[...] = jnp.sum(grad * x * r, axis=0, keepdims=True)


def split_rows(me, n_dp, grad, mine, theirs, flipped):
    half = grad.shape[0] // (2 * n_dp)
    for k in range(n_dp):
        start = (me[0] ^ k if flipped else k) * (2 * half)
        near = pl.multiple_of(start + me[1] * half, 16)
        far = pl.multiple_of(start + (1 - me[1]) * half, 16)
        mine[k] = grad[pl.ds(near, half), :]
        theirs[k] = grad[pl.ds(far, half), :]


def attn_wgrad_kernel(flipped, n_dp, me, a_all, d_all, saved, dq, kv_got, mine, theirs, grad):
    cols = dq.shape[1]
    qcols = cols - HD
    rows = a_all.shape[0] // 4
    got = [kv_got[r * rows : (r + 1) * rows, :] for r in (1, 0, 3, 2)]
    kv = (dq[:, qcols:].astype(F32) + jnp.concatenate(got, axis=0).astype(F32)).astype(BF)
    a = a_all[...]
    grad[:, :qcols] = dot(a, dq[:, :qcols], 0, 0).astype(BF)
    grad[:, qcols:cols] = dot(a, kv, 0, 0).astype(BF)
    grad[:, cols:] = dot(d_all[...], saved[:, qcols + 2 * HD :], 0, 0).astype(BF)
    split_rows(me, n_dp, grad, mine, theirs, flipped)


def slot_rows(pos_row, s, experts, cap):
    slot = lax.broadcasted_iota(jnp.int32, (cap, pos_row.shape[2]), 0)
    hits = [(slot == pos_row[s, e : e + 1, :]).astype(F32) for e in range(experts)]
    return jnp.concatenate(hits, axis=0).astype(BF)


def start_all(*copies):
    for copy in copies:
        copy.start()
    return list(copies)


def wait_all(copies):
    for copy in copies:
        copy.wait()


def slot_gates(hit, gate_cols, s, experts, cap):
    both = dot(hit, gate_cols[s], 1, 0)
    lane = lax.broadcasted_iota(jnp.int32, both.shape, 1)
    own = lax.broadcasted_iota(jnp.int32, both.shape, 0) // cap
    return jnp.sum(jnp.where((lane == own) | (lane == own + experts), both, 0.0), axis=1, keepdims=True)


def gathered(me, ref, batch, count):
    return [[(ref, ((me[0] ^ s) * 4 + (me[3] ^ r), batch)) for r in range(4)] for s in range(count)]


def sequences(refs, count):
    out = []
    for at in range(0, len(refs), 8):
        out.append([(refs[at + r], None) for r in range(4)])
        out += [[(refs[at + 4 + r], s) for r in range(4)] for s in range(count - 1)]
    return out


def dispatch(tasks, ring, sems, pos_row, gate_cols, gates, experts, cap, following=()):
    def fetch(i):
        copies = []
        for r, (ref, at) in enumerate(tasks[i][0]):
            rows = ref.shape[-2]
            target = ring.at[i % DEPTH, pl.ds(r * rows, rows)]
            source = ref if at is None else ref.at[at]
            copies.append(pltpu.make_async_copy(source, target, sems.at[i % DEPTH, r]))
        return start_all(*copies)

    coming = [fetch(i) for i in range(min(DEPTH, len(tasks)))]
    following = list(following)
    for i, (_, s, into) in enumerate(tasks):
        wait_all(coming[i])
        hit = slot_rows(pos_row, s, experts, cap)
        picked = dot(hit, ring[i % DEPTH], 1, 0).astype(BF)
        for e in range(experts):
            into[e, s * cap : (s + 1) * cap, :] = picked[e * cap : (e + 1) * cap, :]
        if gates is not None and i < pos_row.shape[0]:
            gate = slot_gates(hit, gate_cols, s, experts, cap)
            for e in range(experts):
                gates[e, s * cap : (s + 1) * cap, :] = gate[e * cap : (e + 1) * cap, :]
        if i + DEPTH < len(tasks):
            coming.append(fetch(i + DEPTH))
        for copy in following[:2]:
            copy.start()
        following = following[2:]
    start_all(*following)


def place(out, result, e, cap):
    out = out.astype(BF)
    for s in range(result.shape[0]):
        result[s, e * cap : (e + 1) * cap, :] = out[s * cap : (s + 1) * cap, :]


def combine(values, pos_row, keep, send, experts, cap, rows, order=None):
    for s in range(values.shape[0]):
        total = dot(slot_rows(pos_row, s, experts, cap), values[s], 0, 0).astype(BF)
        at = s if order is None else order[s]
        for r in range(4):
            (send if r % 2 else keep)[r // 2, at] = total[r * rows : (r + 1) * rows, :]


def silu_parts(gu):
    half = gu.shape[1] // 2
    gate, up = gu[:, :half], gu[:, half:]
    sg = 1.0 / (1.0 + jnp.exp(-gate))
    return gate, up, sg


def gate_up_grad(dz, gate, up, sg, out):
    half = gate.shape[1]
    out[:, :half] = (dz * up * sg * (1.0 + gate * (1.0 - sg))).astype(BF)
    out[:, half:] = (dz * gate * sg).astype(BF)


def take(refs, *counts):
    parts, at = [], 0
    for count in counts:
        parts.append(refs[at : at + count])
        at += count
    return parts


def expert_weights(w_in, w_out, wi, wo, sems):
    copies = [
        [
            pltpu.make_async_copy(w_in.at[e], wi.at[e], sems.at[2 * e]),
            pltpu.make_async_copy(w_out.at[e], wo.at[e], sems.at[2 * e + 1]),
        ]
        for e in range(w_in.shape[0])
    ]
    return copies, [copy for pair in copies for copy in pair]


def moe_fwd_kernel(experts, cap, rows, count, n_blocks, *refs):
    blocks, ins, outs, scratch = take(refs, n_blocks, 4, 3, 9)
    pos_row, gate_cols, w_in, w_out = ins
    gu_out, keep, send = outs
    ring, x_all, result, gates, gu_all, wi, wo, sems, ring_sems = scratch
    weights, coming = expert_weights(w_in, w_out, wi, wo, sems)
    tasks = [(places, s, x_all) for s, places in enumerate(sequences(blocks, count))]
    dispatch(tasks, ring, ring_sems, pos_row, gate_cols, gates, experts, cap, coming)
    for e in range(experts):
        wait_all(weights[e])
        gu = dot(x_all[e], wi[e], 1, 0)
        gu_all[e] = gu
        gate, up, sg = silu_parts(gu)
        z = (gate * sg * up * gates[e]).astype(BF)
        place(dot(z, wo[e], 1, 0), result, e, cap)
    done = start_all(pltpu.make_async_copy(gu_all, gu_out, sems.at[2 * experts]))
    combine(result, pos_row, keep, send, experts, cap, rows)
    wait_all(done)


def moe_bwd_kernel(experts, cap, rows, count, n_blocks, *refs):
    blocks, ins, outs, scratch = take(refs, n_blocks, 5, 4, 11)
    pos_row, gate_cols, gu_in, w_in, w_out = ins
    z_out, dgu_out, keep, send = outs
    ring, dr_all, result, gates, gu_all, z_all, dgu_all, wi, wo, sems, ring_sems = scratch
    weights, coming = expert_weights(w_in, w_out, wi, wo, sems)
    fetched = pltpu.make_async_copy(gu_in, gu_all, sems.at[2 * experts])
    tasks = [(places, s, dr_all) for s, places in enumerate(sequences(blocks, count))]
    dispatch(tasks, ring, ring_sems, pos_row, gate_cols, gates, experts, cap, [fetched] + coming)
    fetched.wait()
    for e in range(experts):
        wait_all(weights[e])
        gate, up, sg = silu_parts(gu_all[e])
        z_all[e] = (gate * sg * up * gates[e]).astype(BF)
        gate_up_grad(dot(dr_all[e], wo[e], 1, 1) * gates[e], gate, up, sg, dgu_all.at[e])
        place(dot(dgu_all[e], wi[e], 1, 1), result, e, cap)
    done = start_all(
        pltpu.make_async_copy(z_all, z_out, sems.at[2 * experts + 1]),
        pltpu.make_async_copy(dgu_all, dgu_out, sems.at[2 * experts + 2]),
    )
    combine(result, pos_row, keep, send, experts, cap, rows)
    wait_all(done)


def moe_turn_kernel(experts, cap, rows, count, n_blocks, batches, me, *refs):
    blocks, ins, outs, scratch = take(refs, n_blocks, 5, 4, 11)
    grads, pos_row, gate_cols, w_in, w_out = ins
    z_out, dgu_out, keep, send = outs
    ring, x_all, dr_all, result, gates, z_all, dgu_all, wi, wo, sems, ring_sems = scratch
    weights, coming = expert_weights(w_in, w_out, wi, wo, sems)
    grad_places = [places for batch in batches for places in gathered(me, grads, batch, count)]
    tasks = [(places, s, x_all) for s, places in enumerate(sequences(blocks, count))]
    tasks += [(places, s, dr_all) for s, places in enumerate(grad_places)]
    dispatch(tasks, ring, ring_sems, pos_row, gate_cols, gates, experts, cap, coming)
    for e in range(experts):
        wait_all(weights[e])
        gu = dot(x_all[e], wi[e], 1, 0)
        gate, up, sg = silu_parts(gu)
        z_all[e] = (gate * sg * up * gates[e]).astype(BF)
        gate_up_grad(dot(dr_all[e], wo[e], 1, 1) * gates[e], gate, up, sg, dgu_all.at[e])
        place(dot(dgu_all[e], wi[e], 1, 1), result, e, cap)
    done = start_all(
        pltpu.make_async_copy(z_all, z_out, sems.at[2 * experts]),
        pltpu.make_async_copy(dgu_all, dgu_out, sems.at[2 * experts + 1]),
    )
    combine(result, pos_row, keep, send, experts, cap, rows)
    wait_all(done)


def moe_out_kernel(experts, cap, rows, count, me, z, pos_row, w_out, keep, send, result):
    for e in range(experts):
        place(dot(z[e], w_out[e], 1, 0), result, e, cap)
    order = [s // count * count + (me[0] ^ (s % count)) for s in range(pos_row.shape[0])]
    combine(result, pos_row, keep, send, experts, cap, rows, order)


def moe_wgrad_kernel(experts, cap, count, n_blocks, *refs):
    me, refs = refs[0], refs[1:]
    x0, g0, x1, ins, hidden, outs, scratch = take(refs, n_blocks, n_blocks, n_blocks, 2, 4, 2, 9)
    cots, pos_row = ins
    dwin, dwout = outs
    ring, x_all, dr_all, dgu, z, din, dout, sems, ring_sems = scratch

    def tokens(x_places, g_places, dgu_in, z_in):
        fetched = start_all(
            pltpu.make_async_copy(dgu_in, dgu, sems.at[4]), pltpu.make_async_copy(z_in, z, sems.at[5])
        )
        tasks = [(places, s, x_all) for s, places in enumerate(x_places)]
        tasks += [(places, s, dr_all) for s, places in enumerate(g_places)]
        dispatch(tasks, ring, ring_sems, pos_row, None, None, experts, cap)
        wait_all(fetched)

    @pl.when(me[1] == 0)
    def _():
        tokens(sequences(x0, count), sequences(g0, count), hidden[0], hidden[1])

    @pl.when(me[1] == 1)
    def _():
        places = [part for batch in (1, 0) for part in gathered(me, cots, batch, count)]
        tokens(sequences(x1, count), places, hidden[2], hidden[3])

    leaving = [[], []]
    for e in range(experts):
        slot = e % 2
        wait_all(leaving[slot])
        din[slot] = dot(x_all[e], dgu[e], 0, 0)
        dout[slot] = dot(z[e], dr_all[e], 0, 0)
        leaving[slot] = start_all(
            pltpu.make_async_copy(din.at[slot], dwin.at[e], sems.at[slot]),
            pltpu.make_async_copy(dout.at[slot], dwout.at[e], sems.at[2 + slot]),
        )
    wait_all(leaving[0] + leaving[1])


def per_device(
    block_input, segments, expert_ids, gate_values, cotangent, attn_gain,
    query_weight, kv_weight, out_weight, moe_gain, w_in, w_out,
):
    sec = lax.axis_index("section")
    dp = lax.axis_index("dp")
    t = lax.axis_index("tensor")
    n_dp = lax.axis_size("dp")
    n_t = lax.axis_size("tensor")
    first = sec == 0
    core0 = t % 2 == 0
    me = jnp.stack([dp, sec, t % 2, t]).astype(jnp.int32)
    rows, width = block_input.shape[1], block_input.shape[2]
    seq = segments.shape[1]
    top = expert_ids.shape[3]
    heads = query_weight.shape[2] // HD
    qcols = heads * HD
    experts, ffn = w_in.shape[1], w_out.shape[2]
    cap = -(-(seq * top * 9 // (8 * E)) // 16) * 16
    sides = 2 if n_dp <= TOGETHER else 1
    total = 2 * n_dp
    slots = total * cap
    dp_order = jnp.arange(n_dp, dtype=jnp.int32) ^ dp
    t_order = jnp.arange(n_t, dtype=jnp.int32) ^ t
    drows = width // n_dp
    half = drows // 2

    pair = jax.ShapeDtypeStruct((2, rows, width), BF)
    smem = pl.BlockSpec(memory_space=pltpu.SMEM)
    vmem = pl.BlockSpec(memory_space=pltpu.VMEM)
    any_space = pl.BlockSpec(memory_space=pl.ANY)
    hbm = pl.BlockSpec(memory_space=pltpu.HBM)
    seq_scratch = pltpu.VMEM((seq, width), BF)

    def me_after(*tokens):
        return jnp.where(there(*tokens), me, 0) if tokens else me

    def shape(*dims, dtype=BF):
        return jax.ShapeDtypeStruct(dims, dtype)

    def call(
        kernel, name, ins, outs, scratch, limit, cost, in_specs=None, out_specs=None, hold=(), tokens=()
    ):
        n_ins, n_outs, n_hold, n_tok = len(ins), len(outs), len(hold), len(tokens)

        def body(*refs):
            given, results, rest = take(refs, n_ins + n_tok + n_hold, n_outs + n_hold, len(scratch))
            kernel(*given[:n_ins], *results[:n_outs], *rest)

        out = pl.pallas_call(
            body,
            out_shape=list(outs) + [jax.ShapeDtypeStruct(h.shape, h.dtype) for h in hold],
            in_specs=(in_specs or [smem] + [vmem] * (n_ins - 1)) + [any_space] * (n_tok + n_hold),
            out_specs=(out_specs or [vmem] * n_outs) + [any_space] * n_hold,
            scratch_shapes=scratch,
            input_output_aliases={n_ins + n_tok + i: n_outs + i for i in range(n_hold)},
            compiler_params=pltpu.CompilerParams(vmem_limit_bytes=limit * MIB),
            cost_estimate=pl.CostEstimate(flops=cost * 10**9, bytes_accessed=cost * 3 * MIB, transcendentals=0),
            name=name,
        )(*ins, *tokens, *hold)
        return out[:n_outs], out[n_outs:]

    acols = 2 * qcols + 2 * HD
    weights_scratch = pltpu.VMEM((width, acols), BF)
    weights_sems = pltpu.SemaphoreType.DMA((2, n_dp))

    def attn_fwd(a_blocks, weights, tokens=()):
        return call(
            functools.partial(attn_fwd_kernel, heads), "attn_fwd",
            (me, weights, *a_blocks, table),
            [pair, pair, shape(seq, acols), shape(seq, width)],
            [weights_scratch, weights_sems], 20, 0, [smem, hbm] + [vmem] * 5, tokens=tokens,
        )[0]

    def attn_bwd(d_blocks, saved, weights):
        return call(
            functools.partial(attn_bwd_kernel, heads), "attn_bwd",
            (me, weights, *d_blocks, saved, table),
            [pair, pair, shape(seq, qcols + HD), shape(seq, HD), shape(seq, width)],
            [weights_scratch, weights_sems, pltpu.VMEM((seq, qcols + 2 * HD), BF)], 20, 0,
            [smem, hbm] + [vmem] * 6,
        )[0]

    tok_f32, tok_bf = shape(rows, width, dtype=F32), shape(rows, width)

    def finish(base, gain, terms, hold=()):
        (out, normed), held = call(
            functools.partial(finish_kernel, [at for _, at in terms]), "finish",
            (base, gain, *[value for value, _ in terms]), [tok_f32, tok_bf], [], 8, 0,
            [vmem] * (2 + len(terms)), hold=hold,
        )
        return out, normed, held

    def norm_back(x, gain, upper, terms, more=(), tokens=()):
        return call(
            functools.partial(norm_back_kernel, [at for _, at in terms]), "norm_back",
            (x, gain, upper, *[value for value, _ in terms], *more),
            [tok_f32] * (1 + len(more)) + [tok_bf, shape(1, width, dtype=F32)], [], 8, 0,
            [vmem] * (3 + len(terms) + len(more)), tokens=tokens,
        )

    def halves_grad(kernel, name, ins, cols):
        return call(
            functools.partial(kernel, n_dp), name, (me, *ins), [shape(n_dp, half, cols)] * 2,
            [pltpu.VMEM((width, cols), BF)], 20, 1,
        )[0]

    count = sides * n_dp
    part_slots = count * cap
    weight_scratch = [pltpu.VMEM((experts, width, 2 * ffn), BF), pltpu.VMEM((experts, ffn, width), BF)]
    ring_scratch = pltpu.VMEM((DEPTH, seq, width), BF)
    slot_scratch = pltpu.VMEM((experts, part_slots, width), BF)
    result_scratch = pltpu.VMEM((count, experts * cap, width), BF)
    z_scratch = pltpu.VMEM((experts, part_slots, ffn), BF)
    dgu_scratch = pltpu.VMEM((experts, part_slots, 2 * ffn), BF)
    gu_scratch = pltpu.VMEM((experts, part_slots, 2 * ffn), F32)
    gate_scratch = pltpu.VMEM((experts, part_slots, 1), F32)
    copy_sems = pltpu.SemaphoreType.DMA((2 * experts + 3,))
    ring_sems = pltpu.SemaphoreType.DMA((DEPTH, 4))
    gu_shape = shape(experts, part_slots, 2 * ffn, dtype=F32)
    z_shape = shape(experts, part_slots, ffn)
    dgu_shape = shape(experts, part_slots, 2 * ffn)
    sum_shapes = [shape(2, count, rows, width)] * 2
    expert_args = (w_in[0], w_out[0])

    def by_sides(run, arrays, axes):
        if sides == 2:
            return run(arrays, (0, 1))
        size = [value.shape[axis] // 2 for value, axis in zip(arrays, axes)]
        outs = []
        for side in range(2):
            parts = [
                lax.slice_in_dim(value, side * n, (side + 1) * n, axis=axis)
                for value, n, axis in zip(arrays, size, axes)
            ]
            outs.append(run(parts, (side,)))
        return [jnp.concatenate(both, axis=1) for both in zip(*outs)]

    def of_sides(blocks, which):
        return [part for side in which for part in blocks[side]]

    def moe_fwd(blocks, route):
        def run(arrays, which):
            parts = of_sides(blocks, which)
            return call(
                functools.partial(moe_fwd_kernel, experts, cap, rows, n_dp, len(parts)), "moe_fwd",
                (*parts, *arrays, *expert_args), [gu_shape] + sum_shapes,
                [
                    ring_scratch, slot_scratch, result_scratch, gate_scratch, gu_scratch, *weight_scratch, copy_sems, ring_sems,
                ],
                48, COST, [any_space] * len(parts) + [vmem] * 2 + [hbm] * 2, [hbm] + [vmem] * 2,
            )[0]

        gu, keep, send = by_sides(run, route, (0, 0))
        return gu, (keep, send)

    def moe_bwd(blocks, gu, route):
        def run(arrays, which):
            parts = of_sides(blocks, which)
            return call(
                functools.partial(moe_bwd_kernel, experts, cap, rows, n_dp, len(parts)), "moe_bwd",
                (*parts, *arrays, *expert_args), [z_shape, dgu_shape] + sum_shapes,
                [
                    ring_scratch, slot_scratch, result_scratch, gate_scratch, gu_scratch, z_scratch,
                    dgu_scratch,
                    *weight_scratch, copy_sems, ring_sems,
                ],
                50, COST, [any_space] * len(parts) + [vmem] * 2 + [hbm] * 3, [hbm] * 2 + [vmem] * 2,
            )[0]

        z, dgu, keep, send = by_sides(run, (*route, gu), (0, 0, 1))
        return (dgu, z), (keep, send)

    def moe_turn(blocks, grads, route):
        def run(arrays, which):
            parts = of_sides(blocks, which)
            batches = [1 - side for side in which]
            return call(
                functools.partial(
                    moe_turn_kernel, experts, cap, rows, n_dp, len(parts), batches
                ),
                "moe_turn", (me, *parts, grads, *arrays, *expert_args),
                [z_shape, dgu_shape] + sum_shapes,
                [
                    ring_scratch, slot_scratch, slot_scratch, result_scratch, gate_scratch, z_scratch,
                    dgu_scratch,
                    *weight_scratch, copy_sems, ring_sems,
                ],
                57, COST * 2, [smem] + [any_space] * (len(parts) + 1) + [vmem] * 2 + [hbm] * 2,
                [hbm] * 2 + [vmem] * 2,
            )[0]

        z, dgu, keep, send = by_sides(run, route, (0, 0))
        return (dgu, z), (keep, send)

    def moe_out(z, route, *tokens):
        def run(arrays, which):
            return call(
                functools.partial(moe_out_kernel, experts, cap, rows, n_dp), "moe_out",
                (me_after(*tokens), *arrays, w_out[0]), sum_shapes, [result_scratch], 32, COST,
            )[0]

        return by_sides(run, (z, route[0]), (1, 0))

    def moe_wgrad(blocks0, grads0, blocks1, hidden, route, *tokens):
        arrays = [of_sides(blocks, (0, 1)) for blocks in (blocks0, grads0, blocks1)]
        return call(
            functools.partial(moe_wgrad_kernel, experts, cap, n_dp, len(arrays[0])), "moe_wgrad",
            (me_after(*tokens), *arrays[0], *arrays[1], *arrays[2], cot_all, route, *hidden),
            [shape(experts, width, 2 * ffn, dtype=F32), shape(experts, ffn, width, dtype=F32)],
            [
                ring_scratch, pltpu.VMEM((experts, slots, width), BF), pltpu.VMEM((experts, slots, width), BF),
                pltpu.VMEM((experts, slots, 2 * ffn), BF), pltpu.VMEM((experts, slots, ffn), BF),
                pltpu.VMEM((2, width, 2 * ffn), F32), pltpu.VMEM((2, ffn, width), F32),
                pltpu.SemaphoreType.DMA((6,)), ring_sems,
            ],
            48, 10, [smem] + [hbm] * (3 * len(arrays[0]) + 1) + [vmem] + [hbm] * 4, [hbm] * 2,
        )[0]

    gains = jnp.concatenate([attn_gain, moe_gain], axis=0)
    gains = jnp.stack(over_tensor(gains))[t_order].transpose(1, 0, 2).reshape(2, drows)
    gains = jnp.stack([gains] + [move(gains, dp=k) for k in range(1, n_dp)])[dp_order]
    gains = gains.transpose(1, 0, 2).reshape(2, 1, width)
    gains_far = move(gains, section=1)
    layer_gain = [jnp.where(sec == l, gains, gains_far).astype(F32) for l in range(2)]
    (gains0, gains1) = layer_gain

    def seeds_of(matrix):
        low, high = matrix[:half], matrix[half:]
        return jnp.where(first, low, high), move(jnp.where(first, high, low), section=1)

    def gather_weights(seed):
        return lax.all_gather(seed[None, None], ("section", "dp"), axis=0, tiled=True).reshape(
            2, n_dp, half, acols
        )

    kv_own = kv_turn(kv_weight[0])
    kv_core = move(kv_own, tensor=1)
    key_value = jnp.where(
        core0, jnp.concatenate([kv_own, kv_core], axis=1), jnp.concatenate([kv_core, kv_own], axis=1)
    )
    routing = jnp.concatenate([expert_ids[0].astype(F32), gate_values[0]], axis=2)
    routing = [routing] + [move(routing, dp=k) for k in range(1, n_dp)]
    seed_near, seed_far = seeds_of(
        jnp.concatenate([query_weight[0], key_value, out_weight[0].T], axis=1)
    )

    segment = jnp.where(first, segments[0], segments[1])
    ordinal = jnp.arange(seq, dtype=jnp.int32)
    start = jnp.sum((segment[None, :] < segment[:, None]).astype(jnp.int32), axis=1)
    places = (ordinal - start).astype(F32)

    def turned(vector):
        return vector.reshape(n_t, rows)[t_order].reshape(seq)

    start_col = turned(start)[:, None]
    frequency = THETA ** (-2.0 * jnp.arange(HD // 2, dtype=F32) / HD)
    angles = turned(places)[:, None] * frequency[None, :]
    cosine = jnp.cos(angles)
    cosine = jnp.concatenate([cosine, cosine], axis=1)
    sine = jnp.sin(angles)
    sine = jnp.concatenate([-sine, sine], axis=1)
    table = jnp.concatenate([cosine, sine, jnp.pad(start_col.astype(F32), ((0, 0), (0, HD - 1)))], axis=1)

    def routes_of(routing):
        routing = jnp.stack(routing)
        routing = routing.reshape(n_dp, 2, n_t, rows, 2 * top)[:, :, t_order]
        routing = routing.reshape(n_dp, 2, seq, 2 * top)
        names = (dp * experts + jnp.arange(experts, dtype=jnp.int32)).astype(F32)
        chosen = routing[:, :, :, :top, None] == names
        member = jnp.sum(chosen.astype(F32), axis=3)
        gates = jnp.sum(jnp.where(chosen, routing[:, :, :, top:, None], 0.0), axis=3)
        lower = (ordinal[:, None] > ordinal[None, :]).astype(BF)
        rank = jnp.einsum("ij,smje->smei", lower, member.astype(BF), preferred_element_type=F32)
        slot = jnp.where(member.transpose(0, 1, 3, 2) > 0.5, rank, -1.0).astype(jnp.int32)
        gate_high = gates.astype(BF)
        gate_low = (gates - gate_high.astype(F32)).astype(BF)
        gate_cols = jnp.concatenate([gate_high, gate_low], axis=3)
        gate_cols = jnp.pad(gate_cols, ((0, 0), (0, 0), (0, 0), (0, HD - 2 * experts)))
        return [
            tuple(jnp.concatenate([part[:, b], part[:, 1 - b]]) for part in (slot, gate_cols))
            for b in range(2)
        ]

    def spread(value):
        near, far = [value, move(value, tensor=2)], [move(value, section=1), move(value, section=1, tensor=2)]
        return [[part[0], move(part[0], tensor=1), part[1], move(part[1], tensor=1)] for part in (near, far)]

    def to_host(own, *tokens):
        near_own, far_own = spread(own)
        others = jnp.stack([move(own, dp=k) for k in range(1, n_dp)])
        near, far = spread(after(others, near_own[2], far_own[0], far_own[2], *tokens))
        return near_own + near, far_own + far

    def core_sums(keep, send, *tokens):
        got = move(send, tensor=1)
        sums = [
            [keep[y, at : at + n_dp] + got[y, at : at + n_dp] for y in range(2)] for at in (0, n_dp)
        ]
        if tokens:
            sums[1][1] = after(sums[1][1], *tokens)
        return sums

    def gather_sums(near, far, host, *tokens):
        near = near[0] + move(near[1], tensor=2)
        far = move(far[0], section=1) + move(far[1], section=1, tensor=2)
        total = jnp.where(sec == host, near, far)
        return after(total, *tokens) if tokens else total

    def parts_of(near, far, which):
        return [[part[which] for part in side] for side in (near, far)]

    def others_sums(near, far, host, *tokens):
        return gather_sums(*parts_of(near, far, slice(1, None)), host, *tokens)

    def all_sums(near, far, others, host, *tokens):
        total = gather_sums(*parts_of(near, far, 0), host).astype(F32)
        for k in range(1, n_dp):
            total = total + move(others[k - 1], dp=k).astype(F32)
        return [(after(total, *tokens) if tokens else total, None)]

    def from_host(near, far, host):
        return all_sums(near, far, others_sums(near, far, host), host)

    x0 = jnp.where(first, block_input[0], block_input[1])
    seed = jnp.where(first & there(*routing[1:]), seed_near, seed_far)
    weights0 = gather_weights(seed)
    _, a, _ = finish(x0, gains0[0], [])

    routes = routes_of(routing)
    a_blocks = over_tensor(a)
    keep, send, saved, a_all = attn_fwd(
        a_blocks, weights0, routes[0]
    )
    part0, part1 = sum_over_tensor(keep, send)
    mid, m, _ = finish(x0, gains0[1], [(part0, None), (part1, None)])
    kept0 = (x0, a_all, saved, mid, weights0)
    cot_far = move(jnp.where(first, cotangent[0, 1], cotangent[0, 0]), section=1)
    cot_near = jnp.where(first, cotangent[0, 0], cotangent[0, 1])
    cots = jnp.stack([jnp.where(first, cot_near, cot_far), jnp.where(first, cot_far, cot_near)])
    near, far = to_host(m, cots[0])
    there_now = [part.reshape(-1, width)[:half, :acols] for part in (near[6], far[4], far[6])]
    weights1 = gather_weights(after(jnp.where(first, seed_far, seed_near), *there_now))
    cot_all = after(cotangent[0].astype(BF), *[part[:1] for part in (near[6], far[4], far[6])])
    cot_all = lax.all_gather(cot_all[None], ("dp", "tensor"), axis=0, tiled=True)
    blocks0 = (near, far)
    gu0, sums = moe_fwd(blocks0, routes[0])
    terms = from_host(*core_sums(*sums), 0)
    out0, a, _ = finish(mid, gains1[0], terms)

    a_blocks = over_tensor(a)
    keep, send, saved, a_all = attn_fwd(a_blocks, weights1)
    part0, part1 = sum_over_tensor(keep, send)
    mid, m, _ = finish(out0, gains1[1], [(part0, None), (part1, None)])
    kept1 = (out0, a_all, saved, mid, weights1)
    near, far = to_host(m)
    blocks1 = (near, far)
    hidden1, sums = moe_turn(blocks1, cot_all, routes[1])
    terms = from_host(*core_sums(*sums), 1)

    cot_far = move(jnp.where(first, cotangent[0, 1], cotangent[0, 0]), section=1)
    cot_near = jnp.where(first, cotangent[0, 0], cotangent[0, 1])
    cots = (jnp.where(first, cot_near, cot_far), jnp.where(first, cot_far, cot_near))

    def attention_back(kept, l, g, terms, more, beside=None):
        x, a_all, saved, mid, weights = kept
        (dmid, d, moe_gain_sum), _ = norm_back(mid, layer_gain[l][1], g, terms)
        d_blocks = over_tensor(d)
        extra = core_sums(*beside(d)) if beside is not None else None
        if extra is not None:
            d_blocks[3] = after(d_blocks[3], extra[1][0][0])
        keep, send, dq, kv_send, d_all = attn_bwd(d_blocks, saved, weights)
        args = (a_all, d_all, saved, dq, move(kv_send, tensor=1))
        mine, theirs = halves_grad(
            functools.partial(attn_wgrad_kernel, l == 0), "attn_wgrad", args, 2 * qcols + HD
        )
        part0, part1 = sum_over_tensor(keep, send)
        (*outs, attn_gain_sum), _ = norm_back(
            x, layer_gain[l][0], dmid, [(part0, None), (part1, None)], more
        )
        return outs, jnp.concatenate([attn_gain_sum, moe_gain_sum]), mine, theirs, extra

    (in_grad1, g, g_low), gain_sums1, mine, theirs, outs = attention_back(
        kept1, 1, cots[1], terms, (cots[0],), lambda d: moe_out(hidden1[1], routes[1], d)
    )
    out_first, out_second = (jnp.stack([side[y] for side in outs]) for y in range(2))
    grad1 = jnp.where(first, jnp.stack([mine, theirs]), jnp.stack([theirs, mine]))
    near, far = to_host(g_low, grad1[0, 0, :1, :1])
    shard1_sum = lax.psum_scatter(
        grad1.reshape(2 * n_dp, half, acols - HD), ("section", "dp"), scatter_dimension=0, tiled=True
    )
    grads0 = (near, far)
    hidden0, sums = moe_bwd(grads0, gu0, routes[0])
    near_far = core_sums(*sums, shard1_sum[0, :1, :1])
    route = jnp.where(first, routes[0][0], routes[1][0])
    dw_in, dw_out = moe_wgrad(
        blocks0, grads0, blocks1, (*hidden0, *hidden1), route, near_far[1][1]
    )
    others = others_sums(*near_far, 0, dw_out[0, :rows])
    terms = all_sums(*near_far, others, 0)
    (in_grad0, _), gain_sums0, mine, theirs, _ = attention_back(kept0, 0, g, terms, ())
    out_across = move(after(out_second, in_grad0[None, None]), tensor=2)
    out1_sum = lax.psum_scatter(
        (out_first + out_across).swapaxes(0, 1), "dp", scatter_dimension=0, tiled=True
    )[0].astype(F32)

    gain_sums = jnp.concatenate([gain_sums0, gain_sums1])
    gain_sums = gain_sums + move(gain_sums, tensor=1)
    gain_sums = after(gain_sums + move(gain_sums, tensor=2), out_across[0, 0, :4])
    gain_sums = gain_sums.astype(BF).reshape(4, n_dp, drows).transpose(1, 0, 2)[dp_order]
    gain_sums = jnp.pad(gain_sums, ((0, 0), (0, 12), (0, 2 * qcols + HD - drows)))
    parts = jnp.concatenate([mine + move(theirs, section=1), gain_sums], axis=1)
    parts = [parts[0]] + [move(parts[k], dp=k) for k in range(1, n_dp)]
    shard1 = shard1_sum[0].astype(F32)
    shard0 = sum(part.astype(F32) for part in parts)

    gain0, gain1 = shard0[half : half + 2], shard0[half + 2 : half + 4]
    own = jnp.where(first, shard0[:half], shard1)
    own_gain = jnp.where(first, gain0, gain1)[:, :drows]
    far = jnp.concatenate([
        jnp.where(first, shard1, shard0[:half]),
        jnp.pad(jnp.where(first, gain1, gain0), ((0, 14), (0, 0))),
    ])
    far = move(far.astype(BF), section=1).astype(F32)
    grad_shard = jnp.where(
        first, jnp.concatenate([own, far[:half]]), jnp.concatenate([far[:half], own])
    )
    gains = own_gain + far[half : half + 2, :drows]
    gains = lax.dynamic_slice_in_dim(gains, t * attn_gain.shape[1], attn_gain.shape[1], 1)
    cols = qcols + HD
    grad_out = grad_shard[:, cols:].T
    grad_kv = kv_turn(grad_shard[:, qcols:cols])
    def mine_and_theirs(value0, value1):
        return jnp.where(first, value0, value1), jnp.where(first, value1, value0)

    grad_near, grad_far = mine_and_theirs(in_grad0, in_grad1)
    out_swap = jnp.where(first, mid, out0)
    theirs = move(jnp.stack([out_swap, grad_far]).astype(BF), section=1).astype(F32)
    out_near = jnp.where(first, out0, mid + out1_sum[0])
    out_far = jnp.where(first, theirs[0], theirs[0] + out1_sum[1])

    def both_batches(near, far):
        return jnp.where(first, jnp.stack([near, far]), jnp.stack([far, near]))[None]

    return (
        both_batches(out_near, out_far),
        both_batches(grad_near, theirs[1]),
        gains[0:1],
        grad_shard[None, :, :qcols],
        grad_kv[None],
        grad_out[None],
        gains[1:2],
        dw_in[None],
        dw_out[None],
    )


def solution(mesh):
    return jax.shard_map(
        per_device,
        mesh=mesh,
        in_specs=(
            P(None, ("dp", "tensor"), None),
            P(None, "dp"),
            P("section", None, "dp", None),
            P("section", None, "dp", None),
            P("section", None, ("dp", "tensor"), None),
            P("section", ("dp", "tensor")),
            P("section", "dp", "tensor"),
            P("section", "dp", "tensor"),
            P("section", "tensor", "dp"),
            P("section", ("dp", "tensor")),
            P("section", "dp", None, "tensor"),
            P("section", "dp", "tensor", None),
        ),
        out_specs=(
            P("section", None, ("dp", "tensor"), None),
            P("section", None, ("dp", "tensor"), None),
            P("section", ("dp", "tensor")),
            P("section", "dp", "tensor"),
            P("section", "dp", "tensor"),
            P("section", "tensor", "dp"),
            P("section", ("dp", "tensor")),
            P("section", "dp", None, "tensor"),
            P("section", "dp", "tensor", None),
        ),
        check_vma=False,
    )
```

```python
import functools

import jax
import jax.numpy as jnp
from jax import lax
from jax.experimental import pallas as pl
from jax.experimental.pallas import tpu as pltpu
from jax.sharding import PartitionSpec as P

H = 12
KVH = 2
HD = 128
E = 16

EPS = 1e-06
THETA = 10000.0
BF = jnp.bfloat16
F32 = jnp.float32
MIB = 1024 * 1024
COST = 4
TOGETHER = 4
DEPTH = 4


def dot(a, b, ca, cb):
    return lax.dot_general(a, b, (((ca,), (cb,)), ((), ())), preferred_element_type=F32)


def move(value, section=0, dp=0, tensor=0):
    n_dp, n_t = lax.axis_size("dp"), lax.axis_size("tensor")
    pairs = []
    for s in range(2):
        for d in range(n_dp):
            for t in range(n_t):
                here = (s * n_dp + d) * n_t + t
                pairs.append((here, ((s ^ section) * n_dp + (d ^ dp)) * n_t + (t ^ tensor)))
    return lax.ppermute(value, ("section", "dp", "tensor"), pairs)


def kv_turn(value):
    return lax.ppermute(value, "tensor", [(0, 0), (1, 2), (2, 1), (3, 3)])


def over_tensor(value):
    across = move(value, tensor=2)
    return [value, move(value, tensor=1), across, move(across, tensor=1)]


def after(value, *tokens):
    ready = functools.reduce(jnp.logical_and, [token == token for token in tokens])
    return jnp.where(ready, value, jnp.zeros_like(value))


def there(*tokens):
    marks = [token[(0,) * token.ndim].astype(F32) for token in tokens]
    total = functools.reduce(jnp.add, marks)
    return total == total


def sum_over_tensor(keep, send):
    total = keep + move(send, tensor=1)
    return total[0], move(total[1], tensor=2)


def rope(value, cosine, sine):
    return value * cosine + pltpu.roll(value, HD // 2, 1) * sine


def allowed_pairs(me, rows, start):
    def places(axis):
        at = lax.broadcasted_iota(jnp.int32, (4 * rows, 4 * rows), axis)
        return (me[3] ^ (at // rows)) * rows + at % rows

    keys = places(1)
    return (keys <= places(0)) & (keys >= start.astype(jnp.int32))


def assemble(blocks, weights, sems):
    halves, n_dp, half = blocks.shape[:3]
    return start_all(*[
        pltpu.make_async_copy(
            blocks.at[part, k], weights.at[pl.ds((2 * k + part) * half, half)], sems.at[part, k]
        )
        for part in range(halves)
        for k in range(n_dp)
    ])


def whole_sequence(blocks, into):
    rows = blocks[0].shape[0]
    for r, ref in enumerate(blocks):
        into[r * rows : (r + 1) * rows, :] = ref[...]


def attn_fwd_kernel(heads, me, blocks, a0, a1, a2, a3, table, keep, send, saved, a_all, weights, sems):
    rows, qcols = a0.shape[0], heads * HD
    copies = assemble(blocks, weights, sems)
    whole_sequence((a0, a1, a2, a3), a_all)
    wait_all(copies)
    qkv = dot(a_all[...], weights[:, : qcols + 2 * HD], 1, 0)
    co, si = table[:, :HD], table[:, HD : 2 * HD]
    k = rope(qkv[:, qcols : qcols + HD], co, si).astype(BF)
    v = qkv[:, qcols + HD :].astype(BF)
    saved[:, qcols : qcols + HD] = k
    saved[:, qcols + HD : qcols + 2 * HD] = v
    allowed = allowed_pairs(me, rows, table[:, 2 * HD : 2 * HD + 1])
    for h in range(heads):
        qh = rope(qkv[:, h * HD : (h + 1) * HD], co, si).astype(BF)
        saved[:, h * HD : (h + 1) * HD] = qh
        p = softmax(qh, k, allowed).astype(BF)
        at = qcols + 2 * HD + h * HD
        saved[:, at : at + HD] = dot(p, v, 1, 0).astype(BF)
    part = dot(saved[:, qcols + 2 * HD :], weights[:, qcols + 2 * HD :], 1, 1).astype(BF)
    for r in range(4):
        (send if r % 2 else keep)[r // 2] = part[r * rows : (r + 1) * rows, :]


def softmax(qh, k, allowed):
    s = jnp.where(allowed, HD ** (-0.5) * dot(qh, k, 1, 1), -1e30)
    e = jnp.exp(s - jnp.max(s, axis=1, keepdims=True))
    return e * (1.0 / jnp.sum(e, axis=1, keepdims=True))


def attn_bwd_kernel(
    heads, me, blocks, d0, d1, d2, d3, saved, table,
    keep, send, dq_out, kv_send, d_all, weights, sems, dqkv,
):
    rows, qcols = d0.shape[0], heads * HD
    copies = assemble(blocks, weights, sems)
    whole_sequence((d0, d1, d2, d3), d_all)
    wait_all(copies)
    do = dot(d_all[...], weights[:, qcols + 2 * HD :], 1, 0).astype(BF)
    co, si = table[:, :HD], -table[:, HD : 2 * HD]
    k, v = saved[:, qcols : qcols + HD], saved[:, qcols + HD : qcols + 2 * HD]
    allowed = allowed_pairs(me, rows, table[:, 2 * HD : 2 * HD + 1])
    dk = jnp.zeros((do.shape[0], HD), F32)
    dv = jnp.zeros((do.shape[0], HD), F32)
    for h in range(heads):
        qh = saved[:, h * HD : (h + 1) * HD]
        doh = do[:, h * HD : (h + 1) * HD]
        p = softmax(qh, k, allowed)
        dv = dv + dot(p.astype(BF), doh, 0, 0)
        dp = dot(doh, v, 1, 1)
        ds = (p * (dp - jnp.sum(p * dp, axis=1, keepdims=True))).astype(BF)
        dq = HD ** (-0.5) * dot(ds, k, 1, 0)
        dk = dk + dot(ds, qh, 0, 0)
        dqkv[:, h * HD : (h + 1) * HD] = rope(dq, co, si).astype(BF)
    dk = rope(HD ** (-0.5) * dk, co, si).astype(BF)
    dv = dv.astype(BF)
    dqkv[:, qcols : qcols + HD] = dk
    dqkv[:, qcols + HD :] = dv
    core0 = me[2] == 0
    dq_out[:, :qcols] = dqkv[:, :qcols]
    dq_out[:, qcols:] = jnp.where(core0, dk, dv)
    kv_send[...] = jnp.where(core0, dv, dk)
    part = dot(dqkv[...], weights[:, : qcols + 2 * HD], 1, 1).astype(BF)
    for r in range(4):
        (send if r % 2 else keep)[r // 2] = part[r * rows : (r + 1) * rows, :]


def total_of(terms, places):
    total = None
    for ref, place in zip(terms, places):
        term = (ref[...] if place is None else ref[place]).astype(F32)
        total = term if total is None else total + term
    return total


def finish_kernel(places, base, gain, *refs):
    terms, (out, normed) = refs[: len(places)], refs[len(places) :]
    total = base[...]
    if places:
        total = total + total_of(terms, places)
    out[...] = total
    r = lax.rsqrt(jnp.mean(total * total, axis=1, keepdims=True) + EPS)
    normed[...] = (total * r * gain[...]).astype(BF)


def norm_back_kernel(places, rows_in, gain, upper, *refs):
    terms, rest = refs[: len(places)], refs[len(places) :]
    grad = total_of(terms, places)
    x = rows_in[...]
    r = lax.rsqrt(jnp.mean(x * x, axis=1, keepdims=True) + EPS)
    weighted = grad * gain[...]
    projected = jnp.mean(weighted * x, axis=1, keepdims=True)
    total = upper[...] + (r * weighted - x * (r * r * r) * projected)
    if len(rest) == 3:
        out, low, gain_sum = rest
        low[...] = total.astype(BF)
    else:
        more, out, following, low, gain_sum = rest
        after = more[...] + total
        following[...] = after
        low[...] = after.astype(BF)
    out[...] = total
    gain_sum[...] = jnp.sum(grad * x * r, axis=0, keepdims=True)


def split_rows(me, n_dp, grad, mine, theirs, flipped):
    half = grad.shape[0] // (2 * n_dp)
    for k in range(n_dp):
        start = (me[0] ^ k if flipped else k) * (2 * half)
        near = pl.multiple_of(start + me[1] * half, 16)
        far = pl.multiple_of(start + (1 - me[1]) * half, 16)
        mine[k] = grad[pl.ds(near, half), :]
        theirs[k] = grad[pl.ds(far, half), :]


def attn_wgrad_kernel(flipped, n_dp, me, a_all, d_all, saved, dq, kv_got, mine, theirs, grad):
    cols = dq.shape[1]
    qcols = cols - HD
    rows = a_all.shape[0] // 4
    got = [kv_got[r * rows : (r + 1) * rows, :] for r in (1, 0, 3, 2)]
    kv = (dq[:, qcols:].astype(F32) + jnp.concatenate(got, axis=0).astype(F32)).astype(BF)
    a = a_all[...]
    grad[:, :qcols] = dot(a, dq[:, :qcols], 0, 0).astype(BF)
    grad[:, qcols:cols] = dot(a, kv, 0, 0).astype(BF)
    grad[:, cols:] = dot(d_all[...], saved[:, qcols + 2 * HD :], 0, 0).astype(BF)
    split_rows(me, n_dp, grad, mine, theirs, flipped)


def slot_rows(pos_row, s, experts, cap):
    slot = lax.broadcasted_iota(jnp.int32, (cap, pos_row.shape[2]), 0)
    hits = [(slot == pos_row[s, e : e + 1, :]).astype(F32) for e in range(experts)]
    return jnp.concatenate(hits, axis=0).astype(BF)


def start_all(*copies):
    for copy in copies:
        copy.start()
    return list(copies)


def wait_all(copies):
    for copy in copies:
        copy.wait()


def slot_gates(hit, gate_cols, s, experts, cap):
    both = dot(hit, gate_cols[s], 1, 0)
    lane = lax.broadcasted_iota(jnp.int32, both.shape, 1)
    own = lax.broadcasted_iota(jnp.int32, both.shape, 0) // cap
    return jnp.sum(jnp.where((lane == own) | (lane == own + experts), both, 0.0), axis=1, keepdims=True)


def gathered(me, ref, batch, count):
    return [[(ref, ((me[0] ^ s) * 4 + (me[3] ^ r), batch)) for r in range(4)] for s in range(count)]


def sequences(refs, count):
    out = []
    for at in range(0, len(refs), 8):
        out.append([(refs[at + r], None) for r in range(4)])
        out += [[(refs[at + 4 + r], s) for r in range(4)] for s in range(count - 1)]
    return out


def dispatch(tasks, ring, sems, pos_row, gate_cols, gates, experts, cap, following=()):
    def fetch(i):
        copies = []
        for r, (ref, at) in enumerate(tasks[i][0]):
            rows = ref.shape[-2]
            target = ring.at[i % DEPTH, pl.ds(r * rows, rows)]
            source = ref if at is None else ref.at[at]
            copies.append(pltpu.make_async_copy(source, target, sems.at[i % DEPTH, r]))
        return start_all(*copies)

    coming = [fetch(i) for i in range(min(DEPTH, len(tasks)))]
    following = list(following)
    for i, (_, s, into) in enumerate(tasks):
        wait_all(coming[i])
        hit = slot_rows(pos_row, s, experts, cap)
        picked = dot(hit, ring[i % DEPTH], 1, 0).astype(BF)
        for e in range(experts):
            into[e, s * cap : (s + 1) * cap, :] = picked[e * cap : (e + 1) * cap, :]
        if gates is not None and i < pos_row.shape[0]:
            gate = slot_gates(hit, gate_cols, s, experts, cap)
            for e in range(experts):
                gates[e, s * cap : (s + 1) * cap, :] = gate[e * cap : (e + 1) * cap, :]
        if i + DEPTH < len(tasks):
            coming.append(fetch(i + DEPTH))
        for copy in following[:2]:
            copy.start()
        following = following[2:]
    start_all(*following)


def place(out, result, e, cap):
    out = out.astype(BF)
    for s in range(result.shape[0]):
        result[s, e * cap : (e + 1) * cap, :] = out[s * cap : (s + 1) * cap, :]


def combine(values, pos_row, keep, send, experts, cap, rows, order=None):
    for s in range(values.shape[0]):
        total = dot(slot_rows(pos_row, s, experts, cap), values[s], 0, 0).astype(BF)
        at = s if order is None else order[s]
        for r in range(4):
            (send if r % 2 else keep)[r // 2, at] = total[r * rows : (r + 1) * rows, :]


def silu_parts(gu):
    half = gu.shape[1] // 2
    gate, up = gu[:, :half], gu[:, half:]
    sg = 1.0 / (1.0 + jnp.exp(-gate))
    return gate, up, sg


def gate_up_grad(dz, gate, up, sg, out):
    half = gate.shape[1]
    out[:, :half] = (dz * up * sg * (1.0 + gate * (1.0 - sg))).astype(BF)
    out[:, half:] = (dz * gate * sg).astype(BF)


def take(refs, *counts):
    parts, at = [], 0
    for count in counts:
        parts.append(refs[at : at + count])
        at += count
    return parts


def expert_weights(w_in, w_out, wi, wo, sems):
    copies = [
        [
            pltpu.make_async_copy(w_in.at[e], wi.at[e], sems.at[2 * e]),
            pltpu.make_async_copy(w_out.at[e], wo.at[e], sems.at[2 * e + 1]),
        ]
        for e in range(w_in.shape[0])
    ]
    return copies, [copy for pair in copies for copy in pair]


def moe_fwd_kernel(experts, cap, rows, count, n_blocks, *refs):
    blocks, ins, outs, scratch = take(refs, n_blocks, 4, 3, 9)
    pos_row, gate_cols, w_in, w_out = ins
    gu_out, keep, send = outs
    ring, x_all, result, gates, gu_all, wi, wo, sems, ring_sems = scratch
    weights, coming = expert_weights(w_in, w_out, wi, wo, sems)
    tasks = [(places, s, x_all) for s, places in enumerate(sequences(blocks, count))]
    dispatch(tasks, ring, ring_sems, pos_row, gate_cols, gates, experts, cap, coming)
    for e in range(experts):
        wait_all(weights[e])
        gu = dot(x_all[e], wi[e], 1, 0)
        gu_all[e] = gu
        gate, up, sg = silu_parts(gu)
        z = (gate * sg * up * gates[e]).astype(BF)
        place(dot(z, wo[e], 1, 0), result, e, cap)
    done = start_all(pltpu.make_async_copy(gu_all, gu_out, sems.at[2 * experts]))
    combine(result, pos_row, keep, send, experts, cap, rows)
    wait_all(done)


def moe_bwd_kernel(experts, cap, rows, count, n_blocks, *refs):
    blocks, ins, outs, scratch = take(refs, n_blocks, 5, 4, 11)
    pos_row, gate_cols, gu_in, w_in, w_out = ins
    z_out, dgu_out, keep, send = outs
    ring, dr_all, result, gates, gu_all, z_all, dgu_all, wi, wo, sems, ring_sems = scratch
    weights, coming = expert_weights(w_in, w_out, wi, wo, sems)
    fetched = pltpu.make_async_copy(gu_in, gu_all, sems.at[2 * experts])
    tasks = [(places, s, dr_all) for s, places in enumerate(sequences(blocks, count))]
    dispatch(tasks, ring, ring_sems, pos_row, gate_cols, gates, experts, cap, [fetched] + coming)
    fetched.wait()
    for e in range(experts):
        wait_all(weights[e])
        gate, up, sg = silu_parts(gu_all[e])
        z_all[e] = (gate * sg * up * gates[e]).astype(BF)
        gate_up_grad(dot(dr_all[e], wo[e], 1, 1) * gates[e], gate, up, sg, dgu_all.at[e])
        place(dot(dgu_all[e], wi[e], 1, 1), result, e, cap)
    done = start_all(
        pltpu.make_async_copy(z_all, z_out, sems.at[2 * experts + 1]),
        pltpu.make_async_copy(dgu_all, dgu_out, sems.at[2 * experts + 2]),
    )
    combine(result, pos_row, keep, send, experts, cap, rows)
    wait_all(done)


def moe_turn_kernel(experts, cap, rows, count, n_blocks, batches, me, *refs):
    blocks, ins, outs, scratch = take(refs, n_blocks, 5, 4, 11)
    grads, pos_row, gate_cols, w_in, w_out = ins
    z_out, dgu_out, keep, send = outs
    ring, x_all, dr_all, result, gates, z_all, dgu_all, wi, wo, sems, ring_sems = scratch
    weights, coming = expert_weights(w_in, w_out, wi, wo, sems)
    grad_places = [places for batch in batches for places in gathered(me, grads, batch, count)]
    tasks = [(places, s, x_all) for s, places in enumerate(sequences(blocks, count))]
    tasks += [(places, s, dr_all) for s, places in enumerate(grad_places)]
    dispatch(tasks, ring, ring_sems, pos_row, gate_cols, gates, experts, cap, coming)
    for e in range(experts):
        wait_all(weights[e])
        gu = dot(x_all[e], wi[e], 1, 0)
        gate, up, sg = silu_parts(gu)
        z_all[e] = (gate * sg * up * gates[e]).astype(BF)
        gate_up_grad(dot(dr_all[e], wo[e], 1, 1) * gates[e], gate, up, sg, dgu_all.at[e])
        place(dot(dgu_all[e], wi[e], 1, 1), result, e, cap)
    done = start_all(
        pltpu.make_async_copy(z_all, z_out, sems.at[2 * experts]),
        pltpu.make_async_copy(dgu_all, dgu_out, sems.at[2 * experts + 1]),
    )
    combine(result, pos_row, keep, send, experts, cap, rows)
    wait_all(done)


def moe_out_kernel(experts, cap, rows, count, me, z, pos_row, w_out, keep, send, result):
    for e in range(experts):
        place(dot(z[e], w_out[e], 1, 0), result, e, cap)
    order = [s // count * count + (me[0] ^ (s % count)) for s in range(pos_row.shape[0])]
    combine(result, pos_row, keep, send, experts, cap, rows, order)


def moe_wgrad_kernel(experts, cap, count, n_blocks, *refs):
    me, refs = refs[0], refs[1:]
    x0, g0, x1, ins, hidden, outs, scratch = take(refs, n_blocks, n_blocks, n_blocks, 2, 4, 2, 9)
    cots, pos_row = ins
    dwin, dwout = outs
    ring, x_all, dr_all, dgu, z, din, dout, sems, ring_sems = scratch

    def tokens(x_places, g_places, dgu_in, z_in):
        fetched = start_all(
            pltpu.make_async_copy(dgu_in, dgu, sems.at[4]), pltpu.make_async_copy(z_in, z, sems.at[5])
        )
        tasks = [(places, s, x_all) for s, places in enumerate(x_places)]
        tasks += [(places, s, dr_all) for s, places in enumerate(g_places)]
        dispatch(tasks, ring, ring_sems, pos_row, None, None, experts, cap)
        wait_all(fetched)

    @pl.when(me[1] == 0)
    def _():
        tokens(sequences(x0, count), sequences(g0, count), hidden[0], hidden[1])

    @pl.when(me[1] == 1)
    def _():
        places = [part for batch in (1, 0) for part in gathered(me, cots, batch, count)]
        tokens(sequences(x1, count), places, hidden[2], hidden[3])

    leaving = [[], []]
    for e in range(experts):
        slot = e % 2
        wait_all(leaving[slot])
        din[slot] = dot(x_all[e], dgu[e], 0, 0)
        dout[slot] = dot(z[e], dr_all[e], 0, 0)
        leaving[slot] = start_all(
            pltpu.make_async_copy(din.at[slot], dwin.at[e], sems.at[slot]),
            pltpu.make_async_copy(dout.at[slot], dwout.at[e], sems.at[2 + slot]),
        )
    wait_all(leaving[0] + leaving[1])


def per_device(
    block_input, segments, expert_ids, gate_values, cotangent, attn_gain,
    query_weight, kv_weight, out_weight, moe_gain, w_in, w_out,
):
    sec = lax.axis_index("section")
    dp = lax.axis_index("dp")
    t = lax.axis_index("tensor")
    n_dp = lax.axis_size("dp")
    n_t = lax.axis_size("tensor")
    first = sec == 0
    core0 = t % 2 == 0
    me = jnp.stack([dp, sec, t % 2, t]).astype(jnp.int32)
    rows, width = block_input.shape[1], block_input.shape[2]
    seq = segments.shape[1]
    top = expert_ids.shape[3]
    heads = query_weight.shape[2] // HD
    qcols = heads * HD
    experts, ffn = w_in.shape[1], w_out.shape[2]
    cap = -(-(seq * top * 9 // (8 * E)) // 16) * 16
    sides = 2 if n_dp <= TOGETHER else 1
    total = 2 * n_dp
    slots = total * cap
    dp_order = jnp.arange(n_dp, dtype=jnp.int32) ^ dp
    t_order = jnp.arange(n_t, dtype=jnp.int32) ^ t
    drows = width // n_dp
    half = drows // 2

    pair = jax.ShapeDtypeStruct((2, rows, width), BF)
    smem = pl.BlockSpec(memory_space=pltpu.SMEM)
    vmem = pl.BlockSpec(memory_space=pltpu.VMEM)
    any_space = pl.BlockSpec(memory_space=pl.ANY)
    hbm = pl.BlockSpec(memory_space=pltpu.HBM)
    seq_scratch = pltpu.VMEM((seq, width), BF)

    def me_after(*tokens):
        return jnp.where(there(*tokens), me, 0) if tokens else me

    def shape(*dims, dtype=BF):
        return jax.ShapeDtypeStruct(dims, dtype)

    def call(
        kernel, name, ins, outs, scratch, limit, cost, in_specs=None, out_specs=None, hold=(), tokens=()
    ):
        n_ins, n_outs, n_hold, n_tok = len(ins), len(outs), len(hold), len(tokens)

        def body(*refs):
            given, results, rest = take(refs, n_ins + n_tok + n_hold, n_outs + n_hold, len(scratch))
            kernel(*given[:n_ins], *results[:n_outs], *rest)

        out = pl.pallas_call(
            body,
            out_shape=list(outs) + [jax.ShapeDtypeStruct(h.shape, h.dtype) for h in hold],
            in_specs=(in_specs or [smem] + [vmem] * (n_ins - 1)) + [any_space] * (n_tok + n_hold),
            out_specs=(out_specs or [vmem] * n_outs) + [any_space] * n_hold,
            scratch_shapes=scratch,
            input_output_aliases={n_ins + n_tok + i: n_outs + i for i in range(n_hold)},
            compiler_params=pltpu.CompilerParams(vmem_limit_bytes=limit * MIB),
            cost_estimate=pl.CostEstimate(flops=cost * 10**9, bytes_accessed=cost * 3 * MIB, transcendentals=0),
            name=name,
        )(*ins, *tokens, *hold)
        return out[:n_outs], out[n_outs:]

    acols = 2 * qcols + 2 * HD
    weights_scratch = pltpu.VMEM((width, acols), BF)
    weights_sems = pltpu.SemaphoreType.DMA((2, n_dp))

    def attn_fwd(a_blocks, weights, tokens=()):
        return call(
            functools.partial(attn_fwd_kernel, heads), "attn_fwd",
            (me, weights, *a_blocks, table),
            [pair, pair, shape(seq, acols), shape(seq, width)],
            [weights_scratch, weights_sems], 20, 0, [smem, hbm] + [vmem] * 5, tokens=tokens,
        )[0]

    def attn_bwd(d_blocks, saved, weights):
        return call(
            functools.partial(attn_bwd_kernel, heads), "attn_bwd",
            (me, weights, *d_blocks, saved, table),
            [pair, pair, shape(seq, qcols + HD), shape(seq, HD), shape(seq, width)],
            [weights_scratch, weights_sems, pltpu.VMEM((seq, qcols + 2 * HD), BF)], 20, 0,
            [smem, hbm] + [vmem] * 6,
        )[0]

    tok_f32, tok_bf = shape(rows, width, dtype=F32), shape(rows, width)

    def finish(base, gain, terms, hold=()):
        (out, normed), held = call(
            functools.partial(finish_kernel, [at for _, at in terms]), "finish",
            (base, gain, *[value for value, _ in terms]), [tok_f32, tok_bf], [], 8, 0,
            [vmem] * (2 + len(terms)), hold=hold,
        )
        return out, normed, held

    def norm_back(x, gain, upper, terms, more=(), tokens=()):
        return call(
            functools.partial(norm_back_kernel, [at for _, at in terms]), "norm_back",
            (x, gain, upper, *[value for value, _ in terms], *more),
            [tok_f32] * (1 + len(more)) + [tok_bf, shape(1, width, dtype=F32)], [], 8, 0,
            [vmem] * (3 + len(terms) + len(more)), tokens=tokens,
        )

    def halves_grad(kernel, name, ins, cols):
        return call(
            functools.partial(kernel, n_dp), name, (me, *ins), [shape(n_dp, half, cols)] * 2,
            [pltpu.VMEM((width, cols), BF)], 20, 1,
        )[0]

    count = sides * n_dp
    part_slots = count * cap
    weight_scratch = [pltpu.VMEM((experts, width, 2 * ffn), BF), pltpu.VMEM((experts, ffn, width), BF)]
    ring_scratch = pltpu.VMEM((DEPTH, seq, width), BF)
    slot_scratch = pltpu.VMEM((experts, part_slots, width), BF)
    result_scratch = pltpu.VMEM((count, experts * cap, width), BF)
    z_scratch = pltpu.VMEM((experts, part_slots, ffn), BF)
    dgu_scratch = pltpu.VMEM((experts, part_slots, 2 * ffn), BF)
    gu_scratch = pltpu.VMEM((experts, part_slots, 2 * ffn), F32)
    gate_scratch = pltpu.VMEM((experts, part_slots, 1), F32)
    copy_sems = pltpu.SemaphoreType.DMA((2 * experts + 3,))
    ring_sems = pltpu.SemaphoreType.DMA((DEPTH, 4))
    gu_shape = shape(experts, part_slots, 2 * ffn, dtype=F32)
    z_shape = shape(experts, part_slots, ffn)
    dgu_shape = shape(experts, part_slots, 2 * ffn)
    sum_shapes = [shape(2, count, rows, width)] * 2
    expert_args = (w_in[0], w_out[0])

    def by_sides(run, arrays, axes):
        if sides == 2:
            return run(arrays, (0, 1))
        size = [value.shape[axis] // 2 for value, axis in zip(arrays, axes)]
        outs = []
        for side in range(2):
            parts = [
                lax.slice_in_dim(value, side * n, (side + 1) * n, axis=axis)
                for value, n, axis in zip(arrays, size, axes)
            ]
            outs.append(run(parts, (side,)))
        return [jnp.concatenate(both, axis=1) for both in zip(*outs)]

    def of_sides(blocks, which):
        return [part for side in which for part in blocks[side]]

    def moe_fwd(blocks, route):
        def run(arrays, which):
            parts = of_sides(blocks, which)
            return call(
                functools.partial(moe_fwd_kernel, experts, cap, rows, n_dp, len(parts)), "moe_fwd",
                (*parts, *arrays, *expert_args), [gu_shape] + sum_shapes,
                [
                    ring_scratch, slot_scratch, result_scratch, gate_scratch, gu_scratch, *weight_scratch, copy_sems, ring_sems,
                ],
                48, COST, [any_space] * len(parts) + [vmem] * 2 + [hbm] * 2, [hbm] + [vmem] * 2,
            )[0]

        gu, keep, send = by_sides(run, route, (0, 0))
        return gu, (keep, send)

    def moe_bwd(blocks, gu, route):
        def run(arrays, which):
            parts = of_sides(blocks, which)
            return call(
                functools.partial(moe_bwd_kernel, experts, cap, rows, n_dp, len(parts)), "moe_bwd",
                (*parts, *arrays, *expert_args), [z_shape, dgu_shape] + sum_shapes,
                [
                    ring_scratch, slot_scratch, result_scratch, gate_scratch, gu_scratch, z_scratch,
                    dgu_scratch,
                    *weight_scratch, copy_sems, ring_sems,
                ],
                50, COST, [any_space] * len(parts) + [vmem] * 2 + [hbm] * 3, [hbm] * 2 + [vmem] * 2,
            )[0]

        z, dgu, keep, send = by_sides(run, (*route, gu), (0, 0, 1))
        return (dgu, z), (keep, send)

    def moe_turn(blocks, grads, route):
        def run(arrays, which):
            parts = of_sides(blocks, which)
            batches = [1 - side for side in which]
            return call(
                functools.partial(
                    moe_turn_kernel, experts, cap, rows, n_dp, len(parts), batches
                ),
                "moe_turn", (me, *parts, grads, *arrays, *expert_args),
                [z_shape, dgu_shape] + sum_shapes,
                [
                    ring_scratch, slot_scratch, slot_scratch, result_scratch, gate_scratch, z_scratch,
                    dgu_scratch,
                    *weight_scratch, copy_sems, ring_sems,
                ],
                57, COST * 2, [smem] + [any_space] * (len(parts) + 1) + [vmem] * 2 + [hbm] * 2,
                [hbm] * 2 + [vmem] * 2,
            )[0]

        z, dgu, keep, send = by_sides(run, route, (0, 0))
        return (dgu, z), (keep, send)

    def moe_out(z, route, *tokens):
        def run(arrays, which):
            return call(
                functools.partial(moe_out_kernel, experts, cap, rows, n_dp), "moe_out",
                (me_after(*tokens), *arrays, w_out[0]), sum_shapes, [result_scratch], 32, COST,
            )[0]

        return by_sides(run, (z, route[0]), (1, 0))

    def moe_wgrad(blocks0, grads0, blocks1, hidden, route, *tokens):
        arrays = [of_sides(blocks, (0, 1)) for blocks in (blocks0, grads0, blocks1)]
        return call(
            functools.partial(moe_wgrad_kernel, experts, cap, n_dp, len(arrays[0])), "moe_wgrad",
            (me_after(*tokens), *arrays[0], *arrays[1], *arrays[2], cot_all, route, *hidden),
            [shape(experts, width, 2 * ffn, dtype=F32), shape(experts, ffn, width, dtype=F32)],
            [
                ring_scratch, pltpu.VMEM((experts, slots, width), BF), pltpu.VMEM((experts, slots, width), BF),
                pltpu.VMEM((experts, slots, 2 * ffn), BF), pltpu.VMEM((experts, slots, ffn), BF),
                pltpu.VMEM((2, width, 2 * ffn), F32), pltpu.VMEM((2, ffn, width), F32),
                pltpu.SemaphoreType.DMA((6,)), ring_sems,
            ],
            48, 10, [smem] + [hbm] * (3 * len(arrays[0]) + 1) + [vmem] + [hbm] * 4, [hbm] * 2,
        )[0]

    gains = jnp.concatenate([attn_gain, moe_gain], axis=0)
    gains = jnp.stack(over_tensor(gains))[t_order].transpose(1, 0, 2).reshape(2, drows)
    gains = jnp.stack([gains] + [move(gains, dp=k) for k in range(1, n_dp)])[dp_order]
    gains = gains.transpose(1, 0, 2).reshape(2, 1, width)
    gains_far = move(gains, section=1)
    layer_gain = [jnp.where(sec == l, gains, gains_far).astype(F32) for l in range(2)]
    (gains0, gains1) = layer_gain

    def seeds_of(matrix):
        low, high = matrix[:half], matrix[half:]
        return jnp.where(first, low, high), move(jnp.where(first, high, low), section=1)

    def gather_weights(seed):
        return lax.all_gather(seed[None, None], ("section", "dp"), axis=0, tiled=True).reshape(
            2, n_dp, half, acols
        )

    kv_own = kv_turn(kv_weight[0])
    kv_core = move(kv_own, tensor=1)
    key_value = jnp.where(
        core0, jnp.concatenate([kv_own, kv_core], axis=1), jnp.concatenate([kv_core, kv_own], axis=1)
    )
    routing = jnp.concatenate([expert_ids[0].astype(F32), gate_values[0]], axis=2)
    routing = [routing] + [move(routing, dp=k) for k in range(1, n_dp)]
    seed_near, seed_far = seeds_of(
        jnp.concatenate([query_weight[0], key_value, out_weight[0].T], axis=1)
    )

    segment = jnp.where(first, segments[0], segments[1])
    ordinal = jnp.arange(seq, dtype=jnp.int32)
    start = jnp.sum((segment[None, :] < segment[:, None]).astype(jnp.int32), axis=1)
    places = (ordinal - start).astype(F32)

    def turned(vector):
        return vector.reshape(n_t, rows)[t_order].reshape(seq)

    start_col = turned(start)[:, None]
    frequency = THETA ** (-2.0 * jnp.arange(HD // 2, dtype=F32) / HD)
    angles = turned(places)[:, None] * frequency[None, :]
    cosine = jnp.cos(angles)
    cosine = jnp.concatenate([cosine, cosine], axis=1)
    sine = jnp.sin(angles)
    sine = jnp.concatenate([-sine, sine], axis=1)
    table = jnp.concatenate([cosine, sine, jnp.pad(start_col.astype(F32), ((0, 0), (0, HD - 1)))], axis=1)

    def routes_of(routing):
        routing = jnp.stack(routing)
        routing = routing.reshape(n_dp, 2, n_t, rows, 2 * top)[:, :, t_order]
        routing = routing.reshape(n_dp, 2, seq, 2 * top)
        names = (dp * experts + jnp.arange(experts, dtype=jnp.int32)).astype(F32)
        chosen = routing[:, :, :, :top, None] == names
        member = jnp.sum(chosen.astype(F32), axis=3)
        gates = jnp.sum(jnp.where(chosen, routing[:, :, :, top:, None], 0.0), axis=3)
        lower = (ordinal[:, None] > ordinal[None, :]).astype(BF)
        rank = jnp.einsum("ij,smje->smei", lower, member.astype(BF), preferred_element_type=F32)
        slot = jnp.where(member.transpose(0, 1, 3, 2) > 0.5, rank, -1.0).astype(jnp.int32)
        gate_high = gates.astype(BF)
        gate_low = (gates - gate_high.astype(F32)).astype(BF)
        gate_cols = jnp.concatenate([gate_high, gate_low], axis=3)
        gate_cols = jnp.pad(gate_cols, ((0, 0), (0, 0), (0, 0), (0, HD - 2 * experts)))
        return [
            tuple(jnp.concatenate([part[:, b], part[:, 1 - b]]) for part in (slot, gate_cols))
            for b in range(2)
        ]

    def spread(value):
        near, far = [value, move(value, tensor=2)], [move(value, section=1), move(value, section=1, tensor=2)]
        return [[part[0], move(part[0], tensor=1), part[1], move(part[1], tensor=1)] for part in (near, far)]

    def to_host(own, *tokens):
        near_own, far_own = spread(own)
        others = jnp.stack([move(own, dp=k) for k in range(1, n_dp)])
        near, far = spread(after(others, near_own[2], far_own[0], far_own[2], *tokens))
        return near_own + near, far_own + far

    def core_sums(keep, send, *tokens):
        got = move(send, tensor=1)
        sums = [
            [keep[y, at : at + n_dp] + got[y, at : at + n_dp] for y in range(2)] for at in (0, n_dp)
        ]
        if tokens:
            sums[1][1] = after(sums[1][1], *tokens)
        return sums

    def gather_sums(near, far, host, *tokens):
        near = near[0] + move(near[1], tensor=2)
        far = move(far[0], section=1) + move(far[1], section=1, tensor=2)
        total = jnp.where(sec == host, near, far)
        return after(total, *tokens) if tokens else total

    def parts_of(near, far, which):
        return [[part[which] for part in side] for side in (near, far)]

    def others_sums(near, far, host, *tokens):
        return gather_sums(*parts_of(near, far, slice(1, None)), host, *tokens)

    def all_sums(near, far, others, host, *tokens):
        total = gather_sums(*parts_of(near, far, 0), host).astype(F32)
        for k in range(1, n_dp):
            total = total + move(others[k - 1], dp=k).astype(F32)
        return [(after(total, *tokens) if tokens else total, None)]

    def from_host(near, far, host):
        return all_sums(near, far, others_sums(near, far, host), host)

    x0 = jnp.where(first, block_input[0], block_input[1])
    seed = jnp.where(first & there(*routing[1:]), seed_near, seed_far)
    weights0 = gather_weights(seed)
    _, a, _ = finish(x0, gains0[0], [])

    routes = routes_of(routing)
    a_blocks = over_tensor(a)
    keep, send, saved, a_all = attn_fwd(
        a_blocks, weights0, routes[0]
    )
    part0, part1 = sum_over_tensor(keep, send)
    mid, m, _ = finish(x0, gains0[1], [(part0, None), (part1, None)])
    kept0 = (x0, a_all, saved, mid, weights0)
    cot_far = move(jnp.where(first, cotangent[0, 1], cotangent[0, 0]), section=1)
    cot_near = jnp.where(first, cotangent[0, 0], cotangent[0, 1])
    cots = jnp.stack([jnp.where(first, cot_near, cot_far), jnp.where(first, cot_far, cot_near)])
    near, far = to_host(m, cots[0])
    there_now = [part.reshape(-1, width)[:half, :acols] for part in (near[6], far[4], far[6])]
    weights1 = gather_weights(after(jnp.where(first, seed_far, seed_near), *there_now))
    cot_all = after(cotangent[0].astype(BF), *[part[:1] for part in (near[6], far[4], far[6])])
    cot_all = lax.all_gather(cot_all[None], ("dp", "tensor"), axis=0, tiled=True)
    blocks0 = (near, far)
    gu0, sums = moe_fwd(blocks0, routes[0])
    terms = from_host(*core_sums(*sums), 0)
    out0, a, _ = finish(mid, gains1[0], terms)

    a_blocks = over_tensor(a)
    keep, send, saved, a_all = attn_fwd(a_blocks, weights1)
    part0, part1 = sum_over_tensor(keep, send)
    mid, m, _ = finish(out0, gains1[1], [(part0, None), (part1, None)])
    kept1 = (out0, a_all, saved, mid, weights1)
    near, far = to_host(m)
    blocks1 = (near, far)
    hidden1, sums = moe_turn(blocks1, cot_all, routes[1])
    terms = from_host(*core_sums(*sums), 1)

    cot_far = move(jnp.where(first, cotangent[0, 1], cotangent[0, 0]), section=1)
    cot_near = jnp.where(first, cotangent[0, 0], cotangent[0, 1])
    cots = (jnp.where(first, cot_near, cot_far), jnp.where(first, cot_far, cot_near))

    def attention_back(kept, l, g, terms, more, beside=None):
        x, a_all, saved, mid, weights = kept
        (dmid, d, moe_gain_sum), _ = norm_back(mid, layer_gain[l][1], g, terms)
        d_blocks = over_tensor(d)
        extra = core_sums(*beside(d)) if beside is not None else None
        keep, send, dq, kv_send, d_all = attn_bwd(d_blocks, saved, weights)
        args = (a_all, d_all, saved, dq, move(kv_send, tensor=1))
        mine, theirs = halves_grad(
            functools.partial(attn_wgrad_kernel, l == 0), "attn_wgrad", args, 2 * qcols + HD
        )
        part0, part1 = sum_over_tensor(keep, send)
        (*outs, attn_gain_sum), _ = norm_back(
            x, layer_gain[l][0], dmid, [(part0, None), (part1, None)], more
        )
        return outs, jnp.concatenate([attn_gain_sum, moe_gain_sum]), mine, theirs, extra

    (in_grad1, g, g_low), gain_sums1, mine, theirs, outs = attention_back(
        kept1, 1, cots[1], terms, (cots[0],), lambda d: moe_out(hidden1[1], routes[1], d)
    )
    out_first, out_second = (jnp.stack([side[y] for side in outs]) for y in range(2))
    grad1 = jnp.where(first, jnp.stack([mine, theirs]), jnp.stack([theirs, mine]))
    near, far = to_host(g_low, grad1[0, 0, :1, :1])
    shard1_sum = lax.psum_scatter(
        grad1.reshape(2 * n_dp, half, acols - HD), ("section", "dp"), scatter_dimension=0, tiled=True
    )
    grads0 = (near, far)
    hidden0, sums = moe_bwd(grads0, gu0, routes[0])
    near_far = core_sums(*sums, shard1_sum[0, :1, :1])
    route = jnp.where(first, routes[0][0], routes[1][0])
    dw_in, dw_out = moe_wgrad(
        blocks0, grads0, blocks1, (*hidden0, *hidden1), route, near_far[1][1]
    )
    others = others_sums(*near_far, 0, dw_out[0, :rows])
    terms = all_sums(*near_far, others, 0)
    (in_grad0, _), gain_sums0, mine, theirs, _ = attention_back(kept0, 0, g, terms, ())
    out_across = move(after(out_second, in_grad0[None, None]), tensor=2)
    out1_sum = lax.psum_scatter(
        (out_first + out_across).swapaxes(0, 1), "dp", scatter_dimension=0, tiled=True
    )[0].astype(F32)

    gain_sums = jnp.concatenate([gain_sums0, gain_sums1])
    gain_sums = gain_sums + move(gain_sums, tensor=1)
    gain_sums = after(gain_sums + move(gain_sums, tensor=2), out_across[0, 0, :4])
    gain_sums = gain_sums.astype(BF).reshape(4, n_dp, drows).transpose(1, 0, 2)[dp_order]
    gain_sums = jnp.pad(gain_sums, ((0, 0), (0, 12), (0, 2 * qcols + HD - drows)))
    parts = jnp.concatenate([mine + move(theirs, section=1), gain_sums], axis=1)
    parts = [parts[0]] + [move(parts[k], dp=k) for k in range(1, n_dp)]
    shard1 = shard1_sum[0].astype(F32)
    shard0 = sum(part.astype(F32) for part in parts)

    gain0, gain1 = shard0[half : half + 2], shard0[half + 2 : half + 4]
    own = jnp.where(first, shard0[:half], shard1)
    own_gain = jnp.where(first, gain0, gain1)[:, :drows]
    far = jnp.concatenate([
        jnp.where(first, shard1, shard0[:half]),
        jnp.pad(jnp.where(first, gain1, gain0), ((0, 14), (0, 0))),
    ])
    far = move(far.astype(BF), section=1).astype(F32)
    grad_shard = jnp.where(
        first, jnp.concatenate([own, far[:half]]), jnp.concatenate([far[:half], own])
    )
    gains = own_gain + far[half : half + 2, :drows]
    gains = lax.dynamic_slice_in_dim(gains, t * attn_gain.shape[1], attn_gain.shape[1], 1)
    cols = qcols + HD
    grad_out = grad_shard[:, cols:].T
    grad_kv = kv_turn(grad_shard[:, qcols:cols])
    def mine_and_theirs(value0, value1):
        return jnp.where(first, value0, value1), jnp.where(first, value1, value0)

    grad_near, grad_far = mine_and_theirs(in_grad0, in_grad1)
    out_swap = jnp.where(first, mid, out0)
    theirs = move(jnp.stack([out_swap, grad_far]).astype(BF), section=1).astype(F32)
    out_near = jnp.where(first, out0, mid + out1_sum[0])
    out_far = jnp.where(first, theirs[0], theirs[0] + out1_sum[1])

    def both_batches(near, far):
        return jnp.where(first, jnp.stack([near, far]), jnp.stack([far, near]))[None]

    return (
        both_batches(out_near, out_far),
        both_batches(grad_near, theirs[1]),
        gains[0:1],
        grad_shard[None, :, :qcols],
        grad_kv[None],
        grad_out[None],
        gains[1:2],
        dw_in[None],
        dw_out[None],
    )


def solution(mesh):
    return jax.shard_map(
        per_device,
        mesh=mesh,
        in_specs=(
            P(None, ("dp", "tensor"), None),
            P(None, "dp"),
            P("section", None, "dp", None),
            P("section", None, "dp", None),
            P("section", None, ("dp", "tensor"), None),
            P("section", ("dp", "tensor")),
            P("section", "dp", "tensor"),
            P("section", "dp", "tensor"),
            P("section", "tensor", "dp"),
            P("section", ("dp", "tensor")),
            P("section", "dp", None, "tensor"),
            P("section", "dp", "tensor", None),
        ),
        out_specs=(
            P("section", None, ("dp", "tensor"), None),
            P("section", None, ("dp", "tensor"), None),
            P("section", ("dp", "tensor")),
            P("section", "dp", "tensor"),
            P("section", "dp", "tensor"),
            P("section", "tensor", "dp"),
            P("section", ("dp", "tensor")),
            P("section", "dp", None, "tensor"),
            P("section", "dp", "tensor", None),
        ),
        check_vma=False,
    )
```
